128 devices in a mesh: rep: 8 (over x, core), tile: 16 (over z, y).
Axes of the slice: x: 4, y: 4, z: 4, core: 2. Of those that a mesh axis runs over, the one named last changes fastest.
Arguments:
- latents: bfloat16 [8, 5, 128, 8, 256], P('rep', None, 'tile'), may hold values from -6 to 6
- cotangent: bfloat16 [8, 5, 128, 8, 256], P('rep', None, 'tile'), may hold values from -0.119628906 to 0.119628906
- kernel_one: bfloat16 [6912, 256], replicated, may hold values from -0.078125 to 0.078125
- kernel_two: bfloat16 [6912, 256], replicated, may hold values from -0.078125 to 0.078125
- error_one: float32 [8, 6912, 256], P('rep', 'tile'), may hold values from -4 to 4
- error_two: float32 [8, 6912, 256], P('rep', 'tile'), may hold values from -4 to 4
- factor_one: float32 [256, 8], replicated, may hold values from -6 to 6
- factor_two: float32 [256, 8], replicated, may hold values from -6 to 6
Outputs:
- approx_one: float32 [6912, 256], P('tile')
- approx_two: float32 [6912, 256], P('tile')
- new_error_one: float32 [8, 6912, 256], P('rep', 'tile')
- new_error_two: float32 [8, 6912, 256], P('rep', 'tile')
- new_factor_one: float32 [256, 8], replicated
- new_factor_two: float32 [256, 8], replicated
The draws below stay inside these ranges and needn't reach their ends.
All inputs are finite; a program needn't handle non-finite values.
Results may differ from the reference program's by a relative error of at most 0.0075.
Values may be sent and summed in bfloat16 or wider, within the bound.
A program may use at most 320 MiB of HBM per device.

```python
import jax
import jax.numpy as jnp
from jax import lax

C = 256
FR = 5
WC = 8
RANK = 8
SAMPLES = 8
H = 128
ROWS = 6912
N_REP = 8


def block_levels(stream_key, extent, pieces, least, high):
    loudness = 1.0
    for position, shards_of in pieces:
        draws = jax.random.uniform(jax.random.fold_in(jax.random.fold_in(stream_key, 6), position), (shards_of,), jnp.float32, least / len(pieces), high / len(pieces))
        loudness = loudness * jnp.repeat(jnp.exp(draws), extent[position] // shards_of).reshape((-1,) + (1,) * (len(extent) - 1 - position))
    return loudness


def bell_draw(rng, dims, deviation, bound, split=(), dtype=jnp.bfloat16):
    gain = block_levels(rng, dims, split, -0.22, 0.18) if split else 1.0
    array = jax.random.normal(rng, dims, jnp.float32) * deviation * gain
    return jnp.minimum(jnp.maximum(array, -bound), bound).astype(dtype)


def setup_inputs(seed: int = 0) -> dict:
    key_list = jax.random.split(jax.random.key(seed), 9)
    latents = bell_draw(key_list[0], (SAMPLES, FR, H, WC, C), 1.0, 6.0, ((0, 8), (2, 16)))
    cotangent = bell_draw(key_list[1], (SAMPLES, FR, H, WC, C), 0.02, 0.119628906, ((0, 8), (2, 16)))
    kernel_one = bell_draw(key_list[2], (ROWS, C), ROWS ** -0.5, 0.078125)
    kernel_two = bell_draw(key_list[3], (ROWS, C), ROWS ** -0.5, 0.078125)
    error_one = bell_draw(key_list[4], (SAMPLES, ROWS, C), 0.5, 4.0, ((0, 8), (1, 16)), jnp.float32)
    error_two = bell_draw(key_list[5], (SAMPLES, ROWS, C), 0.5, 4.0, ((0, 8), (1, 16)), jnp.float32)
    factor_one = bell_draw(key_list[6], (C, RANK), 1.0, 6.0, (), jnp.float32)
    factor_two = bell_draw(key_list[7], (C, RANK), 1.0, 6.0, (), jnp.float32)
    return {"latents": latents, "cotangent": cotangent, "kernel_one": kernel_one, "kernel_two": kernel_two, "error_one": error_one, "error_two": error_two, "factor_one": factor_one, "factor_two": factor_two}


HIGH = lax.Precision.HIGHEST

def kernel_taps(kernel):
    chans = kernel.shape[1]
    return kernel.reshape(chans, 3, 3, 3, chans).transpose(1, 2, 3, 0, 4)

def causal_conv(field, kernel):
    return lax.conv_general_dilated(field, kernel_taps(kernel), (1, 1, 1), [(2, 0), (1, 1), (1, 1)], dimension_numbers=('NDHWC', 'DHWIO', 'NDHWC'), preferred_element_type=jnp.float32)

def reverse_conv(field, kernel):
    flipped = kernel_taps(kernel)[::-1, ::-1, ::-1].transpose(0, 1, 2, 4, 3)
    return lax.conv_general_dilated(field, flipped, (1, 1, 1), [(0, 2), (1, 1), (1, 1)], dimension_numbers=('NDHWC', 'DHWIO', 'NDHWC'), preferred_element_type=jnp.float32)

def silu_slope(value):
    sig = jax.nn.sigmoid(value)
    return sig * (1.0 + value * (1.0 - sig))

def patch_matrix(field):
    frames, height, width, chans = field.shape
    padded = jnp.pad(field, ((2, 0), (1, 1), (1, 1), (0, 0)))
    taps = [padded[a:a + frames, b:b + height, e:e + width] for a in range(3) for b in range(3) for e in range(3)]
    stacked = jnp.stack(taps, axis=-1)
    return stacked.reshape(frames * height * width, chans * 27)

def sample_gradient(pair):
    field, slope = pair
    patches = patch_matrix(field)
    flat = slope.reshape(-1, slope.shape[-1])
    return lax.dot_general(patches, flat, (((0,), (0,)), ((), ())), preferred_element_type=jnp.float32)

def orthonormal(left):
    columns = []
    for j in range(left.shape[1]):
        vector = left[:, j]
        if j > 0:
            basis = jnp.stack(columns, axis=1)
            coefs = jnp.dot(vector, basis, precision=HIGH)
            vector = vector - jnp.dot(basis, coefs, precision=HIGH)
        columns.append(vector / jnp.sqrt(jnp.sum(vector * vector)))
    return jnp.stack(columns, axis=1)

def compress(grads, error, factor):
    merged = grads + error
    proj = jnp.einsum('brc,ck->brk', merged, factor, precision=HIGH)
    left = lax.optimization_barrier(jnp.sum(proj, axis=0)) / N_REP
    basis = orthonormal(left)
    right = jnp.einsum('brc,rk->ck', merged, basis, precision=HIGH) / N_REP
    approx = jnp.dot(basis, right.T, precision=HIGH)
    return (approx, merged - approx[None], right)

def reference(latents, cotangent, kernel_one, kernel_two, error_one, error_two, factor_one, factor_two):
    pre_one = causal_conv(latents, kernel_one)
    hidden = jax.nn.silu(pre_one).astype(jnp.bfloat16)
    pre_two = causal_conv(hidden, kernel_two)
    slope_two = (cotangent.astype(jnp.float32) * silu_slope(pre_two)).astype(jnp.bfloat16)
    back_one = reverse_conv(slope_two, kernel_two)
    slope_one = (back_one * silu_slope(pre_one)).astype(jnp.bfloat16)
    grads_two = lax.map(sample_gradient, (hidden, slope_two))
    grads_one = lax.map(sample_gradient, (latents, slope_one))
    approx_one, err_one, right_one = compress(grads_one, error_one, factor_one)
    approx_two, err_two, right_two = compress(grads_two, error_two, factor_two)
    return (approx_one, approx_two, err_one, err_two, right_one, right_two)
```

```python
import functools

import jax
import jax.numpy as jnp
from jax import lax
from jax.experimental import pallas as pl
from jax.experimental.pallas import tpu as pltpu
from jax.sharding import PartitionSpec as P

MESH = pl.DeviceIdType.MESH
HIGH = lax.Precision.HIGHEST
BF = jnp.bfloat16
F32 = jnp.float32
FR = 5
WC = 8
C = 256
RANK = 8
OWN = 432
NT = (((1,), (1,)), ((), ()))
TN = (((0,), (0,)), ((), ()))


def sigmoid(v):
    return 1.0 / (1.0 + jnp.exp(-v))


def silu_slope(v):
    sig = sigmoid(v)
    return sig * (1.0 + v * (1.0 - sig))


def valid_rows(field, first, tile):
    row = lax.broadcasted_iota(jnp.int32, field.shape, 0) + first
    inside = jnp.logical_and(
        jnp.logical_or(row >= 0, tile > 0), jnp.logical_or(row < 8, tile < 15)
    )
    return jnp.where(inside, field, 0.0)


def spread(field, frame, even, odd):
    rows = field.shape[0]
    col = lax.broadcasted_iota(jnp.int32, field.shape, 1)
    for e in range(3):
        if e == 1:
            moved = field
        else:
            moved = pltpu.roll(field, 1 if e == 0 else WC - 1, 1)
            moved = jnp.where(col == (0 if e == 0 else WC - 1), 0.0, moved)
        even[e, frame, pl.ds(0, rows * WC), :] = moved.reshape(rows * WC, C).astype(BF)
        inner = moved[1 : rows - 1].reshape((rows - 2) * WC, C)
        odd[e, frame, pl.ds(0, (rows - 2) * WC), :] = inner.astype(BF)


def conv(even, odd, rows, weights, total, reverse):
    for a in (2, 1, 0):
        count = 3 + a
        first_in, first_out = (2 - a, 0) if reverse else (0, 2 - a)
        pieces = []
        for b in range(3):
            for e in range(3):
                bb, ee = (2 - b, 2 - e) if reverse else (b, e)
                source = odd if bb == 1 else even
                start = 16 if bb == 2 else 0
                piece = source[ee, pl.ds(first_in, count), pl.ds(start, rows * WC), :]
                pieces.append(piece.reshape(count * rows * WC, C))
        lhs = jnp.concatenate(pieces, axis=1)
        if reverse:
            taps = [weights[a, pl.ds(i * C, C), :] for i in range(9)]
            out = lax.dot_general(
                lhs, jnp.concatenate(taps, axis=1), NT, preferred_element_type=F32
            )
        else:
            out = jnp.dot(lhs, weights[a], preferred_element_type=F32)
        out = out.reshape(count, rows * WC, C)
        if a == 2:
            total[...] = out
        else:
            total[pl.ds(first_out, count)] += out


def turned(field):
    flat = field.reshape(80, C)
    flat = jnp.concatenate([flat, jnp.zeros((48, C), F32)], axis=0)
    return flat.T.astype(BF).reshape(4, 4, 16, 128)


def train_kernel(
    lat, cot, ker_one, ker_two, err_one, err_two, fac_one, fac_two,
    merged, left_out, right_out,
    raw, weights, chunk, lat_ext, cot_ext, even, odd, acc_one, acc_two, acc_three,
    select, turn, turn_in, slopes, patches, part, part_half, part_in, errs,
    proj, right_rep, right_y, right_z, local_sem, send_sem, recv_sem,
):
    tile = lax.axis_index("tile")
    rep = lax.axis_index("rep")
    tz, ty = tile // 4, tile % 4

    def along(axis, d):
        if axis == "z":
            return lax.rem(tz + d, 4) * 4 + ty
        return tz * 4 + lax.rem(ty + d, 4)

    up, down = lax.rem(tile + 15, 16), lax.rem(tile + 1, 16)
    sends = []
    n_send = [0]

    def remote(src, dst, recv, device):
        copy = pltpu.make_async_remote_copy(
            src_ref=src, dst_ref=dst, send_sem=send_sem.at[n_send[0]], recv_sem=recv_sem.at[recv],
            device_id=device, device_id_type=MESH,
        )
        n_send[0] += 1
        copy.start()
        sends.append(copy)

    def arrived(dst, recv):
        pltpu.make_async_remote_copy(
            src_ref=dst, dst_ref=dst, send_sem=send_sem.at[0], recv_sem=recv_sem.at[recv],
            device_id={"tile": up}, device_id_type=MESH,
        ).wait_recv()

    loads = [
        pltpu.make_async_copy(ker_one, raw.at[0], local_sem.at[0]),
        pltpu.make_async_copy(ker_two, raw.at[1], local_sem.at[1]),
        pltpu.make_async_copy(lat, lat_ext.at[:, pl.ds(32, 64)], local_sem.at[2]),
        pltpu.make_async_copy(cot, cot_ext.at[:, pl.ds(16, 64)], local_sem.at[3]),
        pltpu.make_async_copy(err_one, errs.at[0], local_sem.at[4]),
        pltpu.make_async_copy(err_two, errs.at[1], local_sem.at[5]),
    ]
    for load in loads:
        load.start()

    barrier = pltpu.get_barrier_semaphore()
    greeted = [{"tile": up}, {"tile": down}]
    greeted += [{"tile": along("y", d)} for d in range(1, 4)]
    greeted += [{"tile": along("z", d)} for d in range(1, 4)]
    greeted += [{"rep": lax.rem(rep + d, 8)} for d in range(1, 8)]
    for device in greeted:
        pl.semaphore_signal(barrier, inc=1, device_id=device, device_id_type=MESH)
    pl.semaphore_wait(barrier, len(greeted))

    remote(lat.at[:, pl.ds(32, 32)], lat_ext.at[:, pl.ds(0, 32)], 0, {"tile": down})
    remote(lat.at[:, pl.ds(0, 32)], lat_ext.at[:, pl.ds(96, 32)], 1, {"tile": up})
    remote(cot.at[:, pl.ds(48, 16)], cot_ext.at[:, pl.ds(0, 16)], 2, {"tile": down})
    remote(cot.at[:, pl.ds(0, 16)], cot_ext.at[:, pl.ds(80, 16)], 3, {"tile": up})

    held = lax.broadcasted_iota(jnp.int32, (256, 128), 0)
    want = lax.broadcasted_iota(jnp.int32, (256, 128), 1)
    same = (held // 128) == (want // 64)
    held, want = held % 128, want % 64
    for b in range(3):
        for e in range(3):
            hit = jnp.logical_and(held // 8 == want // 8 + b, held % 8 == want % 8 + (e - 1))
            hit = jnp.logical_and(same, hit)
            select[:, pl.ds((b * 3 + e) * 128, 128)] = jnp.where(hit, 1.0, 0.0).astype(BF)

    for k in range(2):
        loads[k].wait()

        def reorder(j, carry, k=k):
            rows = pl.ds(pl.multiple_of(j * OWN, OWN), OWN)
            for half in range(2):
                lanes = pl.ds(half * 128, 128)
                chunk[half] = raw[k, rows, lanes].astype(F32)
                for tap in range(27):
                    picked = chunk[half, pl.ds(tap, 16, stride=27), :].astype(BF)
                    at = pl.multiple_of((tap % 9) * C + j * 16, 16)
                    weights[k, tap // 9, pl.ds(at, 16), lanes] = picked
            return carry

        lax.fori_loop(0, 16, reorder, 0)

    loads[2].wait()
    loads[3].wait()
    arrived(lat_ext.at[:, pl.ds(0, 32)], 0)
    arrived(lat_ext.at[:, pl.ds(96, 32)], 1)

    def enter_one(f, carry):
        field = lat_ext[f].astype(F32).reshape(16, WC, C)[1:15]
        field = valid_rows(field, -3, tile)
        turn[0, f] = turned(field[2:12])
        spread(field, f, even, odd)
        return carry

    lax.fori_loop(0, FR, enter_one, 0)
    own = [
        pltpu.make_async_copy(turn.at[0, :, tz], turn_in.at[0, 0], local_sem.at[6]),
        pltpu.make_async_copy(turn.at[1, :, :, ty], turn_in.at[1, 0], local_sem.at[7]),
    ]
    own[0].start()
    for d in range(1, 4):
        to = lax.rem(tz + d, 4)
        remote(turn.at[0, :, to], turn_in.at[0, d], 4 + d, {"tile": along("z", d)})
    conv(even, odd, 12, weights.at[0], acc_one, False)

    def enter_two(f, carry):
        pre = acc_one[f]
        hidden = (pre * sigmoid(pre)).astype(BF).astype(F32).reshape(12, WC, C)
        hidden = valid_rows(hidden, -2, tile)
        turn[1, f] = turned(hidden[1:11])
        spread(hidden, f, even, odd)
        return carry

    lax.fori_loop(0, FR, enter_two, 0)
    own[1].start()
    for d in range(1, 4):
        to = lax.rem(ty + d, 4)
        remote(turn.at[1, :, :, to], turn_in.at[1, d], 8 + d, {"tile": along("y", d)})
    conv(even, odd, 10, weights.at[1], acc_two, False)

    arrived(cot_ext.at[:, pl.ds(0, 16)], 2)
    arrived(cot_ext.at[:, pl.ds(80, 16)], 3)

    def enter_three(f, carry):
        cots = cot_ext[f].astype(F32)[8:88]
        slope = (cots * silu_slope(acc_two[f])).astype(BF).astype(F32).reshape(10, WC, C)
        slope = valid_rows(slope, -1, tile)
        spread(slope, f, even, odd)
        slopes[1, f, 0] = slope[1:9].reshape(64, C).astype(BF)
        return carry

    lax.fori_loop(0, FR, enter_three, 0)
    for d in range(1, 4):
        remote(slopes.at[1, :, 0], slopes.at[1, :, d], 12 + d, {"tile": along("y", d)})
    conv(even, odd, 8, weights.at[1], acc_three, True)

    def leave(f, carry):
        pre = acc_one[f, pl.ds(16, 64), :]
        slopes[0, f, 0] = (acc_three[f] * silu_slope(pre)).astype(BF)
        return carry

    lax.fori_loop(0, FR, leave, 0)
    for d in range(1, 4):
        remote(slopes.at[0, :, 0], slopes.at[0, :, d], 16 + d, {"tile": along("z", d)})

    for k in range(2):
        own[k].wait()
        for d in range(1, 4):
            arrived(turn_in.at[k, d], 4 + 4 * k + d)
        for p in range(2):
            lhs = jnp.concatenate(
                [turn_in[k, 2 * p + s].reshape(320, 128) for s in range(2)], axis=1
            )
            out = jnp.dot(lhs, select[...], preferred_element_type=F32).astype(BF)
            for f in range(FR):
                for i in range(9):
                    block = out[f * 64 : f * 64 + 64, i * 128 : i * 128 + 128]
                    patches[k, pl.ds(i * 64, 64), pl.ds(f * 256 + p * 128, 128)] = block

    for k in (1, 0):
        for d in range(1, 4):
            arrived(slopes.at[k, :, d], 16 - 4 * k + d)
        for a in range(3):
            count = 3 + a
            rhs = slopes[k, pl.ds(2 - a, count)].reshape(count * 256, C)
            out = jnp.dot(patches[k, :, pl.ds(0, count * 256)], rhs, preferred_element_type=F32)
            out = out.reshape(9, 4, 16, C)
            for j in range(4):
                part[k, j, pl.ds(a * 9, 9)] = out[:, j]
                part_half[k, j, pl.ds(a * 9, 9)] = out[:, j].astype(BF)
        axis, mine = ("z", tz) if k else ("y", ty)
        for d in range(1, 4):
            to = lax.rem(mine + d, 4)
            remote(part_half.at[k, to], part_in.at[k, d], 20 + 4 * k + d, {"tile": along(axis, d)})

    for k in (1, 0):
        mine = tz if k else ty
        loads[4 + k].wait()
        for d in range(1, 4):
            arrived(part_in.at[k, d], 20 + 4 * k + d)
        for tap in range(27):
            grad = part[k, mine, tap]
            for d in range(1, 4):
                grad = grad + part_in[k, d, tap].astype(F32)
            for half in range(2):
                chunk[half, pl.ds(tap, 16, stride=27), :] = grad[:, half * 128 : half * 128 + 128]
        for half in range(2):
            lanes = pl.ds(half * 128, 128)
            merged[k, :, lanes] = chunk[half] + errs[k, :, lanes]
        factor = fac_two if k else fac_one
        proj[rep, pl.ds(k * 8, 8), :] = lax.dot_general(
            factor[...], merged[k], NT, precision=HIGH, preferred_element_type=F32
        )

    for d in range(1, 8):
        remote(proj.at[rep], proj.at[rep], 28 + rep, {"rep": lax.rem(rep + d, 8)})
    for d in range(1, 8):
        source = lax.rem(rep + d, 8)
        arrived(proj.at[source], 28 + source)
    left = proj[0]
    for s in range(1, 8):
        left = left + proj[s]
    left = left * 0.125
    left_out[...] = left

    grams = []
    for k in range(2):
        mine = left[k * 8 : k * 8 + 8]
        right_rep[rep, pl.ds(k * 8, 8), :] = jnp.dot(
            mine, merged[k], precision=HIGH, preferred_element_type=F32
        )
        gram = lax.dot_general(mine, mine, NT, precision=HIGH, preferred_element_type=F32)
        grams.append(jnp.concatenate([gram, jnp.zeros((8, 120), F32)], axis=1))
    for d in range(1, 8):
        remote(right_rep.at[rep], right_rep.at[rep], 36 + rep, {"rep": lax.rem(rep + d, 8)})
    for d in range(1, 8):
        source = lax.rem(rep + d, 8)
        arrived(right_rep.at[source], 36 + source)
    right = right_rep[0]
    for s in range(1, 8):
        right = right + right_rep[s]
    right_y[ty, :, pl.ds(0, 256)] = right
    for k in range(2):
        right_y[ty, pl.ds(k * 8, 8), pl.ds(256, 128)] = grams[k]
    for d in range(1, 4):
        remote(right_y.at[ty], right_y.at[ty], 44 + ty, {"tile": along("y", d)})
    for d in range(1, 4):
        source = lax.rem(ty + d, 4)
        arrived(right_y.at[source], 44 + source)
    right_z[tz] = right_y[0] + right_y[1] + right_y[2] + right_y[3]
    for d in range(1, 4):
        remote(right_z.at[tz], right_z.at[tz], 48 + tz, {"tile": along("z", d)})
    for d in range(1, 4):
        source = lax.rem(tz + d, 4)
        arrived(right_z.at[source], 48 + source)
    right_out[...] = right_z[0] + right_z[1] + right_z[2] + right_z[3]

    for copy in sends:
        copy.wait_send()


def finish_kernel(merged, left, right, approx_one, approx_two, fresh_one, fresh_two, new_one, new_two):
    table = jnp.concatenate([left[...], right[...]], axis=1).reshape(2, RANK, OWN + 384)
    row = lax.broadcasted_iota(jnp.int32, table.shape, 1)
    for j in range(RANK):
        column = OWN + C + j
        pivot = table[:, j : j + 1, column : column + 1]
        scaled = table[:, j : j + 1, :] * lax.rsqrt(pivot)
        coefs = table[:, :, column : column + 1] * lax.rsqrt(pivot)
        table = jnp.where(row == j, scaled, jnp.where(row > j, table - coefs * scaled, table))
    for k, (approx_ref, fresh_ref, new_ref) in enumerate(
        ((approx_one, fresh_one, new_one), (approx_two, fresh_two, new_two))
    ):
        basis = table[k, :, 0:OWN]
        factor = table[k, :, OWN : OWN + C] * 0.125
        approx = lax.dot_general(basis, factor, TN, precision=HIGH, preferred_element_type=F32)
        new_ref[...] = factor
        approx_ref[...] = approx
        fresh_ref[...] = merged[k] - approx


def on_device(
    latents, cotangent, kernel_one, kernel_two, error_one, error_two, factor_one, factor_two
):
    vmem = pl.BlockSpec(memory_space=pltpu.VMEM)
    hbm = pl.BlockSpec(memory_space=pl.ANY)
    sds = jax.ShapeDtypeStruct
    merged, left, right = pl.pallas_call(
        train_kernel,
        out_shape=(sds((2, OWN, C), F32), sds((16, OWN), F32), sds((16, 384), F32)),
        in_specs=[hbm] * 6 + [vmem] * 2,
        out_specs=(vmem,) * 3,
        scratch_shapes=[
            pltpu.VMEM((2, 6912, C), BF),
            pltpu.VMEM((2, 3, 9 * C, C), BF),
            pltpu.VMEM((2, OWN, 128), F32),
            pltpu.VMEM((FR, 128, C), BF),
            pltpu.VMEM((FR, 96, C), BF),
            pltpu.VMEM((3, FR, 112, C), BF),
            pltpu.VMEM((3, FR, 96, C), BF),
            pltpu.VMEM((FR, 96, C), F32),
            pltpu.VMEM((FR, 80, C), F32),
            pltpu.VMEM((FR, 64, C), F32),
            pltpu.VMEM((256, 9 * 128), BF),
            pltpu.VMEM((2, FR, 4, 4, 16, 128), BF),
            pltpu.VMEM((2, 4, FR, 4, 16, 128), BF),
            pltpu.VMEM((2, FR, 4, 64, C), BF),
            pltpu.VMEM((2, 9 * 64, FR * 256), BF),
            pltpu.VMEM((2, 4, 27, 16, C), F32),
            pltpu.VMEM((2, 4, 27, 16, C), BF),
            pltpu.VMEM((2, 4, 27, 16, C), BF),
            pltpu.VMEM((2, OWN, C), F32),
            pltpu.VMEM((8, 16, OWN), F32),
            pltpu.VMEM((8, 16, C), F32),
            pltpu.VMEM((4, 16, 384), F32),
            pltpu.VMEM((4, 16, 384), F32),
            pltpu.SemaphoreType.DMA((8,)),
            pltpu.SemaphoreType.DMA((48,)),
            pltpu.SemaphoreType.DMA((52,)),
        ],
        compiler_params=pltpu.CompilerParams(
            collective_id=0, has_side_effects=True, vmem_limit_bytes=60 * 2**20
        ),
        name="train",
    )(
        latents.reshape(FR, 64, C),
        cotangent.reshape(FR, 64, C),
        kernel_one,
        kernel_two,
        error_one[0],
        error_two[0],
        factor_one.T,
        factor_two.T,
    )
    block, small = sds((OWN, C), F32), sds((RANK, C), F32)
    approx_one, approx_two, fresh_one, fresh_two, new_one, new_two = pl.pallas_call(
        finish_kernel,
        out_shape=(block, block, block, block, small, small),
        in_specs=[vmem] * 3,
        out_specs=(vmem,) * 6,
        compiler_params=pltpu.CompilerParams(vmem_limit_bytes=32 * 2**20),
        name="finish",
    )(merged, left, right)
    return approx_one, approx_two, fresh_one[None], fresh_two[None], new_one.T, new_two.T


def solution(mesh):
    placed = (
        P("rep", None, "tile", None, None),
        P("rep", None, "tile", None, None),
        P(),
        P(),
        P("rep", "tile", None),
        P("rep", "tile", None),
        P(),
        P(),
    )
    return jax.shard_map(
        on_device,
        mesh=mesh,
        in_specs=placed,
        out_specs=(
            P("tile", None),
            P("tile", None),
            P("rep", "tile", None),
            P("rep", "tile", None),
            P(),
            P(),
        ),
        check_vma=False,
    )
```

```python
import functools

import jax
import jax.numpy as jnp
from jax import lax
from jax.experimental import pallas as pl
from jax.experimental.pallas import tpu as pltpu
from jax.sharding import PartitionSpec as P

MESH = pl.DeviceIdType.MESH
HIGH = lax.Precision.HIGHEST
BF = jnp.bfloat16
F32 = jnp.float32
FR = 5
WC = 8
C = 256
RANK = 8
OWN = 432
NT = (((1,), (1,)), ((), ()))
TN = (((0,), (0,)), ((), ()))


def sigmoid(v):
    return 1.0 / (1.0 + jnp.exp(-v))


def silu_slope(v):
    sig = sigmoid(v)
    return sig * (1.0 + v * (1.0 - sig))


def valid_rows(field, first, tile):
    row = lax.broadcasted_iota(jnp.int32, field.shape, 0) + first
    inside = jnp.logical_and(
        jnp.logical_or(row >= 0, tile > 0), jnp.logical_or(row < 8, tile < 15)
    )
    return jnp.where(inside, field, 0.0)


def spread(field, frame, even, odd):
    rows = field.shape[0]
    col = lax.broadcasted_iota(jnp.int32, field.shape, 1)
    for e in range(3):
        if e == 1:
            moved = field
        else:
            moved = pltpu.roll(field, 1 if e == 0 else WC - 1, 1)
            moved = jnp.where(col == (0 if e == 0 else WC - 1), 0.0, moved)
        even[e, frame, pl.ds(0, rows * WC), :] = moved.reshape(rows * WC, C).astype(BF)
        inner = moved[1 : rows - 1].reshape((rows - 2) * WC, C)
        odd[e, frame, pl.ds(0, (rows - 2) * WC), :] = inner.astype(BF)


def conv(even, odd, rows, weights, total, reverse):
    for a in (2, 1, 0):
        count = 3 + a
        first_in, first_out = (2 - a, 0) if reverse else (0, 2 - a)
        pieces = []
        for b in range(3):
            for e in range(3):
                bb, ee = (2 - b, 2 - e) if reverse else (b, e)
                source = odd if bb == 1 else even
                start = 16 if bb == 2 else 0
                piece = source[ee, pl.ds(first_in, count), pl.ds(start, rows * WC), :]
                pieces.append(piece.reshape(count * rows * WC, C))
        lhs = jnp.concatenate(pieces, axis=1)
        if reverse:
            taps = [weights[a, pl.ds(i * C, C), :] for i in range(9)]
            out = lax.dot_general(
                lhs, jnp.concatenate(taps, axis=1), NT, preferred_element_type=F32
            )
        else:
            out = jnp.dot(lhs, weights[a], preferred_element_type=F32)
        out = out.reshape(count, rows * WC, C)
        if a == 2:
            total[...] = out
        else:
            total[pl.ds(first_out, count)] += out


def turned(field):
    flat = field.reshape(80, C)
    flat = jnp.concatenate([flat, jnp.zeros((48, C), F32)], axis=0)
    return flat.T.astype(BF).reshape(4, 4, 16, 128)


def split(v):
    high = v.astype(BF)
    rest = v - high.astype(F32)
    mid = rest.astype(BF)
    low = (rest - mid.astype(F32)).astype(BF)
    return jnp.concatenate([high.astype(F32), mid.astype(F32), low.astype(F32)], axis=0).astype(BF)


def train_kernel(
    lat, cot, ker_one, ker_two, err_one, err_two, fac_one, fac_two,
    merged, table,
    raw, weights, chunk, lat_ext, cot_ext, even, odd, acc_one, acc_two, acc_three,
    select, order, turn, turn_in, slopes, patches, part, part_half, part_rest, part_in, errs, err_rows,
    err_proj, thin, proj, proj_in, left_in, lefts, right, grams, right_pair, right_in, right_far, right_all, whole_rows,
    local_sem, send_sem, recv_sem,
):
    tile = lax.axis_index("tile")
    rep = lax.axis_index("rep")
    tz, ty = tile // 4, tile % 4
    rx, core = rep // 2, rep % 2
    near = core * tz + (1 - core) * ty
    other = core * ty + (1 - core) * tz
    here = rx * 4 + near
    pair = {"rep": rx * 2 + 1 - core}
    group = [(dx, dg) for dx in range(4) for dg in range(4) if dx or dg]

    def place(dx, dg):
        return lax.rem(rx + dx, 4) * 4 + lax.rem(near + dg, 4)

    def member(dx, dg):
        z, y = lax.rem(tz + core * dg, 4), lax.rem(ty + (1 - core) * dg, 4)
        return {"rep": lax.rem(rx + dx, 4) * 2 + core, "tile": z * 4 + y}

    def across(d):
        z, y = lax.rem(tz + (1 - core) * d, 4), lax.rem(ty + core * d, 4)
        return {"tile": z * 4 + y}

    def along(axis, d):
        if axis == "z":
            return lax.rem(tz + d, 4) * 4 + ty
        return tz * 4 + lax.rem(ty + d, 4)

    up, down = lax.rem(tile + 15, 16), lax.rem(tile + 1, 16)

    region = pl.when(tile >= 0)
    sends = []
    n_send = [0]

    def remote(src, dst, recv, device):
        copy = pltpu.make_async_remote_copy(
            src_ref=src, dst_ref=dst, send_sem=send_sem.at[n_send[0]], recv_sem=recv_sem.at[recv],
            device_id=device, device_id_type=MESH,
        )
        n_send[0] += 1
        copy.start()
        sends.append(copy)

    def arrived(dst, recv):
        pltpu.make_async_remote_copy(
            src_ref=dst, dst_ref=dst, send_sem=send_sem.at[0], recv_sem=recv_sem.at[recv],
            device_id={"tile": up}, device_id_type=MESH,
        ).wait_recv()

    def send_block(k, d):
        to = {"tile": along("y" if k else "z", d)}
        remote(slopes.at[k, :, 0], slopes.at[k, :, d], 16 - 4 * k + d, to)

    def send_part(k, a, d):
        to = {"tile": along("z" if k else "y", d)}
        target = lax.rem((tz if k else ty) + d, 4)
        remote(part_half.at[k, a, target], part_in.at[k, d, a], 92 + 9 * k + 3 * a + d - 1, to)

    def send_slopes(k):
        factor = split((fac_two if k else fac_one)[...])
        rows = slopes[k, :, 0].reshape(320, C)
        out = lax.dot_general(factor, rows, NT, preferred_element_type=F32)
        thin[k, 0] = out[0:8] + out[8:16] + out[16:24]
        axis = "y" if k else "z"
        for d in range(1, 4):
            remote(thin.at[k, 0], thin.at[k, d], 28 + 4 * k + d, {"tile": along(axis, d)})
        for d in (1, 3, 2) if k else (1, 3):
            send_block(k, d)

    def gradients(k):
        for d in range(1, 4):
            arrived(slopes.at[k, :, d], 16 - 4 * k + d)
        mine = tz if k else ty

        @region
        def _():
            for a in range(3):
                count = 3 + a
                rhs = slopes[k, pl.ds(2 - a, count)].reshape(count * 256, C)
                out = jnp.dot(patches[k, :, pl.ds(0, count * 256)], rhs, preferred_element_type=F32)
                part[k, a] = out.reshape(4, 144, C)
                part[k, a, mine] += err_rows[k, a]
            for a in range(3):
                out = part[k, a]
                half = out.astype(BF)
                part_half[k, a] = half
                part_rest[k, a] = (out - half.astype(F32)).astype(BF)

    loads = [
        pltpu.make_async_copy(ker_one, raw.at[0], local_sem.at[0]),
        pltpu.make_async_copy(ker_two, raw.at[1], local_sem.at[1]),
        pltpu.make_async_copy(lat, lat_ext.at[:, pl.ds(32, 64)], local_sem.at[2]),
        pltpu.make_async_copy(cot, cot_ext.at[:, pl.ds(16, 64)], local_sem.at[3]),
    ]
    for k, err in enumerate((err_one, err_two)):
        for half in range(2):
            lanes = pl.ds(half * 128, 128)
            loads.append(
                pltpu.make_async_copy(err.at[:, lanes], errs.at[k, half], local_sem.at[8 + 2 * k + half])
            )
    for load in loads:
        load.start()

    barrier = pltpu.get_barrier_semaphore()
    greeted = [{"tile": up}, {"tile": down}]
    greeted += [{"tile": along("y", d)} for d in range(1, 4)]
    greeted += [{"tile": along("z", d)} for d in range(1, 4)]
    greeted += [pair] + [member(dx, dg) for dx, dg in group if dx]
    for device in greeted:
        pl.semaphore_signal(barrier, inc=1, device_id=device, device_id_type=MESH)
    pl.semaphore_wait(barrier, len(greeted))

    remote(lat.at[:, pl.ds(32, 32)], lat_ext.at[:, pl.ds(0, 32)], 0, {"tile": down})
    remote(lat.at[:, pl.ds(0, 32)], lat_ext.at[:, pl.ds(96, 32)], 1, {"tile": up})
    remote(cot.at[:, pl.ds(48, 16)], cot_ext.at[:, pl.ds(0, 16)], 2, {"tile": down})
    remote(cot.at[:, pl.ds(0, 16)], cot_ext.at[:, pl.ds(80, 16)], 3, {"tile": up})

    held = lax.broadcasted_iota(jnp.int32, (256, 128), 0)
    want = lax.broadcasted_iota(jnp.int32, (256, 128), 1)
    same = (held // 128) == (want // 64)
    held, want = held % 128, want % 64
    for b in range(3):
        for e in range(3):
            hit = jnp.logical_and(held // 8 == want // 8 + b, held % 8 == want % 8 + (e - 1))
            hit = jnp.logical_and(same, hit)
            select[:, pl.ds((b * 3 + e) * 128, 128)] = jnp.where(hit, 1.0, 0.0).astype(BF)

    source = lax.broadcasted_iota(jnp.int32, (OWN, OWN), 0)
    target = lax.broadcasted_iota(jnp.int32, (OWN, OWN), 1)
    order[...] = jnp.where(target == (source % 16) * 27 + source // 16, 1.0, 0.0).astype(BF)

    for k in range(2):
        loads[k].wait()

        def reorder(j, carry, k=k):
            rows = pl.ds(pl.multiple_of(j * OWN, OWN), OWN)
            for half in range(2):
                lanes = pl.ds(half * 128, 128)
                chunk[half] = raw[k, rows, lanes].astype(F32)
                for tap in range(27):
                    picked = chunk[half, pl.ds(tap, 16, stride=27), :].astype(BF)
                    at = pl.multiple_of((tap % 9) * C + j * 16, 16)
                    weights[k, tap // 9, pl.ds(at, 16), lanes] = picked
            return carry

        lax.fori_loop(0, 16, reorder, 0)

    for k in range(2):
        mine = tz if k else ty
        for half in range(2):
            loads[4 + 2 * k + half].wait()

        @region
        def _(k=k, mine=mine):
            for half in range(2):
                for tap in range(27):
                    rows = errs[k, half, pl.ds(tap, 16, stride=27), :]
                    err_rows[k, tap // 9, pl.ds((tap % 9) * 16, 16), pl.ds(half * 128, 128)] = rows
            out = err_rows[k].reshape(OWN, C)
            high = out.astype(BF)
            rest = (out - high.astype(F32)).astype(BF)
            factor = split((fac_two if k else fac_one)[...])
            out = lax.dot_general(factor, high, NT, preferred_element_type=F32)
            out += lax.dot_general(factor, rest, NT, preferred_element_type=F32)
            out = out[0:8] + out[8:16] + out[16:24]
            err_proj[k] = jnp.concatenate(
                [
                    jnp.where(mine == j, out[:, a * 144 : a * 144 + 144], 0.0)
                    for a in range(3)
                    for j in range(4)
                ],
                axis=1,
            )

    loads[2].wait()
    loads[3].wait()
    arrived(lat_ext.at[:, pl.ds(0, 32)], 0)
    arrived(lat_ext.at[:, pl.ds(96, 32)], 1)

    def enter_one(f, carry):
        field = lat_ext[f].astype(F32).reshape(16, WC, C)[1:15]
        field = valid_rows(field, -3, tile)
        turn[0, f] = turned(field[2:12])
        spread(field, f, even, odd)
        return carry

    lax.fori_loop(0, FR, enter_one, 0)
    own = [
        pltpu.make_async_copy(turn.at[0, :, tz], turn_in.at[0, 0], local_sem.at[6]),
        pltpu.make_async_copy(turn.at[1, :, :, ty], turn_in.at[1, 0], local_sem.at[7]),
    ]
    own[0].start()
    for d in range(1, 4):
        to = lax.rem(tz + d, 4)
        remote(turn.at[0, :, to], turn_in.at[0, d], 4 + d, {"tile": along("z", d)})
    region(lambda: conv(even, odd, 12, weights.at[0], acc_one, False))

    def enter_two(f, carry):
        pre = acc_one[f]
        hidden = (pre * sigmoid(pre)).astype(BF).astype(F32).reshape(12, WC, C)
        hidden = valid_rows(hidden, -2, tile)
        turn[1, f] = turned(hidden[1:11])
        spread(hidden, f, even, odd)
        return carry

    lax.fori_loop(0, FR, enter_two, 0)
    own[1].start()
    for d in range(1, 4):
        to = lax.rem(ty + d, 4)
        remote(turn.at[1, :, :, to], turn_in.at[1, d], 8 + d, {"tile": along("y", d)})
    region(lambda: conv(even, odd, 10, weights.at[1], acc_two, False))

    arrived(cot_ext.at[:, pl.ds(0, 16)], 2)
    arrived(cot_ext.at[:, pl.ds(80, 16)], 3)

    def enter_three(f, carry):
        cots = cot_ext[f].astype(F32)[8:88]
        slope = (cots * silu_slope(acc_two[f])).astype(BF).astype(F32).reshape(10, WC, C)
        slope = valid_rows(slope, -1, tile)
        spread(slope, f, even, odd)
        slopes[1, f, 0] = slope[1:9].reshape(64, C).astype(BF)
        return carry

    lax.fori_loop(0, FR, enter_three, 0)
    send_slopes(1)
    region(lambda: conv(even, odd, 8, weights.at[1], acc_three, True))

    def leave(f, carry):
        pre = acc_one[f, pl.ds(16, 64), :]
        slopes[0, f, 0] = (acc_three[f] * silu_slope(pre)).astype(BF)
        return carry

    lax.fori_loop(0, FR, leave, 0)
    send_slopes(0)

    for k in range(2):
        own[k].wait()
        for d in range(1, 4):
            arrived(turn_in.at[k, d], 4 + 4 * k + d)

        @region
        def _(k=k):
            for p in range(2):
                lhs = jnp.concatenate(
                    [turn_in[k, 2 * p + s].reshape(320, 128) for s in range(2)], axis=1
                )
                out = jnp.dot(lhs, select[...], preferred_element_type=F32).astype(BF)
                for f in range(FR):
                    for i in range(9):
                        for j in range(4):
                            block = out[f * 64 + j * 16 : f * 64 + j * 16 + 16, i * 128 : i * 128 + 128]
                            rows = pl.ds(j * 144 + i * 16, 16)
                            patches[k, rows, pl.ds(f * 256 + p * 128, 128)] = block

    for k in (1, 0):
        for d in range(1, 4):
            arrived(thin.at[k, d], 28 + 4 * k + d)

        @region
        def _(k=k):
            blocks = [thin[k, d] for d in range(4)]
            wide = jnp.concatenate(
                [blocks[d][:, f * 64 : f * 64 + 64] for f in range(FR) for d in range(4)], axis=1
            )
            wide = split(wide)
            outs = []
            for a in range(3):
                count = 3 + a
                out = lax.dot_general(
                    wide[:, (2 - a) * 256 :], patches[k, :, pl.ds(0, count * 256)], NT,
                    preferred_element_type=F32,
                )
                outs.append(out[0:8] + out[8:16] + out[16:24])
            sample = jnp.concatenate(outs, axis=1) + err_proj[k]
            sample = jnp.concatenate([sample, jnp.zeros((8, 2048 - 1728), F32)], axis=1)
            for q in range(16):
                proj[k, q] = sample[:, q * 128 : q * 128 + 128]

    remote(proj.at[1 - core], proj_in, 36, pair)
    arrived(proj_in, 36)
    for q in range(16):
        proj_in[q] = proj_in[q] + proj[core, q]
    for dx, dg in group:
        to = place(dx, dg)
        remote(proj_in.at[to], left_in.at[here], 37 + here, member(dx, dg))
    left_in[here] = proj_in[here]
    send_block(0, 2)

    gradients(1)
    for dx, dg in group:
        source = place(dx, dg)
        arrived(left_in.at[source], 37 + source)
    piece = left_in[0]
    for q in range(1, 16):
        piece = piece + left_in[q]
    lefts[core, here] = piece * 0.125
    for dx, dg in group:
        remote(lefts.at[core, here], lefts.at[core, here], 53 + here, member(dx, dg))
    for a in range(3):
        for d in (1, 3):
            send_part(1, a, d)
    gradients(0)
    for d in (1, 3):
        send_part(0, 2, d)
    for dx, dg in group:
        source = place(dx, dg)
        arrived(lefts.at[core, source], 53 + source)
    remote(lefts.at[core], lefts.at[core], 69, pair)
    arrived(lefts.at[1 - core], 69)

    for k in range(2):

        @region
        def _(k=k):
            whole = jnp.concatenate([lefts[k, q] for q in range(16)], axis=1)[:, 0:1728]
            pieces = split(whole)
            out = jnp.dot(pieces, part_half[k].reshape(1728, C), preferred_element_type=F32)
            out += jnp.dot(pieces, part_rest[k].reshape(1728, C), preferred_element_type=F32)
            right[k] = out[0:8] + out[8:16] + out[16:24]

    remote(right.at[1 - core], right_pair, 70, pair)
    arrived(right_pair, 70)
    right_in[here] = right_pair[...] + right[core]
    for dx, dg in group:
        remote(right_in.at[here], right_in.at[here], 71 + here, member(dx, dg))
    for a in range(2):
        for d in (1, 3):
            send_part(0, a, d)
        send_part(1, a, 2)

    for k in range(2):
        mine = tz if k else ty

        @region
        def _(k=k, mine=mine):
            whole = jnp.concatenate([lefts[k, q] for q in range(16)], axis=1)[:, 0:1728]
            gram = lax.dot_general(whole, whole, NT, precision=HIGH, preferred_element_type=F32)
            grams[k] = jnp.concatenate([gram, jnp.zeros((8, 120), F32)], axis=1)
            rows = []
            for a in range(3):
                found = jnp.zeros((8, 144), F32)
                for j in range(4):
                    at = a * 576 + j * 144
                    found = jnp.where(mine == j, whole[:, at : at + 144], found)
                rows.append(found)
            out = split(jnp.concatenate(rows, axis=1))
            out = jnp.dot(out, order[...], preferred_element_type=F32)
            table[k, :, pl.ds(0, OWN)] = out[0:8] + out[8:16] + out[16:24]

    for dx, dg in group:
        source = place(dx, dg)
        arrived(right_in.at[source], 71 + source)
    total = right_in[0]
    for q in range(1, 16):
        total = total + right_in[q]
    right_far[other, :, pl.ds(0, 256)] = total
    right_far[other, :, pl.ds(256, 128)] = grams[core]
    for d in range(1, 4):
        remote(right_far.at[other], right_far.at[other], 87 + other, across(d))
    send_part(1, 2, 2)
    for a in range(3):
        send_part(0, a, 2)

    for d in range(1, 4):
        source = lax.rem(other + d, 4)
        arrived(right_far.at[source], 87 + source)
    right_all[core] = right_far[0] + right_far[1] + right_far[2] + right_far[3]
    remote(right_all.at[core], right_all.at[core], 91, pair)
    arrived(right_all.at[1 - core], 91)
    table[:, :, pl.ds(512, 384)] = right_all[...]

    stores = []
    for k in (1, 0):
        mine = tz if k else ty
        for a in range(3):
            for d in range(1, 4):
                arrived(part_in.at[k, d, a], 92 + 9 * k + 3 * a + d - 1)

        @region
        def _(k=k, mine=mine):
            for tap in range(27):
                a, rows = tap // 9, pl.ds((tap % 9) * 16, 16)
                grad = part[k, a, mine, rows, :]
                for d in range(1, 4):
                    grad = grad + part_in[k, d, a, rows, :].astype(F32)
                for half in range(2):
                    chunk[half, pl.ds(tap, 16, stride=27), :] = grad[:, half * 128 : half * 128 + 128]
            for half in range(2):
                whole_rows[k, :, pl.ds(half * 128, 128)] = chunk[half]

        stores.append(pltpu.make_async_copy(whole_rows.at[k], merged.at[k], local_sem.at[k]))
        stores[-1].start()
    for store in stores:
        store.wait()
    for copy in sends:
        copy.wait_send()


def finish_kernel(
    merged, table_in, approx_one, approx_two, fresh_one, fresh_two, new_one, new_two,
    table_ref, rows, approx_ref, fresh_ref, sem,
):
    load = pltpu.make_async_copy(table_in, table_ref, sem.at[0])
    load.start()
    loads = [pltpu.make_async_copy(merged.at[k], rows.at[k], sem.at[1 + k]) for k in range(2)]
    for copy in loads:
        copy.start()
    load.wait()
    table = table_ref[...]
    row = lax.broadcasted_iota(jnp.int32, table.shape, 1)
    for j in range(RANK):
        column = 512 + C + j
        scale = lax.rsqrt(table[:, j : j + 1, column : column + 1])
        scaled = table[:, j : j + 1, :] * scale
        coefs = table[:, :, column : column + 1] * scale
        table = jnp.where(row == j, scaled, jnp.where(row > j, table - coefs * scaled, table))
    stores = []
    for k, (approx_out, fresh_out, new_ref) in enumerate(
        ((approx_one, fresh_one, new_one), (approx_two, fresh_two, new_two))
    ):
        basis = table[k, :, 0:OWN]
        factor = table[k, :, 512 : 512 + C] * 0.125
        approx = lax.dot_general(basis, factor, TN, precision=HIGH, preferred_element_type=F32)
        new_ref[...] = factor
        approx_ref[k] = approx
        stores.append(pltpu.make_async_copy(approx_ref.at[k], approx_out, sem.at[3 + k]))
        stores[-1].start()
        loads[k].wait()
        fresh_ref[k] = rows[k] - approx
        stores.append(pltpu.make_async_copy(fresh_ref.at[k], fresh_out, sem.at[5 + k]))
        stores[-1].start()
    for copy in stores:
        copy.wait()


def on_device(
    latents, cotangent, kernel_one, kernel_two, error_one, error_two, factor_one, factor_two
):
    vmem = pl.BlockSpec(memory_space=pltpu.VMEM)
    hbm = pl.BlockSpec(memory_space=pl.ANY)
    sds = jax.ShapeDtypeStruct
    merged, table = pl.pallas_call(
        train_kernel,
        out_shape=(sds((2, OWN, C), F32), sds((2, RANK, 896), F32)),
        in_specs=[hbm] * 6 + [vmem] * 2,
        out_specs=(hbm, vmem),
        scratch_shapes=[
            pltpu.VMEM((2, 6912, C), BF),
            pltpu.VMEM((2, 3, 9 * C, C), BF),
            pltpu.VMEM((2, OWN, 128), F32),
            pltpu.VMEM((FR, 128, C), BF),
            pltpu.VMEM((FR, 96, C), BF),
            pltpu.VMEM((3, FR, 112, C), BF),
            pltpu.VMEM((3, FR, 96, C), BF),
            pltpu.VMEM((FR, 96, C), F32),
            pltpu.VMEM((FR, 80, C), F32),
            pltpu.VMEM((FR, 64, C), F32),
            pltpu.VMEM((256, 9 * 128), BF),
            pltpu.VMEM((OWN, OWN), BF),
            pltpu.VMEM((2, FR, 4, 4, 16, 128), BF),
            pltpu.VMEM((2, 4, FR, 4, 16, 128), BF),
            pltpu.VMEM((2, FR, 4, 64, C), BF),
            pltpu.VMEM((2, 9 * 64, FR * 256), BF),
            pltpu.VMEM((2, 3, 4, 144, C), F32),
            pltpu.VMEM((2, 3, 4, 144, C), BF),
            pltpu.VMEM((2, 3, 4, 144, C), BF),
            pltpu.VMEM((2, 4, 3, 144, C), BF),
            pltpu.VMEM((2, 2, OWN, 128), F32),
            pltpu.VMEM((2, 3, 144, C), F32),
            pltpu.VMEM((2, 8, 1728), F32),
            pltpu.VMEM((2, 4, 8, 320), F32),
            pltpu.VMEM((2, 16, 8, 128), F32),
            pltpu.VMEM((16, 8, 128), F32),
            pltpu.VMEM((16, 8, 128), F32),
            pltpu.VMEM((2, 16, 8, 128), F32),
            pltpu.VMEM((2, 8, C), F32),
            pltpu.VMEM((2, 8, 128), F32),
            pltpu.VMEM((8, C), F32),
            pltpu.VMEM((16, 8, C), F32),
            pltpu.VMEM((4, 8, 384), F32),
            pltpu.VMEM((2, 8, 384), F32),
            pltpu.VMEM((2, OWN, C), F32),
            pltpu.SemaphoreType.DMA((12,)),
            pltpu.SemaphoreType.DMA((96,)),
            pltpu.SemaphoreType.DMA((110,)),
        ],
        compiler_params=pltpu.CompilerParams(
            collective_id=0, has_side_effects=True, vmem_limit_bytes=60 * 2**20
        ),
        name="train",
    )(
        latents.reshape(FR, 64, C),
        cotangent.reshape(FR, 64, C),
        kernel_one,
        kernel_two,
        error_one[0],
        error_two[0],
        factor_one.T,
        factor_two.T,
    )
    block, small = sds((OWN, C), F32), sds((RANK, C), F32)
    approx_one, approx_two, fresh_one, fresh_two, new_one, new_two = pl.pallas_call(
        finish_kernel,
        out_shape=(block, block, block, block, small, small),
        in_specs=[hbm] * 2,
        out_specs=(hbm,) * 4 + (vmem,) * 2,
        scratch_shapes=[
            pltpu.VMEM((2, RANK, 896), F32),
            pltpu.VMEM((2, OWN, C), F32),
            pltpu.VMEM((2, OWN, C), F32),
            pltpu.VMEM((2, OWN, C), F32),
            pltpu.SemaphoreType.DMA((7,)),
        ],
        compiler_params=pltpu.CompilerParams(vmem_limit_bytes=60 * 2**20),
        name="finish",
    )(merged, table)
    return approx_one, approx_two, fresh_one[None], fresh_two[None], new_one.T, new_two.T


def solution(mesh):
    placed = (
        P("rep", None, "tile", None, None),
        P("rep", None, "tile", None, None),
        P(),
        P(),
        P("rep", "tile", None),
        P("rep", "tile", None),
        P(),
        P(),
    )
    return jax.shard_map(
        on_device,
        mesh=mesh,
        in_specs=placed,
        out_specs=(
            P("tile", None),
            P("tile", None),
            P("rep", "tile", None),
            P("rep", "tile", None),
            P(),
            P(),
        ),
        check_vma=False,
    )
```

```python
import functools

import jax
import jax.numpy as jnp
from jax import lax
from jax.experimental import pallas as pl
from jax.experimental.pallas import tpu as pltpu
from jax.sharding import PartitionSpec as P

MESH = pl.DeviceIdType.MESH
HIGH = lax.Precision.HIGHEST
BF = jnp.bfloat16
F32 = jnp.float32
FR = 5
WC = 8
C = 256
RANK = 8
OWN = 432
NT = (((1,), (1,)), ((), ()))
TN = (((0,), (0,)), ((), ()))


def sigmoid(v):
    return 1.0 / (1.0 + jnp.exp(-v))


def silu_slope(v):
    sig = sigmoid(v)
    return sig * (1.0 + v * (1.0 - sig))


def valid_rows(field, first, tile):
    row = lax.broadcasted_iota(jnp.int32, field.shape, 0) + first
    inside = jnp.logical_and(
        jnp.logical_or(row >= 0, tile > 0), jnp.logical_or(row < 8, tile < 15)
    )
    return jnp.where(inside, field, 0.0)


def spread(field, frame, even, odd):
    rows = field.shape[0]
    col = lax.broadcasted_iota(jnp.int32, field.shape, 1)
    for e in range(3):
        if e == 1:
            moved = field
        else:
            moved = pltpu.roll(field, 1 if e == 0 else WC - 1, 1)
            moved = jnp.where(col == (0 if e == 0 else WC - 1), 0.0, moved)
        even[e, frame, pl.ds(0, rows * WC), :] = moved.reshape(rows * WC, C).astype(BF)
        inner = moved[1 : rows - 1].reshape((rows - 2) * WC, C)
        odd[e, frame, pl.ds(0, (rows - 2) * WC), :] = inner.astype(BF)


def conv(even, odd, rows, weights, total, reverse):
    for a in (2, 1, 0):
        count = 3 + a
        first_in, first_out = (2 - a, 0) if reverse else (0, 2 - a)
        pieces = []
        for b in range(3):
            for e in range(3):
                bb, ee = (2 - b, 2 - e) if reverse else (b, e)
                source = odd if bb == 1 else even
                start = 16 if bb == 2 else 0
                piece = source[ee, pl.ds(first_in, count), pl.ds(start, rows * WC), :]
                pieces.append(piece.reshape(count * rows * WC, C))
        lhs = jnp.concatenate(pieces, axis=1)
        if reverse:
            taps = [weights[a, pl.ds(i * C, C), :] for i in range(9)]
            out = lax.dot_general(
                lhs, jnp.concatenate(taps, axis=1), NT, preferred_element_type=F32
            )
        else:
            out = jnp.dot(lhs, weights[a], preferred_element_type=F32)
        out = out.reshape(count, rows * WC, C)
        if a == 2:
            total[...] = out
        else:
            total[pl.ds(first_out, count)] += out


def turned(field):
    flat = field.reshape(80, C)
    flat = jnp.concatenate([flat, jnp.zeros((48, C), F32)], axis=0)
    return flat.T.astype(BF).reshape(4, 4, 16, 128)


def split(v):
    high = v.astype(BF)
    rest = v - high.astype(F32)
    mid = rest.astype(BF)
    low = (rest - mid.astype(F32)).astype(BF)
    return jnp.concatenate([high.astype(F32), mid.astype(F32), low.astype(F32)], axis=0).astype(BF)


def train_kernel(
    lat, cot, ker_one, ker_two, err_one, err_two, fac_one, fac_two,
    merged, table,
    raw, weights, chunk, lat_ext, cot_ext, even, odd, acc_one, acc_two, acc_three,
    select, order, turn, turn_in, slopes, patches, part, part_half, part_rest, part_in, errs, err_rows,
    err_proj, thin, proj, proj_in, left_in, lefts, right, grams, right_pair, right_in, right_far, right_all, whole_rows,
    local_sem, send_sem, recv_sem,
):
    tile = lax.axis_index("tile")
    rep = lax.axis_index("rep")
    tz, ty = tile // 4, tile % 4
    rx, core = rep // 2, rep % 2
    near = core * tz + (1 - core) * ty
    other = core * ty + (1 - core) * tz
    here = rx * 4 + near
    pair = {"rep": rx * 2 + 1 - core}
    group = [(dx, dg) for dx in range(4) for dg in range(4) if dx or dg]

    def place(dx, dg):
        return lax.rem(rx + dx, 4) * 4 + lax.rem(near + dg, 4)

    def member(dx, dg):
        z, y = lax.rem(tz + core * dg, 4), lax.rem(ty + (1 - core) * dg, 4)
        return {"rep": lax.rem(rx + dx, 4) * 2 + core, "tile": z * 4 + y}

    def across(d):
        z, y = lax.rem(tz + (1 - core) * d, 4), lax.rem(ty + core * d, 4)
        return {"tile": z * 4 + y}

    def along(axis, d):
        if axis == "z":
            return lax.rem(tz + d, 4) * 4 + ty
        return tz * 4 + lax.rem(ty + d, 4)

    up, down = lax.rem(tile + 15, 16), lax.rem(tile + 1, 16)

    region = pl.when(tile >= 0)
    totals = {}

    def remote(src, dst, phase, device, total=None):
        if phase not in totals:
            totals[phase] = dst if total is None else total
        pltpu.make_async_remote_copy(
            src_ref=src, dst_ref=dst, send_sem=send_sem.at[phase], recv_sem=recv_sem.at[phase],
            device_id=device, device_id_type=MESH,
        ).start()

    def whole(phase):
        ref = totals[phase]
        return pltpu.make_async_remote_copy(
            src_ref=ref, dst_ref=ref, send_sem=send_sem.at[phase], recv_sem=recv_sem.at[phase],
            device_id={"tile": up}, device_id_type=MESH,
        )

    def arrived(phase):
        whole(phase).wait_recv()

    def send_block(k, d):
        to = {"tile": along("y" if k else "z", d)}
        for f in range(FR):
            remote(slopes.at[k, f, 0], slopes.at[k, f, d], 8 + k, to, slopes.at[k, :, pl.ds(1, 3)])

    def send_part(k, a, d):
        to = {"tile": along("z" if k else "y", d)}
        target = lax.rem((tz if k else ty) + d, 4)
        total = part_in.at[k, pl.ds(1, 3)]
        remote(part_half.at[k, a, target], part_in.at[k, d, a], 10 + k, to, total)

    def send_slopes(k):
        factor = split((fac_two if k else fac_one)[...])
        rows = slopes[k, :, 0].reshape(320, C)
        out = lax.dot_general(factor, rows, NT, preferred_element_type=F32)
        thin[k, 0] = out[0:8] + out[8:16] + out[16:24]
        axis = "y" if k else "z"
        for d in range(1, 4):
            to = {"tile": along(axis, d)}
            remote(thin.at[k, 0], thin.at[k, d], 6 + k, to, thin.at[k, pl.ds(1, 3)])
        for d in (1, 3, 2) if k else (1, 3):
            send_block(k, d)

    def gradients(k):
        arrived(8 + k)
        mine = tz if k else ty

        @region
        def _():
            for a in range(3):
                count = 3 + a
                rhs = slopes[k, pl.ds(2 - a, count)].reshape(count * 256, C)
                out = jnp.dot(patches[k, :, pl.ds(0, count * 256)], rhs, preferred_element_type=F32)
                part[k, a] = out.reshape(4, 144, C)
                part[k, a, mine] += err_rows[k, a]
            for a in range(3):
                out = part[k, a]
                half = out.astype(BF)
                part_half[k, a] = half
                part_rest[k, a] = (out - half.astype(F32)).astype(BF)

    def project_errors():
        for k in range(2):
            mine = tz if k else ty
            for half in range(2):
                loads[4 + 2 * k + half].wait()

            @region
            def _(k=k, mine=mine):
                for half in range(2):
                    for tap in range(27):
                        rows = errs[k, half, pl.ds(tap, 16, stride=27), :]
                        err_rows[k, tap // 9, pl.ds((tap % 9) * 16, 16), pl.ds(half * 128, 128)] = rows
                out = err_rows[k].reshape(OWN, C)
                high = out.astype(BF)
                rest = (out - high.astype(F32)).astype(BF)
                factor = split((fac_two if k else fac_one)[...])
                out = lax.dot_general(factor, high, NT, preferred_element_type=F32)
                out += lax.dot_general(factor, rest, NT, preferred_element_type=F32)
                out = out[0:8] + out[8:16] + out[16:24]
                err_proj[k] = jnp.concatenate(
                    [
                        jnp.where(mine == j, out[:, a * 144 : a * 144 + 144], 0.0)
                        for a in range(3)
                        for j in range(4)
                    ],
                    axis=1,
                )

    loads = [
        pltpu.make_async_copy(ker_one, raw.at[0], local_sem.at[0]),
        pltpu.make_async_copy(ker_two, raw.at[1], local_sem.at[1]),
        pltpu.make_async_copy(lat, lat_ext.at[:, pl.ds(32, 64)], local_sem.at[2]),
        pltpu.make_async_copy(cot, cot_ext.at[:, pl.ds(16, 64)], local_sem.at[3]),
    ]
    for k, err in enumerate((err_one, err_two)):
        for half in range(2):
            lanes = pl.ds(half * 128, 128)
            loads.append(
                pltpu.make_async_copy(err.at[:, lanes], errs.at[k, half], local_sem.at[8 + 2 * k + half])
            )
    for load in loads:
        load.start()

    barrier = pltpu.get_barrier_semaphore()
    greeted = [{"tile": up}, {"tile": down}]
    greeted += [{"tile": along("y", d)} for d in range(1, 4)]
    greeted += [{"tile": along("z", d)} for d in range(1, 4)]
    greeted += [pair] + [member(dx, dg) for dx, dg in group if dx]
    for device in greeted:
        pl.semaphore_signal(barrier, inc=1, device_id=device, device_id_type=MESH)
    held = lax.broadcasted_iota(jnp.int32, (256, 128), 0)
    want = lax.broadcasted_iota(jnp.int32, (256, 128), 1)
    same = (held // 128) == (want // 64)
    held, want = held % 128, want % 64
    for b in range(3):
        for e in range(3):
            hit = jnp.logical_and(held // 8 == want // 8 + b, held % 8 == want % 8 + (e - 1))
            hit = jnp.logical_and(same, hit)
            select[:, pl.ds((b * 3 + e) * 128, 128)] = jnp.where(hit, 1.0, 0.0).astype(BF)

    source = lax.broadcasted_iota(jnp.int32, (OWN, OWN), 0)
    target = lax.broadcasted_iota(jnp.int32, (OWN, OWN), 1)
    order[...] = jnp.where(target == (source % 16) * 27 + source // 16, 1.0, 0.0).astype(BF)

    pl.semaphore_wait(barrier, len(greeted))

    remote(lat.at[:, pl.ds(32, 32)], lat_ext.at[:, pl.ds(0, 32)], 0, {"tile": down})
    remote(lat.at[:, pl.ds(0, 32)], lat_ext.at[:, pl.ds(96, 32)], 1, {"tile": up})
    remote(cot.at[:, pl.ds(48, 16)], cot_ext.at[:, pl.ds(0, 16)], 2, {"tile": down})
    remote(cot.at[:, pl.ds(0, 16)], cot_ext.at[:, pl.ds(80, 16)], 3, {"tile": up})

    for k in range(2):
        loads[k].wait()

        def reorder(j, carry, k=k):
            rows = pl.ds(pl.multiple_of(j * OWN, OWN), OWN)
            for half in range(2):
                lanes = pl.ds(half * 128, 128)
                chunk[half] = raw[k, rows, lanes].astype(F32)
                for tap in range(27):
                    picked = chunk[half, pl.ds(tap, 16, stride=27), :].astype(BF)
                    at = pl.multiple_of((tap % 9) * C + j * 16, 16)
                    weights[k, tap // 9, pl.ds(at, 16), lanes] = picked
            return carry

        lax.fori_loop(0, 16, reorder, 0)

    loads[2].wait()
    loads[3].wait()
    arrived(0)
    arrived(1)

    def enter_one(f, carry):
        field = lat_ext[f].astype(F32).reshape(16, WC, C)[1:15]
        field = valid_rows(field, -3, tile)
        turn[0, f] = turned(field[2:12])
        spread(field, f, even, odd)
        return carry

    lax.fori_loop(0, FR, enter_one, 0)
    own = [
        pltpu.make_async_copy(turn.at[0, :, tz], turn_in.at[0, 0], local_sem.at[6]),
        pltpu.make_async_copy(turn.at[1, :, :, ty], turn_in.at[1, 0], local_sem.at[7]),
    ]
    own[0].start()
    for d in range(1, 4):
        to = lax.rem(tz + d, 4)
        remote(turn.at[0, :, to], turn_in.at[0, d], 4, {"tile": along("z", d)}, turn_in.at[0, pl.ds(1, 3)])
    region(lambda: conv(even, odd, 12, weights.at[0], acc_one, False))

    totals[5] = turn_in.at[1, pl.ds(1, 3)]
    def enter_two(f, carry):
        pre = acc_one[f]
        hidden = (pre * sigmoid(pre)).astype(BF).astype(F32).reshape(12, WC, C)
        hidden = valid_rows(hidden, -2, tile)
        turn[1, f] = turned(hidden[1:11])
        for d in range(1, 4):
            to = lax.rem(ty + d, 4)
            remote(turn.at[1, f, :, to], turn_in.at[1, d, f], 5, {"tile": along("y", d)})
        spread(hidden, f, even, odd)
        return carry

    lax.fori_loop(0, FR, enter_two, 0)
    own[1].start()
    region(lambda: conv(even, odd, 10, weights.at[1], acc_two, False))

    arrived(2)
    arrived(3)

    def enter_three(f, carry):
        cots = cot_ext[f].astype(F32)[8:88]
        slope = (cots * silu_slope(acc_two[f])).astype(BF).astype(F32).reshape(10, WC, C)
        slope = valid_rows(slope, -1, tile)
        spread(slope, f, even, odd)
        slopes[1, f, 0] = slope[1:9].reshape(64, C).astype(BF)
        return carry

    lax.fori_loop(0, FR, enter_three, 0)
    send_slopes(1)
    region(lambda: conv(even, odd, 8, weights.at[1], acc_three, True))

    def leave(f, carry):
        pre = acc_one[f, pl.ds(16, 64), :]
        slopes[0, f, 0] = (acc_three[f] * silu_slope(pre)).astype(BF)
        return carry

    lax.fori_loop(0, FR, leave, 0)
    send_slopes(0)

    for k in range(2):
        if k == 1:
            project_errors()
        own[k].wait()
        arrived(4 + k)

        @region
        def _(k=k):
            for p in range(2):
                lhs = jnp.concatenate(
                    [turn_in[k, 2 * p + s].reshape(320, 128) for s in range(2)], axis=1
                )
                out = jnp.dot(lhs, select[...], preferred_element_type=F32).astype(BF)
                for f in range(FR):
                    for i in range(9):
                        for j in range(4):
                            block = out[f * 64 + j * 16 : f * 64 + j * 16 + 16, i * 128 : i * 128 + 128]
                            rows = pl.ds(j * 144 + i * 16, 16)
                            patches[k, rows, pl.ds(f * 256 + p * 128, 128)] = block

    for k in (1, 0):
        arrived(6 + k)

        @region
        def _(k=k):
            blocks = [thin[k, d] for d in range(4)]
            wide = jnp.concatenate(
                [blocks[d][:, f * 64 : f * 64 + 64] for f in range(FR) for d in range(4)], axis=1
            )
            shifts = [
                jnp.concatenate([wide[:, (2 - a) * 256 :], jnp.zeros((8, (2 - a) * 256), F32)], axis=1)
                if a < 2
                else wide
                for a in range(3)
            ]
            wide = split(jnp.concatenate(shifts, axis=0))
            out = lax.dot_general(wide, patches[k], NT, preferred_element_type=F32)
            out = out[0:24] + out[24:48] + out[48:72]
            out = jnp.concatenate([out[0:8], out[8:16], out[16:24]], axis=1)
            sample = out + err_proj[k]
            sample = jnp.concatenate([sample, jnp.zeros((8, 2048 - 1728), F32)], axis=1)
            for q in range(16):
                proj[k, q] = sample[:, q * 128 : q * 128 + 128]

    remote(proj.at[1 - core], proj_in, 12, pair)
    arrived(12)
    for q in range(16):
        proj_in[q] = proj_in[q] + proj[core, q]
    for dx, dg in group:
        to = place(dx, dg)
        remote(proj_in.at[to], left_in.at[here], 13, member(dx, dg), left_in.at[pl.ds(0, 15)])
    left_in[here] = proj_in[here]
    send_block(0, 2)

    arrived(13)
    piece = left_in[0]
    for q in range(1, 16):
        piece = piece + left_in[q]
    lefts[core, here] = piece * 0.125
    for dx, dg in group:
        block = lefts.at[core, here]
        remote(block, block, 14, member(dx, dg), lefts.at[0, pl.ds(0, 15)])
    gradients(1)
    for a in range(3):
        for d in (1, 3):
            send_part(1, a, d)
    gradients(0)
    for a in (2, 1):
        for d in (1, 3):
            send_part(0, a, d)
    arrived(14)
    remote(lefts.at[core], lefts.at[core], 15, pair)
    arrived(15)

    for k in range(2):

        @region
        def _(k=k):
            rows_all = jnp.concatenate([lefts[k, q] for q in range(16)], axis=1)[:, 0:1728]
            pieces = split(rows_all)
            out = jnp.dot(pieces, part_half[k].reshape(1728, C), preferred_element_type=F32)
            out += jnp.dot(pieces, part_rest[k].reshape(1728, C), preferred_element_type=F32)
            right[k] = out[0:8] + out[8:16] + out[16:24]

    remote(right.at[1 - core], right_pair, 16, pair)
    arrived(16)
    right_in[here] = right_pair[...] + right[core]
    for dx, dg in group:
        block = right_in.at[here]
        remote(block, block, 17, member(dx, dg), right_in.at[pl.ds(0, 15)])
    for d in (1, 3):
        send_part(0, 0, d)
    send_part(0, 2, 2)
    for a in range(2):
        send_part(1, a, 2)

    for k in range(2):
        mine = tz if k else ty

        @region
        def _(k=k, mine=mine):
            rows_all = jnp.concatenate([lefts[k, q] for q in range(16)], axis=1)[:, 0:1728]
            gram = lax.dot_general(rows_all, rows_all, NT, precision=HIGH, preferred_element_type=F32)
            grams[k] = jnp.concatenate([gram, jnp.zeros((8, 120), F32)], axis=1)
            rows = []
            for a in range(3):
                found = jnp.zeros((8, 144), F32)
                for j in range(4):
                    at = a * 576 + j * 144
                    found = jnp.where(mine == j, rows_all[:, at : at + 144], found)
                rows.append(found)
            out = split(jnp.concatenate(rows, axis=1))
            out = jnp.dot(out, order[...], preferred_element_type=F32)
            table[k, :, pl.ds(0, OWN)] = out[0:8] + out[8:16] + out[16:24]

    arrived(17)
    total = right_in[0]
    for q in range(1, 16):
        total = total + right_in[q]
    right_far[other, :, pl.ds(0, 256)] = total
    right_far[other, :, pl.ds(256, 128)] = grams[core]
    for d in range(1, 4):
        block = right_far.at[other]
        remote(block, block, 18, across(d), right_far.at[pl.ds(0, 3)])
    send_part(1, 2, 2)
    for a in range(2):
        send_part(0, a, 2)

    arrived(18)
    right_all[core] = right_far[0] + right_far[1] + right_far[2] + right_far[3]
    remote(right_all.at[core], right_all.at[core], 19, pair)
    stores = []
    for k in (1, 0):
        mine = tz if k else ty
        arrived(10 + k)

        @region
        def _(k=k, mine=mine):
            for tap in range(27):
                a, rows = tap // 9, pl.ds((tap % 9) * 16, 16)
                grad = part[k, a, mine, rows, :]
                for d in range(1, 4):
                    grad = grad + part_in[k, d, a, rows, :].astype(F32)
                for half in range(2):
                    chunk[half, pl.ds(tap, 16, stride=27), :] = grad[:, half * 128 : half * 128 + 128]
            for half in range(2):
                whole_rows[k, :, pl.ds(half * 128, 128)] = chunk[half]

        stores.append(pltpu.make_async_copy(whole_rows.at[k], merged.at[k], local_sem.at[k]))
        stores[-1].start()
    arrived(19)
    table[:, :, pl.ds(512, 384)] = right_all[...]

    for store in stores:
        store.wait()
    for phase in totals:
        whole(phase).wait_send()


def finish_kernel(
    merged, table_in, approx_one, approx_two, fresh_one, fresh_two, new_one, new_two,
    table_ref, rows, approx_ref, fresh_ref, sem,
):
    load = pltpu.make_async_copy(table_in, table_ref, sem.at[0])
    load.start()
    loads = [pltpu.make_async_copy(merged.at[k], rows.at[k], sem.at[1 + k]) for k in range(2)]
    for copy in loads:
        copy.start()
    load.wait()
    table = table_ref[...]
    row = lax.broadcasted_iota(jnp.int32, table.shape, 1)
    for j in range(RANK):
        column = 512 + C + j
        scale = lax.rsqrt(table[:, j : j + 1, column : column + 1])
        scaled = table[:, j : j + 1, :] * scale
        coefs = table[:, :, column : column + 1] * scale
        table = jnp.where(row == j, scaled, jnp.where(row > j, table - coefs * scaled, table))
    stores = []
    for k, (approx_out, fresh_out, new_ref) in enumerate(
        ((approx_one, fresh_one, new_one), (approx_two, fresh_two, new_two))
    ):
        basis = table[k, :, 0:OWN]
        factor = table[k, :, 512 : 512 + C] * 0.125
        b, f = split(basis).astype(F32), split(factor)
        b = jnp.concatenate([b[0:8], b[0:8], b[0:8], b[8:16], b[8:16], b[16:24]], axis=0)
        f = jnp.concatenate([f[0:24].astype(F32), f[0:16].astype(F32), f[0:8].astype(F32)], axis=0)
        approx = lax.dot_general(b.astype(BF), f.astype(BF), TN, preferred_element_type=F32)
        new_ref[...] = factor
        approx_ref[k] = approx
        stores.append(pltpu.make_async_copy(approx_ref.at[k], approx_out, sem.at[3 + k]))
        stores[-1].start()
        loads[k].wait()
        fresh_ref[k] = rows[k] - approx
        stores.append(pltpu.make_async_copy(fresh_ref.at[k], fresh_out, sem.at[5 + k]))
        stores[-1].start()
    for copy in stores:
        copy.wait()


def on_device(
    latents, cotangent, kernel_one, kernel_two, error_one, error_two, factor_one, factor_two
):
    vmem = pl.BlockSpec(memory_space=pltpu.VMEM)
    hbm = pl.BlockSpec(memory_space=pl.ANY)
    sds = jax.ShapeDtypeStruct
    merged, table = pl.pallas_call(
        train_kernel,
        out_shape=(sds((2, OWN, C), F32), sds((2, RANK, 896), F32)),
        in_specs=[hbm] * 6 + [vmem] * 2,
        out_specs=(hbm, vmem),
        scratch_shapes=[
            pltpu.VMEM((2, 6912, C), BF),
            pltpu.VMEM((2, 3, 9 * C, C), BF),
            pltpu.VMEM((2, OWN, 128), F32),
            pltpu.VMEM((FR, 128, C), BF),
            pltpu.VMEM((FR, 96, C), BF),
            pltpu.VMEM((3, FR, 112, C), BF),
            pltpu.VMEM((3, FR, 96, C), BF),
            pltpu.VMEM((FR, 96, C), F32),
            pltpu.VMEM((FR, 80, C), F32),
            pltpu.VMEM((FR, 64, C), F32),
            pltpu.VMEM((256, 9 * 128), BF),
            pltpu.VMEM((OWN, OWN), BF),
            pltpu.VMEM((2, FR, 4, 4, 16, 128), BF),
            pltpu.VMEM((2, 4, FR, 4, 16, 128), BF),
            pltpu.VMEM((2, FR, 4, 64, C), BF),
            pltpu.VMEM((2, 9 * 64, FR * 256), BF),
            pltpu.VMEM((2, 3, 4, 144, C), F32),
            pltpu.VMEM((2, 3, 4, 144, C), BF),
            pltpu.VMEM((2, 3, 4, 144, C), BF),
            pltpu.VMEM((2, 4, 3, 144, C), BF),
            pltpu.VMEM((2, 2, OWN, 128), F32),
            pltpu.VMEM((2, 3, 144, C), F32),
            pltpu.VMEM((2, 8, 1728), F32),
            pltpu.VMEM((2, 4, 8, 320), F32),
            pltpu.VMEM((2, 16, 8, 128), F32),
            pltpu.VMEM((16, 8, 128), F32),
            pltpu.VMEM((16, 8, 128), F32),
            pltpu.VMEM((2, 16, 8, 128), F32),
            pltpu.VMEM((2, 8, C), F32),
            pltpu.VMEM((2, 8, 128), F32),
            pltpu.VMEM((8, C), F32),
            pltpu.VMEM((16, 8, C), F32),
            pltpu.VMEM((4, 8, 384), F32),
            pltpu.VMEM((2, 8, 384), F32),
            pltpu.VMEM((2, OWN, C), F32),
            pltpu.SemaphoreType.DMA((12,)),
            pltpu.SemaphoreType.DMA((20,)),
            pltpu.SemaphoreType.DMA((20,)),
        ],
        compiler_params=pltpu.CompilerParams(
            collective_id=0, has_side_effects=True, vmem_limit_bytes=60 * 2**20
        ),
        name="train",
    )(
        latents.reshape(FR, 64, C),
        cotangent.reshape(FR, 64, C),
        kernel_one,
        kernel_two,
        error_one[0],
        error_two[0],
        factor_one.T,
        factor_two.T,
    )
    block, small = sds((OWN, C), F32), sds((RANK, C), F32)
    approx_one, approx_two, fresh_one, fresh_two, new_one, new_two = pl.pallas_call(
        finish_kernel,
        out_shape=(block, block, block, block, small, small),
        in_specs=[hbm] * 2,
        out_specs=(hbm,) * 4 + (vmem,) * 2,
        scratch_shapes=[
            pltpu.VMEM((2, RANK, 896), F32),
            pltpu.VMEM((2, OWN, C), F32),
            pltpu.VMEM((2, OWN, C), F32),
            pltpu.VMEM((2, OWN, C), F32),
            pltpu.SemaphoreType.DMA((7,)),
        ],
        compiler_params=pltpu.CompilerParams(vmem_limit_bytes=60 * 2**20),
        name="finish",
    )(merged, table)
    return approx_one, approx_two, fresh_one[None], fresh_two[None], new_one.T, new_two.T


def solution(mesh):
    placed = (
        P("rep", None, "tile", None, None),
        P("rep", None, "tile", None, None),
        P(),
        P(),
        P("rep", "tile", None),
        P("rep", "tile", None),
        P(),
        P(),
    )
    return jax.shard_map(
        on_device,
        mesh=mesh,
        in_specs=placed,
        out_specs=(
            P("tile", None),
            P("tile", None),
            P("rep", "tile", None),
            P("rep", "tile", None),
            P(),
            P(),
        ),
        check_vma=False,
    )
```

```python
import functools

import jax
import jax.numpy as jnp
from jax import lax
from jax.experimental import pallas as pl
from jax.experimental.pallas import tpu as pltpu
from jax.sharding import PartitionSpec as P

MESH = pl.DeviceIdType.MESH
HIGH = lax.Precision.HIGHEST
BF = jnp.bfloat16
F32 = jnp.float32
FR = 5
WC = 8
C = 256
RANK = 8
OWN = 432
NT = (((1,), (1,)), ((), ()))
TN = (((0,), (0,)), ((), ()))


def sigmoid(v):
    return 1.0 / (1.0 + jnp.exp(-v))


def silu_slope(v):
    sig = sigmoid(v)
    return sig * (1.0 + v * (1.0 - sig))


def valid_rows(field, first, tile):
    row = lax.broadcasted_iota(jnp.int32, field.shape, 0) + first
    inside = jnp.logical_and(
        jnp.logical_or(row >= 0, tile > 0), jnp.logical_or(row < 8, tile < 15)
    )
    return jnp.where(inside, field, 0.0)


def spread(field, frame, even, odd):
    rows = field.shape[0]
    col = lax.broadcasted_iota(jnp.int32, field.shape, 1)
    for e in range(3):
        if e == 1:
            moved = field
        else:
            moved = pltpu.roll(field, 1 if e == 0 else WC - 1, 1)
            moved = jnp.where(col == (0 if e == 0 else WC - 1), 0.0, moved)
        even[e, frame, pl.ds(0, rows * WC), :] = moved.reshape(rows * WC, C).astype(BF)
        inner = moved[1 : rows - 1].reshape((rows - 2) * WC, C)
        odd[e, frame, pl.ds(0, (rows - 2) * WC), :] = inner.astype(BF)


def conv(even, odd, rows, weights, total, reverse):
    for a in (2, 1, 0):
        count = 3 + a
        first_in, first_out = (2 - a, 0) if reverse else (0, 2 - a)
        pieces = []
        for b in range(3):
            for e in range(3):
                bb, ee = (2 - b, 2 - e) if reverse else (b, e)
                source = odd if bb == 1 else even
                start = 16 if bb == 2 else 0
                piece = source[ee, pl.ds(first_in, count), pl.ds(start, rows * WC), :]
                pieces.append(piece.reshape(count * rows * WC, C))
        lhs = jnp.concatenate(pieces, axis=1)
        if reverse:
            taps = [weights[a, pl.ds(i * C, C), :] for i in range(9)]
            out = lax.dot_general(
                lhs, jnp.concatenate(taps, axis=1), NT, preferred_element_type=F32
            )
        else:
            out = jnp.dot(lhs, weights[a], preferred_element_type=F32)
        out = out.reshape(count, rows * WC, C)
        if a == 2:
            total[...] = out
        else:
            total[pl.ds(first_out, count)] += out


def turned(field):
    flat = field.reshape(80, C)
    flat = jnp.concatenate([flat, jnp.zeros((48, C), F32)], axis=0)
    return flat.T.astype(BF).reshape(4, 4, 16, 128)


def split(v):
    high = v.astype(BF)
    rest = v - high.astype(F32)
    mid = rest.astype(BF)
    low = (rest - mid.astype(F32)).astype(BF)
    return jnp.concatenate([high.astype(F32), mid.astype(F32), low.astype(F32)], axis=0).astype(BF)


def train_kernel(
    lat, cot, ker_one, ker_two, err_one, err_two, fac_one, fac_two,
    merged, table,
    raw, weights, chunk, lat_ext, cot_ext, even, odd, acc_one, acc_two, acc_three,
    select, order, turn, turn_in, slopes, patches, part, part_half, part_rest, part_in, part_pass, part_sum, errs, err_rows,
    err_proj, thin, proj, proj_in, left_in, lefts, right, right_in, right_tile, gram_in, right_all, whole_rows,
    local_sem, send_sem, recv_sem,
):
    tile = lax.axis_index("tile")
    rep = lax.axis_index("rep")
    tz, ty = tile // 4, tile % 4
    rx, core = rep // 2, rep % 2
    near = core * tz + (1 - core) * ty
    other = core * ty + (1 - core) * tz
    here = rx * 4 + near
    pair = {"rep": rx * 2 + 1 - core}
    group = [(dx, dg) for dx in range(4) for dg in range(4) if dx or dg]

    def place(dx, dg):
        return lax.rem(rx + dx, 4) * 4 + lax.rem(near + dg, 4)

    def member(dx, dg):
        z, y = lax.rem(tz + core * dg, 4), lax.rem(ty + (1 - core) * dg, 4)
        return {"rep": lax.rem(rx + dx, 4) * 2 + core, "tile": z * 4 + y}

    def across(d):
        z, y = lax.rem(tz + (1 - core) * d, 4), lax.rem(ty + core * d, 4)
        return {"tile": z * 4 + y}

    def along(axis, d):
        if axis == "z":
            return lax.rem(tz + d, 4) * 4 + ty
        return tz * 4 + lax.rem(ty + d, 4)

    up, down = lax.rem(tile + 15, 16), lax.rem(tile + 1, 16)

    region = pl.when(tile >= 0)
    totals = {}

    def remote(src, dst, phase, device, total=None):
        if phase not in totals:
            totals[phase] = dst if total is None else total
        pltpu.make_async_remote_copy(
            src_ref=src, dst_ref=dst, send_sem=send_sem.at[phase], recv_sem=recv_sem.at[phase],
            device_id=device, device_id_type=MESH,
        ).start()

    def whole(phase):
        ref = totals[phase]
        return pltpu.make_async_remote_copy(
            src_ref=ref, dst_ref=ref, send_sem=send_sem.at[phase], recv_sem=recv_sem.at[phase],
            device_id={"tile": up}, device_id_type=MESH,
        )

    def arrived(phase):
        whole(phase).wait_recv()

    def send_blocks(k):
        for f in range(FR):
            for d in (1, 3):
                to = {"tile": along("y" if k else "z", d)}
                remote(slopes.at[k, f, 0], slopes.at[k, f, d], 8 + k, to, slopes.at[k, :, pl.ds(1, 2)])

    def forward_blocks(k):
        arrived(8 + k)
        for f in range(FR):
            for d, half in ((1, pl.ds(0, 32)), (3, pl.ds(32, 32))):
                to = {"tile": along("y" if k else "z", d)}
                remote(slopes.at[k, f, d, half], slopes.at[k, f, 2, half], 20 + k, to, slopes.at[k, :, 2])

    low, high = pl.ds(0, 80), pl.ds(80, 64)

    def send_far(k, a):
        axis, mine = ("z", tz) if k else ("y", ty)
        chunk_of = part_half.at[k, a, lax.rem(mine + 2, 4)]
        remote(chunk_of.at[low], part_pass.at[k, a, low], 23 + k, {"tile": along(axis, 1)}, part_pass.at[k])
        remote(chunk_of.at[high], part_pass.at[k, a, high], 23 + k, {"tile": along(axis, 3)})

    def send_near(k, a):
        axis, mine = ("z", tz) if k else ("y", ty)
        after, before = part_half.at[k, a, lax.rem(mine + 1, 4)], part_half.at[k, a, lax.rem(mine + 3, 4)]
        remote(after.at[high], part_in.at[k, 0, a, high], 10 + k, {"tile": along(axis, 1)}, part_in.at[k])
        remote(before.at[low], part_in.at[k, 1, a, low], 10 + k, {"tile": along(axis, 3)})

    def pass_on(k):
        axis, mine = ("z", tz) if k else ("y", ty)
        arrived(23 + k)

        @region
        def _():
            for a in range(3):
                for rows, step in ((low, 1), (high, 3)):
                    own_part = part[k, a, lax.rem(mine + step, 4), rows, :]
                    part_sum[k, a, rows, :] = (own_part + part_pass[k, a, rows, :].astype(F32)).astype(BF)

        for a in range(3):
            for rows, step in ((low, 1), (high, 3)):
                to = {"tile": along(axis, step)}
                remote(part_sum.at[k, a, rows], part_in.at[k, step // 2, a, rows], 10 + k, to)

    def send_slopes(k):
        factor = split((fac_two if k else fac_one)[...])
        rows = slopes[k, :, 0].reshape(320, C)
        out = lax.dot_general(factor, rows, NT, preferred_element_type=F32)
        thin[k, 0] = out[0:8] + out[8:16] + out[16:24]
        axis = "y" if k else "z"
        for d in range(1, 4):
            to = {"tile": along(axis, d)}
            remote(thin.at[k, 0], thin.at[k, d], 6 + k, to, thin.at[k, pl.ds(1, 3)])
        send_blocks(k)

    def gradients(k):
        arrived(20 + k)
        mine = tz if k else ty
        for a in range(3):

            @region
            def _(a=a):
                count = 3 + a
                rhs = slopes[k, pl.ds(2 - a, count)].reshape(count * 256, C)
                out = jnp.dot(patches[k, :, pl.ds(0, count * 256)], rhs, preferred_element_type=F32)
                part[k, a] = out.reshape(4, 144, C)
                part[k, a, mine] += err_rows[k, a]
                out = part[k, a]
                half = out.astype(BF)
                part_half[k, a] = half
                part_rest[k, a] = (out - half.astype(F32)).astype(BF)

            send_far(k, a)
        for a in range(3):
            send_near(k, a)

    def project_errors():
        for k in range(2):
            mine = tz if k else ty
            for half in range(2):
                loads[4 + 2 * k + half].wait()

            @region
            def _(k=k, mine=mine):
                for half in range(2):
                    for tap in range(27):
                        rows = errs[k, half, pl.ds(tap, 16, stride=27), :]
                        err_rows[k, tap // 9, pl.ds((tap % 9) * 16, 16), pl.ds(half * 128, 128)] = rows
                out = err_rows[k].reshape(OWN, C)
                high = out.astype(BF)
                rest = (out - high.astype(F32)).astype(BF)
                factor = split((fac_two if k else fac_one)[...])
                out = lax.dot_general(factor, high, NT, preferred_element_type=F32)
                out += lax.dot_general(factor, rest, NT, preferred_element_type=F32)
                out = out[0:8] + out[8:16] + out[16:24]
                err_proj[k] = jnp.concatenate(
                    [
                        jnp.where(mine == j, out[:, a * 144 : a * 144 + 144], 0.0)
                        for a in range(3)
                        for j in range(4)
                    ],
                    axis=1,
                )

    loads = [
        pltpu.make_async_copy(ker_one, raw.at[0], local_sem.at[0]),
        pltpu.make_async_copy(ker_two, raw.at[1], local_sem.at[1]),
        pltpu.make_async_copy(lat, lat_ext.at[:, pl.ds(32, 64)], local_sem.at[2]),
        pltpu.make_async_copy(cot, cot_ext.at[:, pl.ds(16, 64)], local_sem.at[3]),
    ]
    for k, err in enumerate((err_one, err_two)):
        for half in range(2):
            lanes = pl.ds(half * 128, 128)
            loads.append(
                pltpu.make_async_copy(err.at[:, lanes], errs.at[k, half], local_sem.at[8 + 2 * k + half])
            )
    for load in loads:
        load.start()

    barrier = pltpu.get_barrier_semaphore()
    greeted = [{"tile": lax.rem(tile + d, 16)} for d in range(1, 16)]
    greeted += [pair] + [member(dx, dg) for dx, dg in group if dx]
    greeted += [{"rep": lax.rem(rx + d, 4) * 2 + 1 - core} for d in range(1, 4)]
    for device in greeted:
        pl.semaphore_signal(barrier, inc=1, device_id=device, device_id_type=MESH)
    held = lax.broadcasted_iota(jnp.int32, (256, 128), 0)
    want = lax.broadcasted_iota(jnp.int32, (256, 128), 1)
    same = (held // 128) == (want // 64)
    held, want = held % 128, want % 64
    for b in range(3):
        for e in range(3):
            hit = jnp.logical_and(held // 8 == want // 8 + b, held % 8 == want % 8 + (e - 1))
            hit = jnp.logical_and(same, hit)
            select[:, pl.ds((b * 3 + e) * 128, 128)] = jnp.where(hit, 1.0, 0.0).astype(BF)

    source = lax.broadcasted_iota(jnp.int32, (OWN, OWN), 0)
    target = lax.broadcasted_iota(jnp.int32, (OWN, OWN), 1)
    order[...] = jnp.where(target == (source % 16) * 27 + source // 16, 1.0, 0.0).astype(BF)

    pl.semaphore_wait(barrier, len(greeted))

    remote(lat.at[:, pl.ds(32, 32)], lat_ext.at[:, pl.ds(0, 32)], 0, {"tile": down})
    remote(lat.at[:, pl.ds(0, 32)], lat_ext.at[:, pl.ds(96, 32)], 1, {"tile": up})
    remote(cot.at[:, pl.ds(48, 16)], cot_ext.at[:, pl.ds(0, 16)], 2, {"tile": down})
    remote(cot.at[:, pl.ds(0, 16)], cot_ext.at[:, pl.ds(80, 16)], 3, {"tile": up})

    for k in range(2):
        loads[k].wait()

        def reorder(j, carry, k=k):
            rows = pl.ds(pl.multiple_of(j * OWN, OWN), OWN)
            for half in range(2):
                lanes = pl.ds(half * 128, 128)
                chunk[half] = raw[k, rows, lanes].astype(F32)
                for tap in range(27):
                    picked = chunk[half, pl.ds(tap, 16, stride=27), :].astype(BF)
                    at = pl.multiple_of((tap % 9) * C + j * 16, 16)
                    weights[k, tap // 9, pl.ds(at, 16), lanes] = picked
            return carry

        lax.fori_loop(0, 16, reorder, 0)

    loads[2].wait()
    loads[3].wait()
    arrived(0)
    arrived(1)

    def enter_one(f, carry):
        field = lat_ext[f].astype(F32).reshape(16, WC, C)[1:15]
        field = valid_rows(field, -3, tile)
        turn[0, f] = turned(field[2:12])
        spread(field, f, even, odd)
        return carry

    region(lambda: [enter_one(f, 0) for f in range(FR)] and None)
    own = [
        pltpu.make_async_copy(turn.at[0, :, tz], turn_in.at[0, 0], local_sem.at[6]),
        pltpu.make_async_copy(turn.at[1, :, :, ty], turn_in.at[1, 0], local_sem.at[7]),
    ]
    own[0].start()
    for d in range(1, 4):
        to = lax.rem(tz + d, 4)
        remote(turn.at[0, :, to], turn_in.at[0, d], 4, {"tile": along("z", d)}, turn_in.at[0, pl.ds(1, 3)])
    region(lambda: conv(even, odd, 12, weights.at[0], acc_one, False))

    totals[5] = turn_in.at[1, pl.ds(1, 3)]
    def enter_two(f, carry):
        pre = acc_one[f]
        hidden = (pre * sigmoid(pre)).astype(BF).astype(F32).reshape(12, WC, C)
        hidden = valid_rows(hidden, -2, tile)
        turn[1, f] = turned(hidden[1:11])
        spread(hidden, f, even, odd)
        return carry

    for group_of in ((0, 1), (2, 3, 4)):
        region(lambda: [enter_two(f, 0) for f in group_of] and None)
        for f in group_of:
            for d in range(1, 4):
                to = lax.rem(ty + d, 4)
                remote(turn.at[1, f, :, to], turn_in.at[1, d, f], 5, {"tile": along("y", d)})
    own[1].start()
    region(lambda: conv(even, odd, 10, weights.at[1], acc_two, False))

    arrived(2)
    arrived(3)

    def enter_three(f, carry):
        cots = cot_ext[f].astype(F32)[8:88]
        slope = (cots * silu_slope(acc_two[f])).astype(BF).astype(F32).reshape(10, WC, C)
        slope = valid_rows(slope, -1, tile)
        spread(slope, f, even, odd)
        slopes[1, f, 0] = slope[1:9].reshape(64, C).astype(BF)
        return carry

    region(lambda: [enter_three(f, 0) for f in range(FR)] and None)
    send_slopes(1)
    region(lambda: conv(even, odd, 8, weights.at[1], acc_three, True))

    def leave(f, carry):
        pre = acc_one[f, pl.ds(16, 64), :]
        slopes[0, f, 0] = (acc_three[f] * silu_slope(pre)).astype(BF)
        return carry

    region(lambda: [leave(f, 0) for f in range(FR)] and None)
    send_slopes(0)

    for k in range(2):
        if k == 1:
            project_errors()
        own[k].wait()
        arrived(4 + k)

        @region
        def _(k=k):
            for p in range(2):
                lhs = jnp.concatenate(
                    [turn_in[k, 2 * p + s].reshape(320, 128) for s in range(2)], axis=1
                )
                out = jnp.dot(lhs, select[...], preferred_element_type=F32).astype(BF)
                for f in range(FR):
                    for i in range(9):
                        for j in range(4):
                            block = out[f * 64 + j * 16 : f * 64 + j * 16 + 16, i * 128 : i * 128 + 128]
                            rows = pl.ds(j * 144 + i * 16, 16)
                            patches[k, rows, pl.ds(f * 256 + p * 128, 128)] = block

    for k in (1, 0):
        arrived(6 + k)

        @region
        def _(k=k):
            blocks = [thin[k, d] for d in range(4)]
            wide = jnp.concatenate(
                [blocks[d][:, f * 64 : f * 64 + 64] for f in range(FR) for d in range(4)], axis=1
            )
            shifts = [
                jnp.concatenate([wide[:, (2 - a) * 256 :], jnp.zeros((8, (2 - a) * 256), F32)], axis=1)
                if a < 2
                else wide
                for a in range(3)
            ]
            wide = split(jnp.concatenate(shifts, axis=0))
            out = lax.dot_general(wide, patches[k], NT, preferred_element_type=F32)
            out = out[0:24] + out[24:48] + out[48:72]
            out = jnp.concatenate([out[0:8], out[8:16], out[16:24]], axis=1)
            sample = out + err_proj[k]
            sample = jnp.concatenate([sample, jnp.zeros((8, 2048 - 1728), F32)], axis=1)
            for q in range(16):
                proj[k, q] = sample[:, q * 128 : q * 128 + 128]

    remote(proj.at[1 - core], proj_in, 12, pair)
    arrived(12)
    for q in range(16):
        proj_in[q] = proj_in[q] + proj[core, q]
    for dx, dg in group:
        to = place(dx, dg)
        remote(proj_in.at[to], left_in.at[here], 13, member(dx, dg), left_in.at[pl.ds(0, 15)])
    left_in[here] = proj_in[here]
    forward_blocks(1)
    forward_blocks(0)

    arrived(13)
    piece = left_in[0]
    for q in range(1, 16):
        piece = piece + left_in[q]
    lefts[core, here] = piece * 0.125
    for dx, dg in group:
        block = lefts.at[core, here]
        remote(block, block, 14, member(dx, dg), lefts.at[0, pl.ds(0, 15)])
    gradients(1)
    gradients(0)
    arrived(14)
    remote(lefts.at[core], lefts.at[core], 15, pair)
    arrived(15)

    for k in range(2):

        @region
        def _(k=k):
            rows_all = jnp.concatenate([lefts[k, q] for q in range(16)], axis=1)[:, 0:1728]
            pieces = split(rows_all)
            out = jnp.dot(pieces, part_half[k].reshape(1728, C), preferred_element_type=F32)
            out += jnp.dot(pieces, part_rest[k].reshape(1728, C), preferred_element_type=F32)
            right[k] = out[0:8] + out[8:16] + out[16:24]

    for d in range(1, 4):
        for on in (core, 1 - core):
            to = {"rep": lax.rem(rx + d, 4) * 2 + on}
            remote(right.at[on], right_in.at[rep], 17, to, right_in.at[pl.ds(0, 7)])
    remote(right.at[1 - core], right_in.at[rep], 17, pair)
    right_in[rep] = right[core]

    for k in range(2):
        mine = tz if k else ty

        @region
        def _(k=k, mine=mine):
            rows_all = jnp.concatenate([lefts[k, q] for q in range(16)], axis=1)[:, 0:1728]
            gram = lax.dot_general(rows_all, rows_all, NT, precision=HIGH, preferred_element_type=F32)
            gram = jnp.concatenate([gram, jnp.zeros((8, 120), F32)], axis=1)

            @pl.when(core == k)
            def _():
                gram_in[other] = gram

            rows = []
            for a in range(3):
                found = jnp.zeros((8, 144), F32)
                for j in range(4):
                    at = a * 576 + j * 144
                    found = jnp.where(mine == j, rows_all[:, at : at + 144], found)
                rows.append(found)
            out = split(jnp.concatenate(rows, axis=1))
            out = jnp.dot(out, order[...], preferred_element_type=F32)
            table[k, :, pl.ds(0, OWN)] = out[0:8] + out[8:16] + out[16:24]

    for d in range(1, 4):
        remote(gram_in.at[other], gram_in.at[other], 22, across(d), gram_in.at[pl.ds(0, 3)])

    pass_on(1)
    pass_on(0)
    arrived(17)
    total = right_in[0]
    for q in range(1, 8):
        total = total + right_in[q]
    right_tile[tile] = total
    for d in range(1, 16):
        block = right_tile.at[tile]
        remote(block, block, 18, {"tile": lax.rem(tile + d, 16)}, right_tile.at[pl.ds(0, 15)])
    arrived(22)
    right_all[core, :, pl.ds(256, 128)] = gram_in[0] + gram_in[1] + gram_in[2] + gram_in[3]
    arrived(18)
    total = right_tile[0]
    for q in range(1, 16):
        total = total + right_tile[q]
    right_all[core, :, pl.ds(0, 256)] = total
    remote(right_all.at[core], right_all.at[core], 19, pair)
    stores = []
    for k in (1, 0):
        mine = tz if k else ty
        arrived(10 + k)

        @region
        def _(k=k, mine=mine):
            for tap in range(27):
                a, rows = tap // 9, pl.ds((tap % 9) * 16, 16)
                grad = part[k, a, mine, rows, :]
                for d in range(2):
                    grad = grad + part_in[k, d, a, rows, :].astype(F32)
                for half in range(2):
                    chunk[half, pl.ds(tap, 16, stride=27), :] = grad[:, half * 128 : half * 128 + 128]
            for half in range(2):
                whole_rows[k, :, pl.ds(half * 128, 128)] = chunk[half]

        stores.append(pltpu.make_async_copy(whole_rows.at[k], merged.at[k], local_sem.at[k]))
        stores[-1].start()
    arrived(19)
    table[:, :, pl.ds(512, 384)] = right_all[...]

    for store in stores:
        store.wait()
    for phase in totals:
        whole(phase).wait_send()


def finish_kernel(
    merged, table_in, approx_one, approx_two, fresh_one, fresh_two, new_one, new_two,
    table_ref, rows, approx_ref, fresh_ref, factor_ref, sem,
):
    load = pltpu.make_async_copy(table_in, table_ref, sem.at[0])
    load.start()
    loads = [pltpu.make_async_copy(merged.at[k], rows.at[k], sem.at[1 + k]) for k in range(2)]
    for copy in loads:
        copy.start()
    load.wait()
    table = table_ref[...]
    row = lax.broadcasted_iota(jnp.int32, table.shape, 1)
    for j in range(RANK):
        column = 512 + C + j
        scale = lax.rsqrt(table[:, j : j + 1, column : column + 1])
        scaled = table[:, j : j + 1, :] * scale
        coefs = table[:, :, column : column + 1] * scale
        table = jnp.where(row == j, scaled, jnp.where(row > j, table - coefs * scaled, table))
    stores = []
    for k, (approx_out, fresh_out, new_out) in enumerate(
        ((approx_one, fresh_one, new_one), (approx_two, fresh_two, new_two))
    ):
        basis = table[k, :, 0:OWN]
        factor = table[k, :, 512 : 512 + C] * 0.125
        b, f = split(basis).astype(F32), split(factor)
        b = jnp.concatenate([b[0:8], b[0:8], b[0:8], b[8:16], b[8:16], b[16:24]], axis=0)
        f = jnp.concatenate([f[0:24].astype(F32), f[0:16].astype(F32), f[0:8].astype(F32)], axis=0)
        approx = lax.dot_general(b.astype(BF), f.astype(BF), TN, preferred_element_type=F32)
        factor_ref[k] = factor
        stores.append(pltpu.make_async_copy(factor_ref.at[k], new_out, sem.at[7 + k]))
        stores[-1].start()
        approx_ref[k] = approx
        stores.append(pltpu.make_async_copy(approx_ref.at[k], approx_out, sem.at[3 + k]))
        stores[-1].start()
        loads[k].wait()
        fresh_ref[k] = rows[k] - approx
        stores.append(pltpu.make_async_copy(fresh_ref.at[k], fresh_out, sem.at[5 + k]))
        stores[-1].start()
    for copy in stores:
        copy.wait()


def on_device(
    latents, cotangent, kernel_one, kernel_two, error_one, error_two, factor_one, factor_two
):
    vmem = pl.BlockSpec(memory_space=pltpu.VMEM)
    hbm = pl.BlockSpec(memory_space=pl.ANY)
    sds = jax.ShapeDtypeStruct
    merged, table = pl.pallas_call(
        train_kernel,
        out_shape=(sds((2, OWN, C), F32), sds((2, RANK, 896), F32)),
        in_specs=[hbm] * 6 + [vmem] * 2,
        out_specs=(hbm, vmem),
        scratch_shapes=[
            pltpu.VMEM((2, 6912, C), BF),
            pltpu.VMEM((2, 3, 9 * C, C), BF),
            pltpu.VMEM((2, OWN, 128), F32),
            pltpu.VMEM((FR, 128, C), BF),
            pltpu.VMEM((FR, 96, C), BF),
            pltpu.VMEM((3, FR, 112, C), BF),
            pltpu.VMEM((3, FR, 96, C), BF),
            pltpu.VMEM((FR, 96, C), F32),
            pltpu.VMEM((FR, 80, C), F32),
            pltpu.VMEM((FR, 64, C), F32),
            pltpu.VMEM((256, 9 * 128), BF),
            pltpu.VMEM((OWN, OWN), BF),
            pltpu.VMEM((2, FR, 4, 4, 16, 128), BF),
            pltpu.VMEM((2, 4, FR, 4, 16, 128), BF),
            pltpu.VMEM((2, FR, 4, 64, C), BF),
            pltpu.VMEM((2, 9 * 64, FR * 256), BF),
            pltpu.VMEM((2, 3, 4, 144, C), F32),
            pltpu.VMEM((2, 3, 4, 144, C), BF),
            pltpu.VMEM((2, 3, 4, 144, C), BF),
            pltpu.VMEM((2, 2, 3, 144, C), BF),
            pltpu.VMEM((2, 3, 144, C), BF),
            pltpu.VMEM((2, 3, 144, C), BF),
            pltpu.VMEM((2, 2, OWN, 128), F32),
            pltpu.VMEM((2, 3, 144, C), F32),
            pltpu.VMEM((2, 8, 1728), F32),
            pltpu.VMEM((2, 4, 8, 320), F32),
            pltpu.VMEM((2, 16, 8, 128), F32),
            pltpu.VMEM((16, 8, 128), F32),
            pltpu.VMEM((16, 8, 128), F32),
            pltpu.VMEM((2, 16, 8, 128), F32),
            pltpu.VMEM((2, 8, C), F32),
            pltpu.VMEM((8, 8, C), F32),
            pltpu.VMEM((16, 8, C), F32),
            pltpu.VMEM((4, 8, 128), F32),
            pltpu.VMEM((2, 8, 384), F32),
            pltpu.VMEM((2, OWN, C), F32),
            pltpu.SemaphoreType.DMA((12,)),
            pltpu.SemaphoreType.DMA((25,)),
            pltpu.SemaphoreType.DMA((25,)),
        ],
        compiler_params=pltpu.CompilerParams(
            collective_id=0, has_side_effects=True, vmem_limit_bytes=60 * 2**20
        ),
        name="train",
    )(
        latents.reshape(FR, 64, C),
        cotangent.reshape(FR, 64, C),
        kernel_one,
        kernel_two,
        error_one[0],
        error_two[0],
        factor_one.T,
        factor_two.T,
    )
    block, small = sds((OWN, C), F32), sds((RANK, C), F32)
    approx_one, approx_two, fresh_one, fresh_two, new_one, new_two = pl.pallas_call(
        finish_kernel,
        out_shape=(block, block, block, block, small, small),
        in_specs=[hbm] * 2,
        out_specs=(hbm,) * 6,
        scratch_shapes=[
            pltpu.VMEM((2, RANK, 896), F32),
            pltpu.VMEM((2, OWN, C), F32),
            pltpu.VMEM((2, OWN, C), F32),
            pltpu.VMEM((2, OWN, C), F32),
            pltpu.VMEM((2, RANK, C), F32),
            pltpu.SemaphoreType.DMA((9,)),
        ],
        compiler_params=pltpu.CompilerParams(vmem_limit_bytes=60 * 2**20),
        name="finish",
    )(merged, table)
    return approx_one, approx_two, fresh_one[None], fresh_two[None], new_one.T, new_two.T


def solution(mesh):
    placed = (
        P("rep", None, "tile", None, None),
        P("rep", None, "tile", None, None),
        P(),
        P(),
        P("rep", "tile", None),
        P("rep", "tile", None),
        P(),
        P(),
    )
    return jax.shard_map(
        on_device,
        mesh=mesh,
        in_specs=placed,
        out_specs=(
            P("tile", None),
            P("tile", None),
            P("rep", "tile", None),
            P("rep", "tile", None),
            P(),
            P(),
        ),
        check_vma=False,
    )
```

```python
import functools

import jax
import jax.numpy as jnp
from jax import lax
from jax.experimental import pallas as pl
from jax.experimental.pallas import tpu as pltpu
from jax.sharding import PartitionSpec as P

MESH = pl.DeviceIdType.MESH
HIGH = lax.Precision.HIGHEST
BF = jnp.bfloat16
F32 = jnp.float32
FR = 5
WC = 8
C = 256
RANK = 8
OWN = 432
NT = (((1,), (1,)), ((), ()))
TN = (((0,), (0,)), ((), ()))


def sigmoid(v):
    return 1.0 / (1.0 + jnp.exp(-v))


def silu_slope(v):
    sig = sigmoid(v)
    return sig * (1.0 + v * (1.0 - sig))


def valid_rows(field, first, tile):
    row = lax.broadcasted_iota(jnp.int32, field.shape, 0) + first
    inside = jnp.logical_and(
        jnp.logical_or(row >= 0, tile > 0), jnp.logical_or(row < 8, tile < 15)
    )
    return jnp.where(inside, field, 0.0)


def spread(field, frame, even, odd):
    rows = field.shape[0]
    col = lax.broadcasted_iota(jnp.int32, field.shape, 1)
    for e in range(3):
        if e == 1:
            moved = field
        else:
            moved = pltpu.roll(field, 1 if e == 0 else WC - 1, 1)
            moved = jnp.where(col == (0 if e == 0 else WC - 1), 0.0, moved)
        even[e, frame, pl.ds(0, rows * WC), :] = moved.reshape(rows * WC, C).astype(BF)
        inner = moved[1 : rows - 1].reshape((rows - 2) * WC, C)
        odd[e, frame, pl.ds(0, (rows - 2) * WC), :] = inner.astype(BF)


def conv(even, odd, rows, weights, total, reverse):
    for a in (2, 1, 0):
        count = 3 + a
        first_in, first_out = (2 - a, 0) if reverse else (0, 2 - a)
        pieces = []
        for b in range(3):
            for e in range(3):
                bb, ee = (2 - b, 2 - e) if reverse else (b, e)
                source = odd if bb == 1 else even
                start = 16 if bb == 2 else 0
                piece = source[ee, pl.ds(first_in, count), pl.ds(start, rows * WC), :]
                pieces.append(piece.reshape(count * rows * WC, C))
        lhs = jnp.concatenate(pieces, axis=1)
        if reverse:
            taps = [weights[a, pl.ds(i * C, C), :] for i in range(9)]
            out = lax.dot_general(
                lhs, jnp.concatenate(taps, axis=1), NT, preferred_element_type=F32
            )
        else:
            out = jnp.dot(lhs, weights[a], preferred_element_type=F32)
        out = out.reshape(count, rows * WC, C)
        if a == 2:
            total[...] = out
        else:
            total[pl.ds(first_out, count)] += out


def turned(field):
    flat = field.reshape(80, C)
    flat = jnp.concatenate([flat, jnp.zeros((48, C), F32)], axis=0)
    return flat.T.astype(BF).reshape(4, 4, 16, 128)


def split(v):
    high = v.astype(BF)
    rest = v - high.astype(F32)
    mid = rest.astype(BF)
    low = (rest - mid.astype(F32)).astype(BF)
    return jnp.concatenate([high.astype(F32), mid.astype(F32), low.astype(F32)], axis=0).astype(BF)


def train_kernel(
    lat, cot, ker_one, ker_two, err_one, err_two, fac_one, fac_two,
    merged, table_out,
    raw, weights, chunk, lat_ext, cot_ext, even, odd, acc_one, acc_two, acc_three,
    select, order, turn, turn_in, slopes, patches, part, part_half, part_rest, part_in, part_pass, part_sum, errs, err_rows,
    err_proj, thin, proj, proj_in, left_in, lefts, right, right_in, right_tile, gram_in, gram_all, right_all, whole_rows, factors, table,
    local_sem, send_sem, recv_sem,
):
    tile = lax.axis_index("tile")
    rep = lax.axis_index("rep")
    tz, ty = tile // 4, tile % 4
    rx, core = rep // 2, rep % 2
    near = core * tz + (1 - core) * ty
    other = core * ty + (1 - core) * tz
    here = rx * 4 + near
    pair = {"rep": rx * 2 + 1 - core}
    group = [(dx, dg) for dx in range(4) for dg in range(4) if dx or dg]

    def place(dx, dg):
        return lax.rem(rx + dx, 4) * 4 + lax.rem(near + dg, 4)

    def member(dx, dg):
        z, y = lax.rem(tz + core * dg, 4), lax.rem(ty + (1 - core) * dg, 4)
        return {"rep": lax.rem(rx + dx, 4) * 2 + core, "tile": z * 4 + y}

    def across(d):
        z, y = lax.rem(tz + (1 - core) * d, 4), lax.rem(ty + core * d, 4)
        return {"tile": z * 4 + y}

    def along(axis, d):
        if axis == "z":
            return lax.rem(tz + d, 4) * 4 + ty
        return tz * 4 + lax.rem(ty + d, 4)

    up, down = lax.rem(tile + 15, 16), lax.rem(tile + 1, 16)

    region = pl.when(tile >= 0)
    totals = {}

    def remote(src, dst, phase, device, total=None):
        if phase not in totals:
            totals[phase] = dst if total is None else total
        pltpu.make_async_remote_copy(
            src_ref=src, dst_ref=dst, send_sem=send_sem.at[phase], recv_sem=recv_sem.at[phase],
            device_id=device, device_id_type=MESH,
        ).start()

    def whole(phase):
        ref = totals[phase]
        return pltpu.make_async_remote_copy(
            src_ref=ref, dst_ref=ref, send_sem=send_sem.at[phase], recv_sem=recv_sem.at[phase],
            device_id={"tile": up}, device_id_type=MESH,
        )

    def arrived(phase):
        whole(phase).wait_recv()

    def send_blocks(k):
        for f in range(FR):
            for d in (1, 3):
                to = {"tile": along("y" if k else "z", d)}
                remote(slopes.at[k, f, 0], slopes.at[k, f, d], 8 + k, to, slopes.at[k, :, pl.ds(1, 2)])

    def forward_blocks(k):
        arrived(8 + k)
        for f in range(FR):
            for d, half in ((1, pl.ds(0, 32)), (3, pl.ds(32, 32))):
                to = {"tile": along("y" if k else "z", d)}
                remote(slopes.at[k, f, d, half], slopes.at[k, f, 2, half], 20 + k, to, slopes.at[k, :, 2])

    low, high = pl.ds(0, 80), pl.ds(80, 64)

    def send_far(k, a):
        axis, mine = ("z", tz) if k else ("y", ty)
        chunk_of = part_half.at[k, a, lax.rem(mine + 2, 4)]
        remote(chunk_of.at[low], part_pass.at[k, a, low], 23 + k, {"tile": along(axis, 1)}, part_pass.at[k])
        remote(chunk_of.at[high], part_pass.at[k, a, high], 23 + k, {"tile": along(axis, 3)})

    def send_near(k, a):
        axis, mine = ("z", tz) if k else ("y", ty)
        after, before = part_half.at[k, a, lax.rem(mine + 1, 4)], part_half.at[k, a, lax.rem(mine + 3, 4)]
        remote(after.at[high], part_in.at[k, 0, a, high], 10 + k, {"tile": along(axis, 1)}, part_in.at[k])
        remote(before.at[low], part_in.at[k, 1, a, low], 10 + k, {"tile": along(axis, 3)})

    def pass_on(k):
        axis, mine = ("z", tz) if k else ("y", ty)
        arrived(23 + k)

        @region
        def _():
            for a in range(3):
                for rows, step in ((low, 1), (high, 3)):
                    own_part = part[k, a, lax.rem(mine + step, 4), rows, :]
                    part_sum[k, a, rows, :] = (own_part + part_pass[k, a, rows, :].astype(F32)).astype(BF)

        for a in range(3):
            for rows, step in ((low, 1), (high, 3)):
                to = {"tile": along(axis, step)}
                remote(part_sum.at[k, a, rows], part_in.at[k, step // 2, a, rows], 10 + k, to)

    def send_slopes(k):
        factor = split(factors[k])
        rows = slopes[k, :, 0].reshape(320, C)
        out = lax.dot_general(factor, rows, NT, preferred_element_type=F32)
        thin[k, 0] = out[0:8] + out[8:16] + out[16:24]
        axis = "y" if k else "z"
        for d in range(1, 4):
            to = {"tile": along(axis, d)}
            remote(thin.at[k, 0], thin.at[k, d], 6 + k, to, thin.at[k, pl.ds(1, 3)])
        send_blocks(k)

    def gradients(k):
        arrived(20 + k)
        mine = tz if k else ty
        for a in range(3):

            @region
            def _(a=a):
                count = 3 + a
                rhs = slopes[k, pl.ds(2 - a, count)].reshape(count * 256, C)
                out = jnp.dot(patches[k, :, pl.ds(0, count * 256)], rhs, preferred_element_type=F32)
                part[k, a] = out.reshape(4, 144, C)
                part[k, a, mine] += err_rows[k, a]
                out = part[k, a]
                half = out.astype(BF)
                part_half[k, a] = half
                part_rest[k, a] = (out - half.astype(F32)).astype(BF)

            send_far(k, a)
        for a in range(3):
            send_near(k, a)

    def project_errors():
        for k in range(2):
            mine = tz if k else ty
            for half in range(2):
                loads[6 + 2 * k + half].wait()

            @region
            def _(k=k, mine=mine):
                for half in range(2):
                    for tap in range(27):
                        rows = errs[k, half, pl.ds(tap, 16, stride=27), :]
                        err_rows[k, tap // 9, pl.ds((tap % 9) * 16, 16), pl.ds(half * 128, 128)] = rows
                out = err_rows[k].reshape(OWN, C)
                high = out.astype(BF)
                rest = (out - high.astype(F32)).astype(BF)
                factor = split(factors[k])
                out = lax.dot_general(factor, high, NT, preferred_element_type=F32)
                out += lax.dot_general(factor, rest, NT, preferred_element_type=F32)
                out = out[0:8] + out[8:16] + out[16:24]
                err_proj[k] = jnp.concatenate(
                    [
                        jnp.where(mine == j, out[:, a * 144 : a * 144 + 144], 0.0)
                        for a in range(3)
                        for j in range(4)
                    ],
                    axis=1,
                )

    loads = [
        pltpu.make_async_copy(ker_one, raw.at[0], local_sem.at[0]),
        pltpu.make_async_copy(ker_two, raw.at[1], local_sem.at[1]),
        pltpu.make_async_copy(lat, lat_ext.at[:, pl.ds(32, 64)], local_sem.at[2]),
        pltpu.make_async_copy(cot, cot_ext.at[:, pl.ds(16, 64)], local_sem.at[3]),
    ]
    for k, fac in enumerate((fac_one, fac_two)):
        loads.append(pltpu.make_async_copy(fac, factors.at[k], local_sem.at[4 + k]))
    for k, err in enumerate((err_one, err_two)):
        for half in range(2):
            lanes = pl.ds(half * 128, 128)
            loads.append(
                pltpu.make_async_copy(err.at[:, lanes], errs.at[k, half], local_sem.at[8 + 2 * k + half])
            )
    for load in loads:
        load.start()

    barrier = pltpu.get_barrier_semaphore()
    greeted = [{"tile": lax.rem(tile + d, 16)} for d in range(1, 16)]
    greeted += [pair] + [member(dx, dg) for dx, dg in group if dx]
    greeted += [{"rep": lax.rem(rx + d, 4) * 2 + 1 - core} for d in range(1, 4)]
    for device in greeted:
        pl.semaphore_signal(barrier, inc=1, device_id=device, device_id_type=MESH)
    held = lax.broadcasted_iota(jnp.int32, (256, 128), 0)
    want = lax.broadcasted_iota(jnp.int32, (256, 128), 1)
    same = (held // 128) == (want // 64)
    held, want = held % 128, want % 64
    for b in range(3):
        for e in range(3):
            hit = jnp.logical_and(held // 8 == want // 8 + b, held % 8 == want % 8 + (e - 1))
            hit = jnp.logical_and(same, hit)
            select[:, pl.ds((b * 3 + e) * 128, 128)] = jnp.where(hit, 1.0, 0.0).astype(BF)

    source = lax.broadcasted_iota(jnp.int32, (OWN, OWN), 0)
    target = lax.broadcasted_iota(jnp.int32, (OWN, OWN), 1)
    order[...] = jnp.where(target == (source % 16) * 27 + source // 16, 1.0, 0.0).astype(BF)

    pl.semaphore_wait(barrier, len(greeted))

    remote(lat.at[:, pl.ds(32, 32)], lat_ext.at[:, pl.ds(0, 32)], 0, {"tile": down})
    remote(lat.at[:, pl.ds(0, 32)], lat_ext.at[:, pl.ds(96, 32)], 1, {"tile": up})
    remote(cot.at[:, pl.ds(48, 16)], cot_ext.at[:, pl.ds(0, 16)], 2, {"tile": down})
    remote(cot.at[:, pl.ds(0, 16)], cot_ext.at[:, pl.ds(80, 16)], 3, {"tile": up})

    for k in range(2):
        loads[k].wait()

        def reorder(j, carry, k=k):
            rows = pl.ds(pl.multiple_of(j * OWN, OWN), OWN)
            for half in range(2):
                lanes = pl.ds(half * 128, 128)
                chunk[half] = raw[k, rows, lanes].astype(F32)
                for tap in range(27):
                    picked = chunk[half, pl.ds(tap, 16, stride=27), :].astype(BF)
                    at = pl.multiple_of((tap % 9) * C + j * 16, 16)
                    weights[k, tap // 9, pl.ds(at, 16), lanes] = picked
            return carry

        lax.fori_loop(0, 16, reorder, 0)

    loads[2].wait()
    loads[3].wait()
    arrived(0)
    arrived(1)

    def enter_one(f, carry):
        field = lat_ext[f].astype(F32).reshape(16, WC, C)[1:15]
        field = valid_rows(field, -3, tile)
        turn[0, f] = turned(field[2:12])
        spread(field, f, even, odd)
        return carry

    region(lambda: [enter_one(f, 0) for f in range(FR)] and None)
    own = [
        pltpu.make_async_copy(turn.at[0, :, tz], turn_in.at[0, 0], local_sem.at[6]),
        pltpu.make_async_copy(turn.at[1, :, :, ty], turn_in.at[1, 0], local_sem.at[7]),
    ]
    own[0].start()
    for d in range(1, 4):
        to = lax.rem(tz + d, 4)
        remote(turn.at[0, :, to], turn_in.at[0, d], 4, {"tile": along("z", d)}, turn_in.at[0, pl.ds(1, 3)])
    region(lambda: conv(even, odd, 12, weights.at[0], acc_one, False))

    totals[5] = turn_in.at[1, pl.ds(1, 3)]
    def enter_two(f, carry):
        pre = acc_one[f]
        hidden = (pre * sigmoid(pre)).astype(BF).astype(F32).reshape(12, WC, C)
        hidden = valid_rows(hidden, -2, tile)
        turn[1, f] = turned(hidden[1:11])
        spread(hidden, f, even, odd)
        return carry

    for group_of in ((0, 1), (2, 3, 4)):
        region(lambda: [enter_two(f, 0) for f in group_of] and None)
        for f in group_of:
            for d in range(1, 4):
                to = lax.rem(ty + d, 4)
                remote(turn.at[1, f, :, to], turn_in.at[1, d, f], 5, {"tile": along("y", d)})
    own[1].start()
    region(lambda: conv(even, odd, 10, weights.at[1], acc_two, False))

    arrived(2)
    arrived(3)
    loads[4].wait()
    loads[5].wait()

    def enter_three(f, carry):
        cots = cot_ext[f].astype(F32)[8:88]
        slope = (cots * silu_slope(acc_two[f])).astype(BF).astype(F32).reshape(10, WC, C)
        slope = valid_rows(slope, -1, tile)
        spread(slope, f, even, odd)
        slopes[1, f, 0] = slope[1:9].reshape(64, C).astype(BF)
        return carry

    region(lambda: [enter_three(f, 0) for f in range(FR)] and None)
    send_slopes(1)
    region(lambda: conv(even, odd, 8, weights.at[1], acc_three, True))

    def leave(f, carry):
        pre = acc_one[f, pl.ds(16, 64), :]
        slopes[0, f, 0] = (acc_three[f] * silu_slope(pre)).astype(BF)
        return carry

    region(lambda: [leave(f, 0) for f in range(FR)] and None)
    send_slopes(0)

    for k in range(2):
        if k == 1:
            project_errors()
        own[k].wait()
        arrived(4 + k)

        @region
        def _(k=k):
            for p in range(2):
                lhs = jnp.concatenate(
                    [turn_in[k, 2 * p + s].reshape(320, 128) for s in range(2)], axis=1
                )
                out = jnp.dot(lhs, select[...], preferred_element_type=F32).astype(BF)
                for f in range(FR):
                    for i in range(9):
                        for j in range(4):
                            block = out[f * 64 + j * 16 : f * 64 + j * 16 + 16, i * 128 : i * 128 + 128]
                            rows = pl.ds(j * 144 + i * 16, 16)
                            patches[k, rows, pl.ds(f * 256 + p * 128, 128)] = block

    for k in (1, 0):
        arrived(6 + k)

        @region
        def _(k=k):
            blocks = [thin[k, d] for d in range(4)]
            wide = jnp.concatenate(
                [blocks[d][:, f * 64 : f * 64 + 64] for f in range(FR) for d in range(4)], axis=1
            )
            shifts = [
                jnp.concatenate([wide[:, (2 - a) * 256 :], jnp.zeros((8, (2 - a) * 256), F32)], axis=1)
                if a < 2
                else wide
                for a in range(3)
            ]
            wide = split(jnp.concatenate(shifts, axis=0))
            out = lax.dot_general(wide, patches[k], NT, preferred_element_type=F32)
            out = out[0:24] + out[24:48] + out[48:72]
            out = jnp.concatenate([out[0:8], out[8:16], out[16:24]], axis=1)
            sample = out + err_proj[k]
            sample = jnp.concatenate([sample, jnp.zeros((8, 2048 - 1728), F32)], axis=1)
            for q in range(16):
                proj[k, q] = sample[:, q * 128 : q * 128 + 128]

    remote(proj.at[1 - core], proj_in, 12, pair)
    arrived(12)
    for q in range(16):
        proj_in[q] = proj_in[q] + proj[core, q]
    for dx, dg in group:
        to = place(dx, dg)
        remote(proj_in.at[to], left_in.at[here], 13, member(dx, dg), left_in.at[pl.ds(0, 15)])
    left_in[here] = proj_in[here]
    forward_blocks(1)
    forward_blocks(0)

    arrived(13)
    piece = left_in[0]
    for q in range(1, 16):
        piece = piece + left_in[q]
    lefts[core, here] = piece * 0.125
    for dx, dg in group:
        block = lefts.at[core, here]
        remote(block, block, 14, member(dx, dg), lefts.at[0, pl.ds(0, 15)])
    gradients(1)
    gradients(0)
    arrived(14)
    remote(lefts.at[core], lefts.at[core], 15, pair)
    arrived(15)

    for k in range(2):

        @region
        def _(k=k):
            rows_all = jnp.concatenate([lefts[k, q] for q in range(16)], axis=1)[:, 0:1728]
            pieces = split(rows_all)
            out = jnp.dot(pieces, part_half[k].reshape(1728, C), preferred_element_type=F32)
            out += jnp.dot(pieces, part_rest[k].reshape(1728, C), preferred_element_type=F32)
            right[k] = out[0:8] + out[8:16] + out[16:24]

    for d in range(1, 4):
        for on in (core, 1 - core):
            to = {"rep": lax.rem(rx + d, 4) * 2 + on}
            remote(right.at[on], right_in.at[rep], 17, to, right_in.at[pl.ds(0, 7)])
    remote(right.at[1 - core], right_in.at[rep], 17, pair)
    right_in[rep] = right[core]

    for k in range(2):
        mine = tz if k else ty

        @region
        def _(k=k, mine=mine):
            rows_all = jnp.concatenate([lefts[k, q] for q in range(16)], axis=1)[:, 0:1728]
            gram = lax.dot_general(rows_all, rows_all, NT, precision=HIGH, preferred_element_type=F32)
            gram = jnp.concatenate([gram, jnp.zeros((8, 120), F32)], axis=1)

            @pl.when(core == k)
            def _():
                gram_in[other] = gram

            rows = []
            for a in range(3):
                found = jnp.zeros((8, 144), F32)
                for j in range(4):
                    at = a * 576 + j * 144
                    found = jnp.where(mine == j, rows_all[:, at : at + 144], found)
                rows.append(found)
            out = split(jnp.concatenate(rows, axis=1))
            out = jnp.dot(out, order[...], preferred_element_type=F32)
            out = out[0:8] + out[8:16] + out[16:24]
            table[k, :, pl.ds(0, 512)] = jnp.concatenate([out, jnp.zeros((8, 80), F32)], axis=1)

    for d in range(1, 4):
        remote(gram_in.at[other], gram_in.at[other], 22, across(d), gram_in.at[pl.ds(0, 3)])

    pass_on(1)
    pass_on(0)
    arrived(17)
    total = right_in[0]
    for q in range(1, 8):
        total = total + right_in[q]
    right_tile[tile] = total
    for d in range(1, 16):
        block = right_tile.at[tile]
        remote(block, block, 18, {"tile": lax.rem(tile + d, 16)}, right_tile.at[pl.ds(0, 15)])
    arrived(22)
    gram_all[core] = gram_in[0] + gram_in[1] + gram_in[2] + gram_in[3]
    remote(gram_all.at[core], gram_all.at[core], 16, pair)
    arrived(16)

    @region
    def _():
        row = lax.broadcasted_iota(jnp.int32, (2, RANK, 768), 1)
        lane = lax.broadcasted_iota(jnp.int32, (2, RANK, 128), 2)
        eye = jnp.where(lane == row[:, :, 0:128], 1.0, 0.0)
        rows = jnp.concatenate([table[:, :, 0:512], gram_all[...], eye], axis=2)
        for j in range(RANK):
            scale = lax.rsqrt(rows[:, j : j + 1, 512 + j : 513 + j])
            scaled = rows[:, j : j + 1, :] * scale
            coefs = rows[:, :, 512 + j : 513 + j] * scale
            rows = jnp.where(row == j, scaled, jnp.where(row > j, rows - coefs * scaled, rows))
        table[:, :, pl.ds(0, 512)] = rows[:, :, 0:512]
        table[:, :, pl.ds(768, 128)] = rows[:, :, 640:768]

    arrived(18)
    total = right_tile[0]
    for q in range(1, 16):
        total = total + right_tile[q]
    right_all[core] = total
    remote(right_all.at[core], right_all.at[core], 19, pair)
    stores = []
    for k in (1, 0):
        mine = tz if k else ty
        arrived(10 + k)

        @region
        def _(k=k, mine=mine):
            for tap in range(27):
                a, rows = tap // 9, pl.ds((tap % 9) * 16, 16)
                grad = part[k, a, mine, rows, :]
                for d in range(2):
                    grad = grad + part_in[k, d, a, rows, :].astype(F32)
                for half in range(2):
                    chunk[half, pl.ds(tap, 16, stride=27), :] = grad[:, half * 128 : half * 128 + 128]
            for half in range(2):
                whole_rows[k, :, pl.ds(half * 128, 128)] = chunk[half]

        stores.append(pltpu.make_async_copy(whole_rows.at[k], merged.at[k], local_sem.at[k]))
        stores[-1].start()
    arrived(19)
    table[:, :, pl.ds(512, C)] = right_all[...]
    stores.append(pltpu.make_async_copy(table, table_out, local_sem.at[2]))
    stores[-1].start()

    for store in stores:
        store.wait()
    for phase in totals:
        whole(phase).wait_send()


def finish_kernel(
    merged, table_in, approx_one, approx_two, fresh_one, fresh_two, new_one, new_two,
    table_ref, rows, approx_ref, fresh_ref, factor_ref, sem,
):
    load = pltpu.make_async_copy(table_in, table_ref, sem.at[0])
    load.start()
    loads = [pltpu.make_async_copy(merged.at[k], rows.at[k], sem.at[1 + k]) for k in range(2)]
    for copy in loads:
        copy.start()
    load.wait()
    table = table_ref[...]
    factors = table[:, :, 768:769] * table[:, 0:1, 512:768]
    for j in range(1, RANK):
        factors += table[:, :, 768 + j : 769 + j] * table[:, j : j + 1, 512:768]
    factors = factors * 0.125
    stores = []
    for k, (approx_out, fresh_out, new_out) in enumerate(
        ((approx_one, fresh_one, new_one), (approx_two, fresh_two, new_two))
    ):
        basis = table[k, :, 0:OWN]
        factor = factors[k]
        b, f = split(basis).astype(F32), split(factor)
        b = jnp.concatenate([b[0:8], b[0:8], b[0:8], b[8:16], b[8:16], b[16:24]], axis=0)
        f = jnp.concatenate([f[0:24].astype(F32), f[0:16].astype(F32), f[0:8].astype(F32)], axis=0)
        approx = lax.dot_general(b.astype(BF), f.astype(BF), TN, preferred_element_type=F32)
        factor_ref[k] = factor
        stores.append(pltpu.make_async_copy(factor_ref.at[k], new_out, sem.at[7 + k]))
        stores[-1].start()
        approx_ref[k] = approx
        stores.append(pltpu.make_async_copy(approx_ref.at[k], approx_out, sem.at[3 + k]))
        stores[-1].start()
        loads[k].wait()
        fresh_ref[k] = rows[k] - approx
        stores.append(pltpu.make_async_copy(fresh_ref.at[k], fresh_out, sem.at[5 + k]))
        stores[-1].start()
    for copy in stores:
        copy.wait()


def on_device(
    latents, cotangent, kernel_one, kernel_two, error_one, error_two, factor_one, factor_two
):
    vmem = pl.BlockSpec(memory_space=pltpu.VMEM)
    hbm = pl.BlockSpec(memory_space=pl.ANY)
    sds = jax.ShapeDtypeStruct
    merged, table = pl.pallas_call(
        train_kernel,
        out_shape=(sds((2, OWN, C), F32), sds((2, RANK, 896), F32)),
        in_specs=[hbm] * 8,
        out_specs=(hbm, hbm),
        scratch_shapes=[
            pltpu.VMEM((2, 6912, C), BF),
            pltpu.VMEM((2, 3, 9 * C, C), BF),
            pltpu.VMEM((2, OWN, 128), F32),
            pltpu.VMEM((FR, 128, C), BF),
            pltpu.VMEM((FR, 96, C), BF),
            pltpu.VMEM((3, FR, 112, C), BF),
            pltpu.VMEM((3, FR, 96, C), BF),
            pltpu.VMEM((FR, 96, C), F32),
            pltpu.VMEM((FR, 80, C), F32),
            pltpu.VMEM((FR, 64, C), F32),
            pltpu.VMEM((256, 9 * 128), BF),
            pltpu.VMEM((OWN, OWN), BF),
            pltpu.VMEM((2, FR, 4, 4, 16, 128), BF),
            pltpu.VMEM((2, 4, FR, 4, 16, 128), BF),
            pltpu.VMEM((2, FR, 4, 64, C), BF),
            pltpu.VMEM((2, 9 * 64, FR * 256), BF),
            pltpu.VMEM((2, 3, 4, 144, C), F32),
            pltpu.VMEM((2, 3, 4, 144, C), BF),
            pltpu.VMEM((2, 3, 4, 144, C), BF),
            pltpu.VMEM((2, 2, 3, 144, C), BF),
            pltpu.VMEM((2, 3, 144, C), BF),
            pltpu.VMEM((2, 3, 144, C), BF),
            pltpu.VMEM((2, 2, OWN, 128), F32),
            pltpu.VMEM((2, 3, 144, C), F32),
            pltpu.VMEM((2, 8, 1728), F32),
            pltpu.VMEM((2, 4, 8, 320), F32),
            pltpu.VMEM((2, 16, 8, 128), F32),
            pltpu.VMEM((16, 8, 128), F32),
            pltpu.VMEM((16, 8, 128), F32),
            pltpu.VMEM((2, 16, 8, 128), F32),
            pltpu.VMEM((2, 8, C), F32),
            pltpu.VMEM((8, 8, C), F32),
            pltpu.VMEM((16, 8, C), F32),
            pltpu.VMEM((4, 8, 128), F32),
            pltpu.VMEM((2, 8, 128), F32),
            pltpu.VMEM((2, 8, C), F32),
            pltpu.VMEM((2, OWN, C), F32),
            pltpu.VMEM((2, RANK, C), F32),
            pltpu.VMEM((2, RANK, 896), F32),
            pltpu.SemaphoreType.DMA((12,)),
            pltpu.SemaphoreType.DMA((25,)),
            pltpu.SemaphoreType.DMA((25,)),
        ],
        compiler_params=pltpu.CompilerParams(
            collective_id=0, has_side_effects=True, vmem_limit_bytes=60 * 2**20
        ),
        name="train",
    )(
        latents.reshape(FR, 64, C),
        cotangent.reshape(FR, 64, C),
        kernel_one,
        kernel_two,
        error_one[0],
        error_two[0],
        factor_one.T,
        factor_two.T,
    )
    block, small = sds((OWN, C), F32), sds((RANK, C), F32)
    approx_one, approx_two, fresh_one, fresh_two, new_one, new_two = pl.pallas_call(
        finish_kernel,
        out_shape=(block, block, block, block, small, small),
        in_specs=[hbm] * 2,
        out_specs=(hbm,) * 6,
        scratch_shapes=[
            pltpu.VMEM((2, RANK, 896), F32),
            pltpu.VMEM((2, OWN, C), F32),
            pltpu.VMEM((2, OWN, C), F32),
            pltpu.VMEM((2, OWN, C), F32),
            pltpu.VMEM((2, RANK, C), F32),
            pltpu.SemaphoreType.DMA((9,)),
        ],
        compiler_params=pltpu.CompilerParams(vmem_limit_bytes=60 * 2**20),
        name="finish",
    )(merged, table)
    return approx_one, approx_two, fresh_one[None], fresh_two[None], new_one.T, new_two.T


def solution(mesh):
    placed = (
        P("rep", None, "tile", None, None),
        P("rep", None, "tile", None, None),
        P(),
        P(),
        P("rep", "tile", None),
        P("rep", "tile", None),
        P(),
        P(),
    )
    return jax.shard_map(
        on_device,
        mesh=mesh,
        in_specs=placed,
        out_specs=(
            P("tile", None),
            P("tile", None),
            P("rep", "tile", None),
            P("rep", "tile", None),
            P(),
            P(),
        ),
        check_vma=False,
    )
```

```python
import functools

import jax
import jax.numpy as jnp
from jax import lax
from jax.experimental import pallas as pl
from jax.experimental.pallas import tpu as pltpu
from jax.sharding import PartitionSpec as P

MESH = pl.DeviceIdType.MESH
HIGH = lax.Precision.HIGHEST
BF = jnp.bfloat16
F32 = jnp.float32
FR = 5
WC = 8
C = 256
RANK = 8
OWN = 432
NT = (((1,), (1,)), ((), ()))
TN = (((0,), (0,)), ((), ()))


def sigmoid(v):
    return 1.0 / (1.0 + jnp.exp(-v))


def silu_slope(v):
    sig = sigmoid(v)
    return sig * (1.0 + v * (1.0 - sig))


def valid_rows(field, first, tile):
    row = lax.broadcasted_iota(jnp.int32, field.shape, 0) + first
    inside = jnp.logical_and(
        jnp.logical_or(row >= 0, tile > 0), jnp.logical_or(row < 8, tile < 15)
    )
    return jnp.where(inside, field, 0.0)


def spread(field, frame, even, odd):
    rows = field.shape[0]
    col = lax.broadcasted_iota(jnp.int32, field.shape, 1)
    for e in range(3):
        if e == 1:
            moved = field
        else:
            moved = pltpu.roll(field, 1 if e == 0 else WC - 1, 1)
            moved = jnp.where(col == (0 if e == 0 else WC - 1), 0.0, moved)
        even[e, frame, pl.ds(0, rows * WC), :] = moved.reshape(rows * WC, C).astype(BF)
        inner = moved[1 : rows - 1].reshape((rows - 2) * WC, C)
        odd[e, frame, pl.ds(0, (rows - 2) * WC), :] = inner.astype(BF)


def conv(even, odd, rows, weights, total, reverse):
    for a in (2, 1, 0):
        count = 3 + a
        first_in, first_out = (2 - a, 0) if reverse else (0, 2 - a)
        pieces = []
        for b in range(3):
            for e in range(3):
                bb, ee = (2 - b, 2 - e) if reverse else (b, e)
                source = odd if bb == 1 else even
                start = 16 if bb == 2 else 0
                piece = source[ee, pl.ds(first_in, count), pl.ds(start, rows * WC), :]
                pieces.append(piece.reshape(count * rows * WC, C))
        lhs = jnp.concatenate(pieces, axis=1)
        if reverse:
            taps = [weights[a, pl.ds(i * C, C), :] for i in range(9)]
            out = lax.dot_general(
                lhs, jnp.concatenate(taps, axis=1), NT, preferred_element_type=F32
            )
        else:
            out = jnp.dot(lhs, weights[a], preferred_element_type=F32)
        out = out.reshape(count, rows * WC, C)
        if a == 2:
            total[...] = out
        else:
            total[pl.ds(first_out, count)] += out


def row_tiles(v):
    return v.reshape(FR, 8, WC, 2, 128).transpose(0, 1, 3, 2, 4).reshape(FR, 8, 16, 128)


def rows_of(v):
    v = v.astype(F32)
    return jnp.concatenate([v[:, 0:8], v[:, 8:16]], axis=2)


def split(v):
    high = v.astype(BF)
    rest = v - high.astype(F32)
    mid = rest.astype(BF)
    low = (rest - mid.astype(F32)).astype(BF)
    return jnp.concatenate([high.astype(F32), mid.astype(F32), low.astype(F32)], axis=0).astype(BF)


def train_kernel(
    lat, cot, ker_one, ker_two, err_one, err_two, fac_one, fac_two,
    merged, table_out,
    raw, weights, chunk, lat_ext, cot_ext, even, odd, acc_one, acc_two, acc_three,
    select, order, flat, turn, turn_in, slopes, patches, part, part_half, part_rest, part_in, part_pass, part_sum, errs, err_rows,
    err_proj, thin, proj, proj_in, left_in, lefts, right, right_in, right_tile, gram_in, gram_all, right_all, whole_rows, factors, table,
    local_sem, send_sem, recv_sem,
):
    tile = lax.axis_index("tile")
    rep = lax.axis_index("rep")
    tz, ty = tile // 4, tile % 4
    rx, core = rep // 2, rep % 2
    near = core * tz + (1 - core) * ty
    other = core * ty + (1 - core) * tz
    here = rx * 4 + near
    pair = {"rep": rx * 2 + 1 - core}
    group = [(dx, dg) for dx in range(4) for dg in range(4) if dx or dg]

    def place(dx, dg):
        return lax.rem(rx + dx, 4) * 4 + lax.rem(near + dg, 4)

    def member(dx, dg):
        z, y = lax.rem(tz + core * dg, 4), lax.rem(ty + (1 - core) * dg, 4)
        return {"rep": lax.rem(rx + dx, 4) * 2 + core, "tile": z * 4 + y}

    def across(d):
        z, y = lax.rem(tz + (1 - core) * d, 4), lax.rem(ty + core * d, 4)
        return {"tile": z * 4 + y}

    def along(axis, d):
        if axis == "z":
            return lax.rem(tz + d, 4) * 4 + ty
        return tz * 4 + lax.rem(ty + d, 4)

    up, down = lax.rem(tile + 15, 16), lax.rem(tile + 1, 16)

    region = pl.when(tile >= 0)
    totals = {}

    def remote(src, dst, phase, device, total=None):
        if phase not in totals:
            totals[phase] = dst if total is None else total
        pltpu.make_async_remote_copy(
            src_ref=src, dst_ref=dst, send_sem=send_sem.at[phase], recv_sem=recv_sem.at[phase],
            device_id=device, device_id_type=MESH,
        ).start()

    def whole(phase):
        ref = totals[phase]
        return pltpu.make_async_remote_copy(
            src_ref=ref, dst_ref=ref, send_sem=send_sem.at[phase], recv_sem=recv_sem.at[phase],
            device_id={"tile": up}, device_id_type=MESH,
        )

    def arrived(phase):
        whole(phase).wait_recv()

    def send_blocks(k):
        for f in range(FR):
            for d in (1, 3):
                to = {"tile": along("y" if k else "z", d)}
                remote(slopes.at[k, f, 0], slopes.at[k, f, d], 8 + k, to, slopes.at[k, :, pl.ds(1, 2)])

    def forward_blocks(k):
        arrived(8 + k)
        for f in range(FR):
            for d, half in ((1, pl.ds(0, 32)), (3, pl.ds(32, 32))):
                to = {"tile": along("y" if k else "z", d)}
                remote(slopes.at[k, f, d, half], slopes.at[k, f, 2, half], 20 + k, to, slopes.at[k, :, 2])

    low, high = pl.ds(0, 80), pl.ds(80, 64)

    def send_far(k, a):
        axis, mine = ("z", tz) if k else ("y", ty)
        chunk_of = part_half.at[k, a, lax.rem(mine + 2, 4)]
        remote(chunk_of.at[low], part_pass.at[k, a, low], 23 + k, {"tile": along(axis, 1)}, part_pass.at[k])
        remote(chunk_of.at[high], part_pass.at[k, a, high], 23 + k, {"tile": along(axis, 3)})

    def send_near(k, a):
        axis, mine = ("z", tz) if k else ("y", ty)
        after, before = part_half.at[k, a, lax.rem(mine + 1, 4)], part_half.at[k, a, lax.rem(mine + 3, 4)]
        remote(after.at[high], part_in.at[k, 0, a, high], 10 + k, {"tile": along(axis, 1)}, part_in.at[k])
        remote(before.at[low], part_in.at[k, 1, a, low], 10 + k, {"tile": along(axis, 3)})

    def pass_on(k):
        axis, mine = ("z", tz) if k else ("y", ty)
        arrived(23 + k)

        @region
        def _():
            for a in range(3):
                for rows, step in ((low, 1), (high, 3)):
                    own_part = part[k, a, lax.rem(mine + step, 4), rows, :]
                    part_sum[k, a, rows, :] = (own_part + part_pass[k, a, rows, :].astype(F32)).astype(BF)

        for a in range(3):
            for rows, step in ((low, 1), (high, 3)):
                to = {"tile": along(axis, step)}
                remote(part_sum.at[k, a, rows], part_in.at[k, step // 2, a, rows], 10 + k, to)

    def send_slopes(k):
        factor = split(factors[k])
        rows = slopes[k, :, 0].reshape(320, C)
        out = lax.dot_general(factor, rows, NT, preferred_element_type=F32)
        thin[k, 0] = out[0:8] + out[8:16] + out[16:24]
        axis = "y" if k else "z"
        for d in range(1, 4):
            to = {"tile": along(axis, d)}
            remote(thin.at[k, 0], thin.at[k, d], 6 + k, to, thin.at[k, pl.ds(1, 3)])
        send_blocks(k)

    def gradients(k):
        arrived(20 + k)
        mine = tz if k else ty
        for a in range(3):

            @region
            def _(a=a):
                count = 3 + a
                rhs = slopes[k, pl.ds(2 - a, count)].reshape(count * 256, C)
                out = jnp.dot(patches[k, :, pl.ds(0, count * 256)], rhs, preferred_element_type=F32)
                part[k, a] = out.reshape(4, 144, C)
                part[k, a, mine] += err_rows[k, a]
                out = part[k, a]
                half = out.astype(BF)
                part_half[k, a] = half
                part_rest[k, a] = (out - half.astype(F32)).astype(BF)

            send_far(k, a)
        for a in range(3):
            send_near(k, a)

    def project_errors():
        for k in range(2):
            mine = tz if k else ty
            for half in range(2):
                loads[6 + 2 * k + half].wait()

            @region
            def _(k=k, mine=mine):
                for half in range(2):
                    for tap in range(27):
                        rows = errs[k, half, pl.ds(tap, 16, stride=27), :]
                        err_rows[k, tap // 9, pl.ds((tap % 9) * 16, 16), pl.ds(half * 128, 128)] = rows
                out = err_rows[k].reshape(OWN, C)
                high = out.astype(BF)
                rest = (out - high.astype(F32)).astype(BF)
                factor = split(factors[k])
                out = lax.dot_general(factor, high, NT, preferred_element_type=F32)
                out += lax.dot_general(factor, rest, NT, preferred_element_type=F32)
                out = out[0:8] + out[8:16] + out[16:24]
                err_proj[k] = jnp.concatenate(
                    [
                        jnp.where(mine == j, out[:, a * 144 : a * 144 + 144], 0.0)
                        for a in range(3)
                        for j in range(4)
                    ],
                    axis=1,
                )

    loads = [
        pltpu.make_async_copy(ker_one, raw.at[0], local_sem.at[0]),
        pltpu.make_async_copy(ker_two, raw.at[1], local_sem.at[1]),
        pltpu.make_async_copy(lat, lat_ext.at[:, pl.ds(3, 8)], local_sem.at[2]),
        pltpu.make_async_copy(cot, cot_ext.at[:, pl.ds(1, 8)], local_sem.at[3]),
    ]
    for k, fac in enumerate((fac_one, fac_two)):
        loads.append(pltpu.make_async_copy(fac, factors.at[k], local_sem.at[4 + k]))
    for k, err in enumerate((err_one, err_two)):
        for half in range(2):
            lanes = pl.ds(half * 128, 128)
            loads.append(
                pltpu.make_async_copy(err.at[:, lanes], errs.at[k, half], local_sem.at[8 + 2 * k + half])
            )
    for load in loads:
        load.start()

    barrier = pltpu.get_barrier_semaphore()
    greeted = [{"tile": lax.rem(tile + d, 16)} for d in range(1, 16)]
    greeted += [pair] + [member(dx, dg) for dx, dg in group if dx]
    greeted += [{"rep": lax.rem(rx + d, 4) * 2 + 1 - core} for d in range(1, 4)]
    for device in greeted:
        pl.semaphore_signal(barrier, inc=1, device_id=device, device_id_type=MESH)
    held = lax.broadcasted_iota(jnp.int32, (256, 128), 0)
    want = lax.broadcasted_iota(jnp.int32, (256, 128), 1)
    same = (held // 128) == (want // 64)
    held, want = held % 128, want % 64
    for b in range(3):
        for e in range(3):
            hit = jnp.logical_and(held // 8 == want // 8 + b, held % 8 == want % 8 + (e - 1))
            hit = jnp.logical_and(same, hit)
            select[:, pl.ds((b * 3 + e) * 128, 128)] = jnp.where(hit, 1.0, 0.0).astype(BF)

    source = lax.broadcasted_iota(jnp.int32, (OWN, OWN), 0)
    target = lax.broadcasted_iota(jnp.int32, (OWN, OWN), 1)
    order[...] = jnp.where(target == (source % 16) * 27 + source // 16, 1.0, 0.0).astype(BF)

    for k in range(2):
        flat[k, pl.ds(400, 112), :] = jnp.zeros((112, C), F32)

    pl.semaphore_wait(barrier, len(greeted))

    remote(lat.at[:, pl.ds(5, 3)], lat_ext.at[:, pl.ds(0, 3)], 0, {"tile": down})
    remote(lat.at[:, pl.ds(0, 3)], lat_ext.at[:, pl.ds(11, 3)], 1, {"tile": up})
    remote(cot.at[:, pl.ds(7, 1)], cot_ext.at[:, pl.ds(0, 1)], 2, {"tile": down})
    remote(cot.at[:, pl.ds(0, 1)], cot_ext.at[:, pl.ds(9, 1)], 3, {"tile": up})

    for k in range(2):
        loads[k].wait()

        def reorder(j, carry, k=k):
            rows = pl.ds(pl.multiple_of(j * OWN, OWN), OWN)
            for half in range(2):
                lanes = pl.ds(half * 128, 128)
                chunk[half] = raw[k, rows, lanes].astype(F32)
                for tap in range(27):
                    picked = chunk[half, pl.ds(tap, 16, stride=27), :].astype(BF)
                    at = pl.multiple_of((tap % 9) * C + j * 16, 16)
                    weights[k, tap // 9, pl.ds(at, 16), lanes] = picked
            return carry

        lax.fori_loop(0, 16, reorder, 0)

    loads[2].wait()
    loads[3].wait()
    arrived(0)
    arrived(1)

    def enter_one(f, carry):
        field = rows_of(lat_ext[f])
        field = valid_rows(field, -3, tile)
        flat[0, pl.ds(f * 80, 80), :] = field[2:12].reshape(80, C)
        spread(field, f, even, odd)
        return carry

    def transpose(k, first, last):
        for t in range(first, last):
            turn[k, t] = flat[k, pl.ds(t * 128, 128), :].T.astype(BF).reshape(4, 4, 16, 128)

    @region
    def _():
        for f in range(FR):
            enter_one(f, 0)
        transpose(0, 0, 4)

    own = [
        pltpu.make_async_copy(turn.at[0, :, tz], turn_in.at[0, 0], local_sem.at[6]),
        pltpu.make_async_copy(turn.at[1, :, :, ty], turn_in.at[1, 0], local_sem.at[7]),
    ]
    own[0].start()
    for d in range(1, 4):
        to = lax.rem(tz + d, 4)
        remote(turn.at[0, :, to], turn_in.at[0, d], 4, {"tile": along("z", d)}, turn_in.at[0, pl.ds(1, 3)])
    region(lambda: conv(even, odd, 12, weights.at[0], acc_one, False))

    totals[5] = turn_in.at[1, pl.ds(1, 3)]
    def enter_two(f, carry):
        pre = acc_one[f]
        hidden = (pre * sigmoid(pre)).astype(BF).astype(F32).reshape(12, WC, C)
        hidden = valid_rows(hidden, -2, tile)
        flat[1, pl.ds(f * 80, 80), :] = hidden[1:11].reshape(80, C)
        spread(hidden, f, even, odd)
        return carry

    for frames, first, last in (((0, 1), 0, 1), ((2, 3, 4), 1, 4)):

        @region
        def _():
            for f in frames:
                enter_two(f, 0)
            transpose(1, first, last)

        for t in range(first, last):
            for d in range(1, 4):
                to = lax.rem(ty + d, 4)
                remote(turn.at[1, t, :, to], turn_in.at[1, d, t], 5, {"tile": along("y", d)})
    own[1].start()
    region(lambda: conv(even, odd, 10, weights.at[1], acc_two, False))

    arrived(2)
    arrived(3)
    loads[4].wait()
    loads[5].wait()

    def enter_three(f, carry):
        cots = rows_of(cot_ext[f]).reshape(80, C)
        slope = (cots * silu_slope(acc_two[f])).astype(BF).astype(F32).reshape(10, WC, C)
        slope = valid_rows(slope, -1, tile)
        spread(slope, f, even, odd)
        slopes[1, f, 0] = slope[1:9].reshape(64, C).astype(BF)
        return carry

    region(lambda: [enter_three(f, 0) for f in range(FR)] and None)
    send_slopes(1)
    region(lambda: conv(even, odd, 8, weights.at[1], acc_three, True))

    def leave(f, carry):
        pre = acc_one[f, pl.ds(16, 64), :]
        slopes[0, f, 0] = (acc_three[f] * silu_slope(pre)).astype(BF)
        return carry

    region(lambda: [leave(f, 0) for f in range(FR)] and None)
    send_slopes(0)

    for k in range(2):
        if k == 1:
            project_errors()
        own[k].wait()
        arrived(4 + k)

        @region
        def _(k=k):
            for p in range(2):
                blocks = []
                for s in range(2):
                    wide = [turn_in[k, 2 * p + s, t].reshape(64, 128) for t in range(4)]
                    wide = jnp.concatenate(wide, axis=1)
                    wide = [wide[:, f * 80 : f * 80 + 128] for f in range(FR)]
                    blocks.append(jnp.concatenate(wide, axis=0))
                lhs = jnp.concatenate(blocks, axis=1)
                out = jnp.dot(lhs, select[...], preferred_element_type=F32).astype(BF)
                for f in range(FR):
                    for i in range(9):
                        for j in range(4):
                            block = out[f * 64 + j * 16 : f * 64 + j * 16 + 16, i * 128 : i * 128 + 128]
                            rows = pl.ds(j * 144 + i * 16, 16)
                            patches[k, rows, pl.ds(f * 256 + p * 128, 128)] = block

    for k in (1, 0):
        arrived(6 + k)

        @region
        def _(k=k):
            blocks = [thin[k, d] for d in range(4)]
            wide = jnp.concatenate(
                [blocks[d][:, f * 64 : f * 64 + 64] for f in range(FR) for d in range(4)], axis=1
            )
            shifts = [
                jnp.concatenate([wide[:, (2 - a) * 256 :], jnp.zeros((8, (2 - a) * 256), F32)], axis=1)
                if a < 2
                else wide
                for a in range(3)
            ]
            wide = split(jnp.concatenate(shifts, axis=0))
            out = lax.dot_general(wide, patches[k], NT, preferred_element_type=F32)
            out = out[0:24] + out[24:48] + out[48:72]
            out = jnp.concatenate([out[0:8], out[8:16], out[16:24]], axis=1)
            sample = out + err_proj[k]
            sample = jnp.concatenate([sample, jnp.zeros((8, 2048 - 1728), F32)], axis=1)
            for q in range(16):
                proj[k, q] = sample[:, q * 128 : q * 128 + 128]

    remote(proj.at[1 - core], proj_in, 12, pair)
    arrived(12)
    for q in range(16):
        proj_in[q] = proj_in[q] + proj[core, q]
    for dx, dg in group:
        to = place(dx, dg)
        remote(proj_in.at[to], left_in.at[here], 13, member(dx, dg), left_in.at[pl.ds(0, 15)])
    left_in[here] = proj_in[here]
    forward_blocks(1)
    forward_blocks(0)

    arrived(13)
    piece = left_in[0]
    for q in range(1, 16):
        piece = piece + left_in[q]
    lefts[core, here] = piece * 0.125
    for dx, dg in group:
        block = lefts.at[core, here]
        remote(block, block, 14, member(dx, dg), lefts.at[0, pl.ds(0, 15)])
    gradients(1)
    gradients(0)
    arrived(14)
    remote(lefts.at[core], lefts.at[core], 15, pair)
    arrived(15)

    for k in range(2):

        @region
        def _(k=k):
            rows_all = jnp.concatenate([lefts[k, q] for q in range(16)], axis=1)[:, 0:1728]
            pieces = split(rows_all)
            out = jnp.dot(pieces, part_half[k].reshape(1728, C), preferred_element_type=F32)
            out += jnp.dot(pieces, part_rest[k].reshape(1728, C), preferred_element_type=F32)
            right[k] = out[0:8] + out[8:16] + out[16:24]

    for d in range(1, 4):
        for on in (core, 1 - core):
            to = {"rep": lax.rem(rx + d, 4) * 2 + on}
            remote(right.at[on], right_in.at[rep], 17, to, right_in.at[pl.ds(0, 7)])
    remote(right.at[1 - core], right_in.at[rep], 17, pair)
    right_in[rep] = right[core]

    for k in range(2):
        mine = tz if k else ty

        @region
        def _(k=k, mine=mine):
            rows_all = jnp.concatenate([lefts[k, q] for q in range(16)], axis=1)[:, 0:1728]
            gram = lax.dot_general(rows_all, rows_all, NT, precision=HIGH, preferred_element_type=F32)
            gram = jnp.concatenate([gram, jnp.zeros((8, 120), F32)], axis=1)

            @pl.when(core == k)
            def _():
                gram_in[other] = gram

            rows = []
            for a in range(3):
                found = jnp.zeros((8, 144), F32)
                for j in range(4):
                    at = a * 576 + j * 144
                    found = jnp.where(mine == j, rows_all[:, at : at + 144], found)
                rows.append(found)
            out = split(jnp.concatenate(rows, axis=1))
            out = jnp.dot(out, order[...], preferred_element_type=F32)
            out = out[0:8] + out[8:16] + out[16:24]
            table[k, :, pl.ds(0, 512)] = jnp.concatenate([out, jnp.zeros((8, 80), F32)], axis=1)

    for d in range(1, 4):
        remote(gram_in.at[other], gram_in.at[other], 22, across(d), gram_in.at[pl.ds(0, 3)])

    pass_on(1)
    pass_on(0)
    arrived(17)
    total = right_in[0]
    for q in range(1, 8):
        total = total + right_in[q]
    right_tile[tile] = total
    for d in range(1, 16):
        block = right_tile.at[tile]
        remote(block, block, 18, {"tile": lax.rem(tile + d, 16)}, right_tile.at[pl.ds(0, 15)])
    arrived(22)
    gram_all[core] = gram_in[0] + gram_in[1] + gram_in[2] + gram_in[3]
    remote(gram_all.at[core], gram_all.at[core], 16, pair)
    arrived(16)

    @region
    def _():
        row = lax.broadcasted_iota(jnp.int32, (2, RANK, 768), 1)
        lane = lax.broadcasted_iota(jnp.int32, (2, RANK, 128), 2)
        eye = jnp.where(lane == row[:, :, 0:128], 1.0, 0.0)
        rows = jnp.concatenate([table[:, :, 0:512], gram_all[...], eye], axis=2)
        for j in range(RANK):
            scale = lax.rsqrt(rows[:, j : j + 1, 512 + j : 513 + j])
            scaled = rows[:, j : j + 1, :] * scale
            coefs = rows[:, :, 512 + j : 513 + j] * scale
            rows = jnp.where(row == j, scaled, jnp.where(row > j, rows - coefs * scaled, rows))
        table[:, :, pl.ds(0, 512)] = rows[:, :, 0:512]
        table[:, :, pl.ds(768, 128)] = rows[:, :, 640:768]

    arrived(18)
    total = right_tile[0]
    for q in range(1, 16):
        total = total + right_tile[q]
    right_all[core] = total
    remote(right_all.at[core], right_all.at[core], 19, pair)
    stores = []
    for k in (1, 0):
        mine = tz if k else ty
        arrived(10 + k)

        @region
        def _(k=k, mine=mine):
            for tap in range(27):
                a, rows = tap // 9, pl.ds((tap % 9) * 16, 16)
                grad = part[k, a, mine, rows, :]
                for d in range(2):
                    grad = grad + part_in[k, d, a, rows, :].astype(F32)
                for half in range(2):
                    chunk[half, pl.ds(tap, 16, stride=27), :] = grad[:, half * 128 : half * 128 + 128]
            for half in range(2):
                whole_rows[k, :, pl.ds(half * 128, 128)] = chunk[half]

        stores.append(pltpu.make_async_copy(whole_rows.at[k], merged.at[k], local_sem.at[k]))
        stores[-1].start()
    arrived(19)
    table[:, :, pl.ds(512, C)] = right_all[...]
    stores.append(pltpu.make_async_copy(table, table_out, local_sem.at[2]))
    stores[-1].start()

    for store in stores:
        store.wait()
    for phase in totals:
        whole(phase).wait_send()


def finish_kernel(
    merged, table_in, approx_one, approx_two, fresh_one, fresh_two, new_one, new_two,
    table_ref, rows, approx_ref, fresh_ref, factor_ref, sem,
):
    load = pltpu.make_async_copy(table_in, table_ref, sem.at[0])
    load.start()
    loads = [pltpu.make_async_copy(merged.at[k], rows.at[k], sem.at[1 + k]) for k in range(2)]
    for copy in loads:
        copy.start()
    load.wait()
    table = table_ref[...]
    factors = table[:, :, 768:769] * table[:, 0:1, 512:768]
    for j in range(1, RANK):
        factors += table[:, :, 768 + j : 769 + j] * table[:, j : j + 1, 512:768]
    factors = factors * 0.125
    stores = []
    for k, (approx_out, fresh_out, new_out) in enumerate(
        ((approx_one, fresh_one, new_one), (approx_two, fresh_two, new_two))
    ):
        basis = table[k, :, 0:OWN]
        factor = factors[k]
        b, f = split(basis).astype(F32), split(factor)
        b = jnp.concatenate([b[0:8], b[0:8], b[0:8], b[8:16], b[8:16], b[16:24]], axis=0)
        f = jnp.concatenate([f[0:24].astype(F32), f[0:16].astype(F32), f[0:8].astype(F32)], axis=0)
        approx = lax.dot_general(b.astype(BF), f.astype(BF), TN, preferred_element_type=F32)
        factor_ref[k] = factor
        stores.append(pltpu.make_async_copy(factor_ref.at[k], new_out, sem.at[7 + k]))
        stores[-1].start()
        approx_ref[k] = approx
        stores.append(pltpu.make_async_copy(approx_ref.at[k], approx_out, sem.at[3 + k]))
        stores[-1].start()
        loads[k].wait()
        fresh_ref[k] = rows[k] - approx
        stores.append(pltpu.make_async_copy(fresh_ref.at[k], fresh_out, sem.at[5 + k]))
        stores[-1].start()
    for copy in stores:
        copy.wait()


def on_device(
    latents, cotangent, kernel_one, kernel_two, error_one, error_two, factor_one, factor_two
):
    vmem = pl.BlockSpec(memory_space=pltpu.VMEM)
    hbm = pl.BlockSpec(memory_space=pl.ANY)
    sds = jax.ShapeDtypeStruct
    merged, table = pl.pallas_call(
        train_kernel,
        out_shape=(sds((2, OWN, C), F32), sds((2, RANK, 896), F32)),
        in_specs=[hbm] * 8,
        out_specs=(hbm, hbm),
        scratch_shapes=[
            pltpu.VMEM((2, 6912, C), BF),
            pltpu.VMEM((2, 3, 9 * C, C), BF),
            pltpu.VMEM((2, OWN, 128), F32),
            pltpu.VMEM((FR, 14, 16, 128), BF),
            pltpu.VMEM((FR, 10, 16, 128), BF),
            pltpu.VMEM((3, FR, 112, C), BF),
            pltpu.VMEM((3, FR, 96, C), BF),
            pltpu.VMEM((FR, 96, C), F32),
            pltpu.VMEM((FR, 80, C), F32),
            pltpu.VMEM((FR, 64, C), F32),
            pltpu.VMEM((256, 9 * 128), BF),
            pltpu.VMEM((OWN, OWN), BF),
            pltpu.VMEM((2, 512, C), F32),
            pltpu.VMEM((2, 4, 4, 4, 16, 128), BF),
            pltpu.VMEM((2, 4, 4, 4, 16, 128), BF),
            pltpu.VMEM((2, FR, 4, 64, C), BF),
            pltpu.VMEM((2, 9 * 64, FR * 256), BF),
            pltpu.VMEM((2, 3, 4, 144, C), F32),
            pltpu.VMEM((2, 3, 4, 144, C), BF),
            pltpu.VMEM((2, 3, 4, 144, C), BF),
            pltpu.VMEM((2, 2, 3, 144, C), BF),
            pltpu.VMEM((2, 3, 144, C), BF),
            pltpu.VMEM((2, 3, 144, C), BF),
            pltpu.VMEM((2, 2, OWN, 128), F32),
            pltpu.VMEM((2, 3, 144, C), F32),
            pltpu.VMEM((2, 8, 1728), F32),
            pltpu.VMEM((2, 4, 8, 320), F32),
            pltpu.VMEM((2, 16, 8, 128), F32),
            pltpu.VMEM((16, 8, 128), F32),
            pltpu.VMEM((16, 8, 128), F32),
            pltpu.VMEM((2, 16, 8, 128), F32),
            pltpu.VMEM((2, 8, C), F32),
            pltpu.VMEM((8, 8, C), F32),
            pltpu.VMEM((16, 8, C), F32),
            pltpu.VMEM((4, 8, 128), F32),
            pltpu.VMEM((2, 8, 128), F32),
            pltpu.VMEM((2, 8, C), F32),
            pltpu.VMEM((2, OWN, C), F32),
            pltpu.VMEM((2, RANK, C), F32),
            pltpu.VMEM((2, RANK, 896), F32),
            pltpu.SemaphoreType.DMA((12,)),
            pltpu.SemaphoreType.DMA((25,)),
            pltpu.SemaphoreType.DMA((25,)),
        ],
        compiler_params=pltpu.CompilerParams(
            collective_id=0, has_side_effects=True, vmem_limit_bytes=60 * 2**20
        ),
        name="train",
    )(
        row_tiles(latents[0]),
        row_tiles(cotangent[0]),
        kernel_one,
        kernel_two,
        error_one[0],
        error_two[0],
        factor_one.T,
        factor_two.T,
    )
    block, small = sds((OWN, C), F32), sds((RANK, C), F32)
    approx_one, approx_two, fresh_one, fresh_two, new_one, new_two = pl.pallas_call(
        finish_kernel,
        out_shape=(block, block, block, block, small, small),
        in_specs=[hbm] * 2,
        out_specs=(hbm,) * 6,
        scratch_shapes=[
            pltpu.VMEM((2, RANK, 896), F32),
            pltpu.VMEM((2, OWN, C), F32),
            pltpu.VMEM((2, OWN, C), F32),
            pltpu.VMEM((2, OWN, C), F32),
            pltpu.VMEM((2, RANK, C), F32),
            pltpu.SemaphoreType.DMA((9,)),
        ],
        compiler_params=pltpu.CompilerParams(vmem_limit_bytes=60 * 2**20),
        name="finish",
    )(merged, table)
    return approx_one, approx_two, fresh_one[None], fresh_two[None], new_one.T, new_two.T


def solution(mesh):
    placed = (
        P("rep", None, "tile", None, None),
        P("rep", None, "tile", None, None),
        P(),
        P(),
        P("rep", "tile", None),
        P("rep", "tile", None),
        P(),
        P(),
    )
    return jax.shard_map(
        on_device,
        mesh=mesh,
        in_specs=placed,
        out_specs=(
            P("tile", None),
            P("tile", None),
            P("rep", "tile", None),
            P("rep", "tile", None),
            P(),
            P(),
        ),
        check_vma=False,
    )
```

```python
import functools

import jax
import jax.numpy as jnp
from jax import lax
from jax.experimental import pallas as pl
from jax.experimental.pallas import tpu as pltpu
from jax.sharding import PartitionSpec as P

MESH = pl.DeviceIdType.MESH
HIGH = lax.Precision.HIGHEST
BF = jnp.bfloat16
F32 = jnp.float32
FR = 5
WC = 8
C = 256
RANK = 8
OWN = 432
NT = (((1,), (1,)), ((), ()))
TN = (((0,), (0,)), ((), ()))


def sigmoid(v):
    return 1.0 / (1.0 + jnp.exp(-v))


def silu_slope(v):
    sig = sigmoid(v)
    return sig * (1.0 + v * (1.0 - sig))


def valid_rows(field, first, tile):
    row = lax.broadcasted_iota(jnp.int32, field.shape, 0) + first
    inside = jnp.logical_and(
        jnp.logical_or(row >= 0, tile > 0), jnp.logical_or(row < 8, tile < 15)
    )
    return jnp.where(inside, field, 0.0)


def spread(field, frame, even, odd):
    rows = field.shape[0]
    col = lax.broadcasted_iota(jnp.int32, field.shape, 1)
    for e in range(3):
        if e == 1:
            moved = field
        else:
            moved = pltpu.roll(field, 1 if e == 0 else WC - 1, 1)
            moved = jnp.where(col == (0 if e == 0 else WC - 1), 0.0, moved)
        even[e, frame, pl.ds(0, rows * WC), :] = moved.reshape(rows * WC, C).astype(BF)
        inner = moved[1 : rows - 1].reshape((rows - 2) * WC, C)
        odd[e, frame, pl.ds(0, (rows - 2) * WC), :] = inner.astype(BF)


def conv(even, odd, rows, weights, total, reverse):
    for a in (2, 1, 0):
        count = 3 + a
        first_in, first_out = (2 - a, 0) if reverse else (0, 2 - a)
        pieces = []
        for b in range(3):
            for e in range(3):
                bb, ee = (2 - b, 2 - e) if reverse else (b, e)
                source = odd if bb == 1 else even
                start = 16 if bb == 2 else 0
                piece = source[ee, pl.ds(first_in, count), pl.ds(start, rows * WC), :]
                pieces.append(piece.reshape(count * rows * WC, C))
        lhs = jnp.concatenate(pieces, axis=1)
        if reverse:
            taps = [weights[a, pl.ds(i * C, C), :] for i in range(9)]
            out = lax.dot_general(
                lhs, jnp.concatenate(taps, axis=1), NT, preferred_element_type=F32
            )
        else:
            out = jnp.dot(lhs, weights[a], preferred_element_type=F32)
        out = out.reshape(count, rows * WC, C)
        if a == 2:
            total[...] = out
        else:
            total[pl.ds(first_out, count)] += out


def row_tiles(v):
    return v.reshape(FR, 8, WC, 2, 128).transpose(0, 1, 3, 2, 4).reshape(FR, 8, 16, 128)


def rows_of(v):
    v = v.astype(F32)
    return jnp.concatenate([v[:, 0:8], v[:, 8:16]], axis=2)


def split(v):
    high = v.astype(BF)
    rest = v - high.astype(F32)
    mid = rest.astype(BF)
    low = (rest - mid.astype(F32)).astype(BF)
    return jnp.concatenate([high.astype(F32), mid.astype(F32), low.astype(F32)], axis=0).astype(BF)


def train_kernel(
    lat, cot, ker_one, ker_two, err_one, err_two, fac_one, fac_two,
    merged, table_out,
    raw, weights, chunk, lat_ext, cot_ext, even, odd, acc_one, acc_two, acc_three,
    select, order, flat, turn, turn_in, slopes, patches, part, part_half, part_rest, part_in, part_pass, part_sum, errs, err_rows,
    err_proj, thin, proj, proj_in, left_in, lefts, right, right_in, right_tile, gram_in, gram_all, right_all, whole_rows, factors, table,
    local_sem, send_sem, recv_sem,
):
    tile = lax.axis_index("tile")
    rep = lax.axis_index("rep")
    tz, ty = tile // 4, tile % 4
    rx, core = rep // 2, rep % 2
    near = core * tz + (1 - core) * ty
    other = core * ty + (1 - core) * tz
    here = rx * 4 + near
    pair = {"rep": rx * 2 + 1 - core}
    group = sorted(
        [(dx, dg) for dx in range(4) for dg in range(4) if dx or dg],
        key=lambda step: -min(step[0], 4 - step[0]) - min(step[1], 4 - step[1]),
    )

    def place(dx, dg):
        return lax.rem(rx + dx, 4) * 4 + lax.rem(near + dg, 4)

    def member(dx, dg):
        z, y = lax.rem(tz + core * dg, 4), lax.rem(ty + (1 - core) * dg, 4)
        return {"rep": lax.rem(rx + dx, 4) * 2 + core, "tile": z * 4 + y}

    def across(d):
        z, y = lax.rem(tz + (1 - core) * d, 4), lax.rem(ty + core * d, 4)
        return {"tile": z * 4 + y}

    def along(axis, d):
        if axis == "z":
            return lax.rem(tz + d, 4) * 4 + ty
        return tz * 4 + lax.rem(ty + d, 4)

    up, down = lax.rem(tile + 15, 16), lax.rem(tile + 1, 16)

    region = pl.when(tile >= 0)
    totals = {}

    def remote(src, dst, phase, device, total=None):
        if phase not in totals:
            totals[phase] = dst if total is None else total
        pltpu.make_async_remote_copy(
            src_ref=src, dst_ref=dst, send_sem=send_sem.at[phase], recv_sem=recv_sem.at[phase],
            device_id=device, device_id_type=MESH,
        ).start()

    def whole(phase):
        ref = totals[phase]
        return pltpu.make_async_remote_copy(
            src_ref=ref, dst_ref=ref, send_sem=send_sem.at[phase], recv_sem=recv_sem.at[phase],
            device_id={"tile": up}, device_id_type=MESH,
        )

    def arrived(phase):
        whole(phase).wait_recv()

    def send_blocks(k):
        for f in range(FR):
            for d in (1, 3):
                to = {"tile": along("y" if k else "z", d)}
                remote(slopes.at[k, f, 0], slopes.at[k, f, d], 8 + k, to, slopes.at[k, :, pl.ds(1, 2)])

    def forward_blocks(k):
        arrived(8 + k)
        for f in range(FR):
            for d, half in ((1, pl.ds(0, 32)), (3, pl.ds(32, 32))):
                to = {"tile": along("y" if k else "z", d)}
                remote(slopes.at[k, f, d, half], slopes.at[k, f, 2, half], 20 + k, to, slopes.at[k, :, 2])

    low, high = pl.ds(0, 80), pl.ds(80, 64)

    def send_far(k, a):
        axis, mine = ("z", tz) if k else ("y", ty)
        chunk_of = part_half.at[k, a, lax.rem(mine + 2, 4)]
        remote(chunk_of.at[low], part_pass.at[k, a, low], 23 + k, {"tile": along(axis, 1)}, part_pass.at[k])
        remote(chunk_of.at[high], part_pass.at[k, a, high], 23 + k, {"tile": along(axis, 3)})

    def send_near(k, a):
        axis, mine = ("z", tz) if k else ("y", ty)
        after, before = part_half.at[k, a, lax.rem(mine + 1, 4)], part_half.at[k, a, lax.rem(mine + 3, 4)]
        remote(after.at[high], part_in.at[k, 0, a, high], 10 + k, {"tile": along(axis, 1)}, part_in.at[k])
        remote(before.at[low], part_in.at[k, 1, a, low], 10 + k, {"tile": along(axis, 3)})

    def pass_on(k):
        axis, mine = ("z", tz) if k else ("y", ty)
        arrived(23 + k)

        @region
        def _():
            for a in range(3):
                for rows, step in ((low, 1), (high, 3)):
                    own_part = part[k, a, lax.rem(mine + step, 4), rows, :]
                    part_sum[k, a, rows, :] = (own_part + part_pass[k, a, rows, :].astype(F32)).astype(BF)

        for a in range(3):
            for rows, step in ((low, 1), (high, 3)):
                to = {"tile": along(axis, step)}
                remote(part_sum.at[k, a, rows], part_in.at[k, step // 2, a, rows], 10 + k, to)

    def send_slopes(k):
        factor = split(factors[k])
        rows = slopes[k, :, 0].reshape(320, C)
        out = lax.dot_general(factor, rows, NT, preferred_element_type=F32)
        thin[k, 0] = out[0:8] + out[8:16] + out[16:24]
        axis = "y" if k else "z"
        for d in range(1, 4):
            to = {"tile": along(axis, d)}
            remote(thin.at[k, 0], thin.at[k, d], 6 + k, to, thin.at[k, pl.ds(1, 3)])
        send_blocks(k)

    def gradients(k):
        arrived(20 + k)
        mine = tz if k else ty
        for a in range(3):

            @region
            def _(a=a):
                count = 3 + a
                rhs = slopes[k, pl.ds(2 - a, count)].reshape(count * 256, C)
                out = jnp.dot(patches[k, :, pl.ds(0, count * 256)], rhs, preferred_element_type=F32)
                part[k, a] = out.reshape(4, 144, C)
                part[k, a, mine] += err_rows[k, a]
                out = part[k, a]
                half = out.astype(BF)
                part_half[k, a] = half
                part_rest[k, a] = (out - half.astype(F32)).astype(BF)

            send_far(k, a)
        for a in range(3):
            send_near(k, a)

    def project_errors():
        for k in range(2):
            mine = tz if k else ty
            for half in range(2):
                loads[6 + 2 * k + half].wait()

            @region
            def _(k=k, mine=mine):
                for half in range(2):
                    for tap in range(27):
                        rows = errs[k, half, pl.ds(tap, 16, stride=27), :]
                        err_rows[k, tap // 9, pl.ds((tap % 9) * 16, 16), pl.ds(half * 128, 128)] = rows
                out = err_rows[k].reshape(OWN, C)
                high = out.astype(BF)
                rest = (out - high.astype(F32)).astype(BF)
                factor = split(factors[k])
                out = lax.dot_general(factor, high, NT, preferred_element_type=F32)
                out += lax.dot_general(factor, rest, NT, preferred_element_type=F32)
                out = out[0:8] + out[8:16] + out[16:24]
                err_proj[k] = jnp.concatenate(
                    [
                        jnp.where(mine == j, out[:, a * 144 : a * 144 + 144], 0.0)
                        for a in range(3)
                        for j in range(4)
                    ],
                    axis=1,
                )

    loads = [
        pltpu.make_async_copy(ker_one, raw.at[0], local_sem.at[0]),
        pltpu.make_async_copy(ker_two, raw.at[1], local_sem.at[1]),
        pltpu.make_async_copy(lat, lat_ext.at[:, pl.ds(3, 8)], local_sem.at[2]),
        pltpu.make_async_copy(cot, cot_ext.at[:, pl.ds(1, 8)], local_sem.at[3]),
    ]
    for k, fac in enumerate((fac_one, fac_two)):
        loads.append(pltpu.make_async_copy(fac, factors.at[k], local_sem.at[4 + k]))
    for k, err in enumerate((err_one, err_two)):
        for half in range(2):
            lanes = pl.ds(half * 128, 128)
            loads.append(
                pltpu.make_async_copy(err.at[:, lanes], errs.at[k, half], local_sem.at[8 + 2 * k + half])
            )
    for load in loads:
        load.start()

    barrier = pltpu.get_barrier_semaphore()
    greeted = [{"tile": lax.rem(tile + d, 16)} for d in range(1, 16)]
    greeted += [pair] + [member(dx, dg) for dx, dg in group if dx]
    greeted += [{"rep": lax.rem(rx + d, 4) * 2 + 1 - core} for d in range(1, 4)]
    for device in greeted:
        pl.semaphore_signal(barrier, inc=1, device_id=device, device_id_type=MESH)
    held = lax.broadcasted_iota(jnp.int32, (256, 128), 0)
    want = lax.broadcasted_iota(jnp.int32, (256, 128), 1)
    same = (held // 128) == (want // 64)
    held, want = held % 128, want % 64
    for b in range(3):
        for e in range(3):
            hit = jnp.logical_and(held // 8 == want // 8 + b, held % 8 == want % 8 + (e - 1))
            hit = jnp.logical_and(same, hit)
            select[:, pl.ds((b * 3 + e) * 128, 128)] = jnp.where(hit, 1.0, 0.0).astype(BF)

    source = lax.broadcasted_iota(jnp.int32, (OWN, OWN), 0)
    target = lax.broadcasted_iota(jnp.int32, (OWN, OWN), 1)
    order[...] = jnp.where(target == (source % 16) * 27 + source // 16, 1.0, 0.0).astype(BF)

    for k in range(2):
        flat[k, pl.ds(400, 112), :] = jnp.zeros((112, C), F32)

    pl.semaphore_wait(barrier, len(greeted))

    remote(lat.at[:, pl.ds(5, 3)], lat_ext.at[:, pl.ds(0, 3)], 0, {"tile": down})
    remote(lat.at[:, pl.ds(0, 3)], lat_ext.at[:, pl.ds(11, 3)], 1, {"tile": up})
    remote(cot.at[:, pl.ds(7, 1)], cot_ext.at[:, pl.ds(0, 1)], 2, {"tile": down})
    remote(cot.at[:, pl.ds(0, 1)], cot_ext.at[:, pl.ds(9, 1)], 3, {"tile": up})

    for k in range(2):
        loads[k].wait()

        def reorder(j, carry, k=k):
            rows = pl.ds(pl.multiple_of(j * OWN, OWN), OWN)
            for half in range(2):
                lanes = pl.ds(half * 128, 128)
                chunk[half] = raw[k, rows, lanes].astype(F32)
                for tap in range(27):
                    picked = chunk[half, pl.ds(tap, 16, stride=27), :].astype(BF)
                    at = pl.multiple_of((tap % 9) * C + j * 16, 16)
                    weights[k, tap // 9, pl.ds(at, 16), lanes] = picked
            return carry

        lax.fori_loop(0, 16, reorder, 0)

    loads[2].wait()
    loads[3].wait()
    arrived(0)
    arrived(1)

    def enter_one(f, carry):
        field = rows_of(lat_ext[f])
        field = valid_rows(field, -3, tile)
        flat[0, pl.ds(f * 80, 80), :] = field[2:12].reshape(80, C)
        spread(field, f, even, odd)
        return carry

    def transpose(k, first, last):
        for t in range(first, last):
            turn[k, t] = flat[k, pl.ds(t * 128, 128), :].T.astype(BF).reshape(4, 4, 16, 128)

    @region
    def _():
        for f in range(FR):
            enter_one(f, 0)
        transpose(0, 0, 4)

    own = [
        pltpu.make_async_copy(turn.at[0, :, tz], turn_in.at[0, 0], local_sem.at[6]),
        pltpu.make_async_copy(turn.at[1, :, :, ty], turn_in.at[1, 0], local_sem.at[7]),
    ]
    own[0].start()
    for d in range(1, 4):
        to = lax.rem(tz + d, 4)
        remote(turn.at[0, :, to], turn_in.at[0, d], 4, {"tile": along("z", d)}, turn_in.at[0, pl.ds(1, 3)])
    region(lambda: conv(even, odd, 12, weights.at[0], acc_one, False))

    totals[5] = turn_in.at[1, pl.ds(1, 3)]
    def enter_two(f, carry):
        pre = acc_one[f]
        hidden = (pre * sigmoid(pre)).astype(BF).astype(F32).reshape(12, WC, C)
        hidden = valid_rows(hidden, -2, tile)
        flat[1, pl.ds(f * 80, 80), :] = hidden[1:11].reshape(80, C)
        spread(hidden, f, even, odd)
        return carry

    for frames, first, last in (((0, 1), 0, 1), ((2, 3, 4), 1, 4)):

        @region
        def _():
            for f in frames:
                enter_two(f, 0)
            transpose(1, first, last)

        for t in range(first, last):
            for d in range(1, 4):
                to = lax.rem(ty + d, 4)
                remote(turn.at[1, t, :, to], turn_in.at[1, d, t], 5, {"tile": along("y", d)})
    own[1].start()
    region(lambda: conv(even, odd, 10, weights.at[1], acc_two, False))

    arrived(2)
    arrived(3)
    loads[4].wait()
    loads[5].wait()

    def enter_three(f, carry):
        cots = rows_of(cot_ext[f]).reshape(80, C)
        slope = (cots * silu_slope(acc_two[f])).astype(BF).astype(F32).reshape(10, WC, C)
        slope = valid_rows(slope, -1, tile)
        spread(slope, f, even, odd)
        slopes[1, f, 0] = slope[1:9].reshape(64, C).astype(BF)
        return carry

    region(lambda: [enter_three(f, 0) for f in range(FR)] and None)
    send_slopes(1)
    region(lambda: conv(even, odd, 8, weights.at[1], acc_three, True))

    def leave(f, carry):
        pre = acc_one[f, pl.ds(16, 64), :]
        slopes[0, f, 0] = (acc_three[f] * silu_slope(pre)).astype(BF)
        return carry

    region(lambda: [leave(f, 0) for f in range(FR)] and None)
    send_slopes(0)

    for k in range(2):
        if k == 1:
            project_errors()
        own[k].wait()
        arrived(4 + k)

        @region
        def _(k=k):
            for p in range(2):
                blocks = []
                for s in range(2):
                    wide = [turn_in[k, 2 * p + s, t].reshape(64, 128) for t in range(4)]
                    wide = jnp.concatenate(wide, axis=1)
                    wide = [wide[:, f * 80 : f * 80 + 128] for f in range(FR)]
                    blocks.append(jnp.concatenate(wide, axis=0))
                lhs = jnp.concatenate(blocks, axis=1)
                out = jnp.dot(lhs, select[...], preferred_element_type=F32).astype(BF)
                for f in range(FR):
                    for i in range(9):
                        for j in range(4):
                            block = out[f * 64 + j * 16 : f * 64 + j * 16 + 16, i * 128 : i * 128 + 128]
                            rows = pl.ds(j * 144 + i * 16, 16)
                            patches[k, rows, pl.ds(f * 256 + p * 128, 128)] = block

    for k in (1, 0):
        arrived(6 + k)

        @region
        def _(k=k):
            blocks = [thin[k, d] for d in range(4)]
            wide = jnp.concatenate(
                [blocks[d][:, f * 64 : f * 64 + 64] for f in range(FR) for d in range(4)], axis=1
            )
            shifts = [
                jnp.concatenate([wide[:, (2 - a) * 256 :], jnp.zeros((8, (2 - a) * 256), F32)], axis=1)
                if a < 2
                else wide
                for a in range(3)
            ]
            wide = split(jnp.concatenate(shifts, axis=0))
            out = lax.dot_general(wide, patches[k], NT, preferred_element_type=F32)
            out = out[0:24] + out[24:48] + out[48:72]
            out = jnp.concatenate([out[0:8], out[8:16], out[16:24]], axis=1)
            sample = out + err_proj[k]
            sample = jnp.concatenate([sample, jnp.zeros((8, 2048 - 1728), F32)], axis=1)
            for q in range(16):
                proj[k, q] = sample[:, q * 128 : q * 128 + 128]

    remote(proj.at[1 - core], proj_in, 12, pair)
    arrived(12)
    for q in range(16):
        proj_in[q] = proj_in[q] + proj[core, q]
    for dx, dg in group:
        to = place(dx, dg)
        remote(proj_in.at[to], left_in.at[here], 13, member(dx, dg), left_in.at[pl.ds(0, 15)])
    left_in[here] = proj_in[here]
    forward_blocks(1)
    forward_blocks(0)

    arrived(13)
    piece = left_in[0]
    for q in range(1, 16):
        piece = piece + left_in[q]
    lefts[core, here] = piece * 0.125
    for dx, dg in group:
        block = lefts.at[core, here]
        remote(block, block, 14, member(dx, dg), lefts.at[0, pl.ds(0, 15)])
    gradients(1)
    gradients(0)
    arrived(14)
    remote(lefts.at[core], lefts.at[core], 15, pair)
    arrived(15)

    for k in range(2):

        @region
        def _(k=k):
            rows_all = jnp.concatenate([lefts[k, q] for q in range(16)], axis=1)[:, 0:1728]
            pieces = split(rows_all)
            out = jnp.dot(pieces, part_half[k].reshape(1728, C), preferred_element_type=F32)
            out += jnp.dot(pieces, part_rest[k].reshape(1728, C), preferred_element_type=F32)
            right[k] = out[0:8] + out[8:16] + out[16:24]

    for d in (2, 1, 3):
        for on in (core, 1 - core):
            to = {"rep": lax.rem(rx + d, 4) * 2 + on}
            remote(right.at[on], right_in.at[rep], 17, to, right_in.at[pl.ds(0, 7)])
    remote(right.at[1 - core], right_in.at[rep], 17, pair)
    right_in[rep] = right[core]

    for k in range(2):
        mine = tz if k else ty

        @region
        def _(k=k, mine=mine):
            rows_all = jnp.concatenate([lefts[k, q] for q in range(16)], axis=1)[:, 0:1728]
            gram = lax.dot_general(rows_all, rows_all, NT, precision=HIGH, preferred_element_type=F32)
            gram = jnp.concatenate([gram, jnp.zeros((8, 120), F32)], axis=1)

            @pl.when(core == k)
            def _():
                gram_in[other] = gram

            rows = []
            for a in range(3):
                found = jnp.zeros((8, 144), F32)
                for j in range(4):
                    at = a * 576 + j * 144
                    found = jnp.where(mine == j, rows_all[:, at : at + 144], found)
                rows.append(found)
            out = split(jnp.concatenate(rows, axis=1))
            out = jnp.dot(out, order[...], preferred_element_type=F32)
            out = out[0:8] + out[8:16] + out[16:24]
            table[k, :, pl.ds(0, 512)] = jnp.concatenate([out, jnp.zeros((8, 80), F32)], axis=1)

    for d in range(1, 4):
        remote(gram_in.at[other], gram_in.at[other], 22, across(d), gram_in.at[pl.ds(0, 3)])

    pass_on(1)
    pass_on(0)
    arrived(17)
    total = right_in[0]
    for q in range(1, 8):
        total = total + right_in[q]
    right_tile[tile] = total
    for dz, dy in group:
        block = right_tile.at[tile]
        to = lax.rem(tz + dz, 4) * 4 + lax.rem(ty + dy, 4)
        remote(block, block, 18, {"tile": to}, right_tile.at[pl.ds(0, 15)])
    arrived(22)
    gram_all[core] = gram_in[0] + gram_in[1] + gram_in[2] + gram_in[3]
    remote(gram_all.at[core], gram_all.at[core], 16, pair)
    arrived(16)

    @region
    def _():
        row = lax.broadcasted_iota(jnp.int32, (2, RANK, 768), 1)
        lane = lax.broadcasted_iota(jnp.int32, (2, RANK, 128), 2)
        eye = jnp.where(lane == row[:, :, 0:128], 1.0, 0.0)
        rows = jnp.concatenate([table[:, :, 0:512], gram_all[...], eye], axis=2)
        for j in range(RANK):
            scale = lax.rsqrt(rows[:, j : j + 1, 512 + j : 513 + j])
            scaled = rows[:, j : j + 1, :] * scale
            coefs = rows[:, :, 512 + j : 513 + j] * scale
            rows = jnp.where(row == j, scaled, jnp.where(row > j, rows - coefs * scaled, rows))
        table[:, :, pl.ds(0, 512)] = rows[:, :, 0:512]
        table[:, :, pl.ds(768, 128)] = rows[:, :, 640:768]

    arrived(18)
    total = right_tile[0]
    for q in range(1, 16):
        total = total + right_tile[q]
    right_all[core] = total
    remote(right_all.at[core], right_all.at[core], 19, pair)
    stores = []
    for k in (1, 0):
        mine = tz if k else ty
        arrived(10 + k)

        @region
        def _(k=k, mine=mine):
            for tap in range(27):
                a, rows = tap // 9, pl.ds((tap % 9) * 16, 16)
                grad = part[k, a, mine, rows, :]
                for d in range(2):
                    grad = grad + part_in[k, d, a, rows, :].astype(F32)
                for half in range(2):
                    chunk[half, pl.ds(tap, 16, stride=27), :] = grad[:, half * 128 : half * 128 + 128]
            for half in range(2):
                whole_rows[k, :, pl.ds(half * 128, 128)] = chunk[half]

        stores.append(pltpu.make_async_copy(whole_rows.at[k], merged.at[k], local_sem.at[k]))
        stores[-1].start()
    arrived(19)
    table[:, :, pl.ds(512, C)] = right_all[...]
    stores.append(pltpu.make_async_copy(table, table_out, local_sem.at[2]))
    stores[-1].start()

    for store in stores:
        store.wait()
    for phase in totals:
        whole(phase).wait_send()


def finish_kernel(
    merged, table_in, approx_one, approx_two, fresh_one, fresh_two, new_one, new_two,
    table_ref, rows, approx_ref, fresh_ref, factor_ref, sem,
):
    load = pltpu.make_async_copy(table_in, table_ref, sem.at[0])
    load.start()
    loads = [pltpu.make_async_copy(merged.at[k], rows.at[k], sem.at[1 + k]) for k in range(2)]
    for copy in loads:
        copy.start()
    load.wait()
    table = table_ref[...]
    factors = table[:, :, 768:769] * table[:, 0:1, 512:768]
    for j in range(1, RANK):
        factors += table[:, :, 768 + j : 769 + j] * table[:, j : j + 1, 512:768]
    factors = factors * 0.125
    stores = []
    for k, (approx_out, fresh_out, new_out) in enumerate(
        ((approx_one, fresh_one, new_one), (approx_two, fresh_two, new_two))
    ):
        basis = table[k, :, 0:OWN]
        factor = factors[k]
        b, f = split(basis).astype(F32), split(factor)
        b = jnp.concatenate([b[0:8], b[0:8], b[0:8], b[8:16], b[8:16], b[16:24]], axis=0)
        f = jnp.concatenate([f[0:24].astype(F32), f[0:16].astype(F32), f[0:8].astype(F32)], axis=0)
        approx = lax.dot_general(b.astype(BF), f.astype(BF), TN, preferred_element_type=F32)
        factor_ref[k] = factor
        stores.append(pltpu.make_async_copy(factor_ref.at[k], new_out, sem.at[7 + k]))
        stores[-1].start()
        approx_ref[k] = approx
        stores.append(pltpu.make_async_copy(approx_ref.at[k], approx_out, sem.at[3 + k]))
        stores[-1].start()
        loads[k].wait()
        fresh_ref[k] = rows[k] - approx
        stores.append(pltpu.make_async_copy(fresh_ref.at[k], fresh_out, sem.at[5 + k]))
        stores[-1].start()
    for copy in stores:
        copy.wait()


def on_device(
    latents, cotangent, kernel_one, kernel_two, error_one, error_two, factor_one, factor_two
):
    vmem = pl.BlockSpec(memory_space=pltpu.VMEM)
    hbm = pl.BlockSpec(memory_space=pl.ANY)
    sds = jax.ShapeDtypeStruct
    merged, table = pl.pallas_call(
        train_kernel,
        out_shape=(sds((2, OWN, C), F32), sds((2, RANK, 896), F32)),
        in_specs=[hbm] * 8,
        out_specs=(hbm, hbm),
        scratch_shapes=[
            pltpu.VMEM((2, 6912, C), BF),
            pltpu.VMEM((2, 3, 9 * C, C), BF),
            pltpu.VMEM((2, OWN, 128), F32),
            pltpu.VMEM((FR, 14, 16, 128), BF),
            pltpu.VMEM((FR, 10, 16, 128), BF),
            pltpu.VMEM((3, FR, 112, C), BF),
            pltpu.VMEM((3, FR, 96, C), BF),
            pltpu.VMEM((FR, 96, C), F32),
            pltpu.VMEM((FR, 80, C), F32),
            pltpu.VMEM((FR, 64, C), F32),
            pltpu.VMEM((256, 9 * 128), BF),
            pltpu.VMEM((OWN, OWN), BF),
            pltpu.VMEM((2, 512, C), F32),
            pltpu.VMEM((2, 4, 4, 4, 16, 128), BF),
            pltpu.VMEM((2, 4, 4, 4, 16, 128), BF),
            pltpu.VMEM((2, FR, 4, 64, C), BF),
            pltpu.VMEM((2, 9 * 64, FR * 256), BF),
            pltpu.VMEM((2, 3, 4, 144, C), F32),
            pltpu.VMEM((2, 3, 4, 144, C), BF),
            pltpu.VMEM((2, 3, 4, 144, C), BF),
            pltpu.VMEM((2, 2, 3, 144, C), BF),
            pltpu.VMEM((2, 3, 144, C), BF),
            pltpu.VMEM((2, 3, 144, C), BF),
            pltpu.VMEM((2, 2, OWN, 128), F32),
            pltpu.VMEM((2, 3, 144, C), F32),
            pltpu.VMEM((2, 8, 1728), F32),
            pltpu.VMEM((2, 4, 8, 320), F32),
            pltpu.VMEM((2, 16, 8, 128), F32),
            pltpu.VMEM((16, 8, 128), F32),
            pltpu.VMEM((16, 8, 128), F32),
            pltpu.VMEM((2, 16, 8, 128), F32),
            pltpu.VMEM((2, 8, C), F32),
            pltpu.VMEM((8, 8, C), F32),
            pltpu.VMEM((16, 8, C), F32),
            pltpu.VMEM((4, 8, 128), F32),
            pltpu.VMEM((2, 8, 128), F32),
            pltpu.VMEM((2, 8, C), F32),
            pltpu.VMEM((2, OWN, C), F32),
            pltpu.VMEM((2, RANK, C), F32),
            pltpu.VMEM((2, RANK, 896), F32),
            pltpu.SemaphoreType.DMA((12,)),
            pltpu.SemaphoreType.DMA((25,)),
            pltpu.SemaphoreType.DMA((25,)),
        ],
        compiler_params=pltpu.CompilerParams(
            collective_id=0, has_side_effects=True, vmem_limit_bytes=60 * 2**20
        ),
        name="train",
    )(
        row_tiles(latents[0]),
        row_tiles(cotangent[0]),
        kernel_one,
        kernel_two,
        error_one[0],
        error_two[0],
        factor_one.T,
        factor_two.T,
    )
    block, small = sds((OWN, C), F32), sds((RANK, C), F32)
    approx_one, approx_two, fresh_one, fresh_two, new_one, new_two = pl.pallas_call(
        finish_kernel,
        out_shape=(block, block, block, block, small, small),
        in_specs=[hbm] * 2,
        out_specs=(hbm,) * 6,
        scratch_shapes=[
            pltpu.VMEM((2, RANK, 896), F32),
            pltpu.VMEM((2, OWN, C), F32),
            pltpu.VMEM((2, OWN, C), F32),
            pltpu.VMEM((2, OWN, C), F32),
            pltpu.VMEM((2, RANK, C), F32),
            pltpu.SemaphoreType.DMA((9,)),
        ],
        compiler_params=pltpu.CompilerParams(vmem_limit_bytes=60 * 2**20),
        name="finish",
    )(merged, table)
    return approx_one, approx_two, fresh_one[None], fresh_two[None], new_one.T, new_two.T


def solution(mesh):
    placed = (
        P("rep", None, "tile", None, None),
        P("rep", None, "tile", None, None),
        P(),
        P(),
        P("rep", "tile", None),
        P("rep", "tile", None),
        P(),
        P(),
    )
    return jax.shard_map(
        on_device,
        mesh=mesh,
        in_specs=placed,
        out_specs=(
            P("tile", None),
            P("tile", None),
            P("rep", "tile", None),
            P("rep", "tile", None),
            P(),
            P(),
        ),
        check_vma=False,
    )
```

```python
import functools

import jax
import jax.numpy as jnp
from jax import lax
from jax.experimental import pallas as pl
from jax.experimental.pallas import tpu as pltpu
from jax.sharding import PartitionSpec as P

MESH = pl.DeviceIdType.MESH
HIGH = lax.Precision.HIGHEST
BF = jnp.bfloat16
F32 = jnp.float32
FR = 5
WC = 8
C = 256
RANK = 8
OWN = 432
NT = (((1,), (1,)), ((), ()))
TN = (((0,), (0,)), ((), ()))


def sigmoid(v):
    return 1.0 / (1.0 + jnp.exp(-v))


def silu_slope(v):
    sig = sigmoid(v)
    return sig * (1.0 + v * (1.0 - sig))


def valid_rows(field, first, tile):
    row = lax.broadcasted_iota(jnp.int32, field.shape, 0) + first
    inside = jnp.logical_and(
        jnp.logical_or(row >= 0, tile > 0), jnp.logical_or(row < 8, tile < 15)
    )
    return jnp.where(inside, field, 0.0)


def spread(field, frame, even, odd):
    rows = field.shape[0]
    col = lax.broadcasted_iota(jnp.int32, field.shape, 1)
    for e in range(3):
        if e == 1:
            moved = field
        else:
            moved = pltpu.roll(field, 1 if e == 0 else WC - 1, 1)
            moved = jnp.where(col == (0 if e == 0 else WC - 1), 0.0, moved)
        even[e, frame, pl.ds(0, rows * WC), :] = moved.reshape(rows * WC, C).astype(BF)
        inner = moved[1 : rows - 1].reshape((rows - 2) * WC, C)
        odd[e, frame, pl.ds(0, (rows - 2) * WC), :] = inner.astype(BF)


def conv(even, odd, rows, weights, total, reverse):
    for a in (2, 1, 0):
        count = 3 + a
        first_in, first_out = (2 - a, 0) if reverse else (0, 2 - a)
        pieces = []
        for b in range(3):
            for e in range(3):
                bb, ee = (2 - b, 2 - e) if reverse else (b, e)
                source = odd if bb == 1 else even
                start = 16 if bb == 2 else 0
                piece = source[ee, pl.ds(first_in, count), pl.ds(start, rows * WC), :]
                pieces.append(piece.reshape(count * rows * WC, C))
        lhs = jnp.concatenate(pieces, axis=1)
        if reverse:
            taps = [weights[a, pl.ds(i * C, C), :] for i in range(9)]
            out = lax.dot_general(
                lhs, jnp.concatenate(taps, axis=1), NT, preferred_element_type=F32
            )
        else:
            out = jnp.dot(lhs, weights[a], preferred_element_type=F32)
        out = out.reshape(count, rows * WC, C)
        if a == 2:
            total[...] = out
        else:
            total[pl.ds(first_out, count)] += out


def row_tiles(v):
    return v.reshape(FR, 8, WC, 2, 128).transpose(0, 1, 3, 2, 4).reshape(FR, 8, 16, 128)


def rows_of(v):
    v = v.astype(F32)
    return jnp.concatenate([v[:, 0:8], v[:, 8:16]], axis=2)


def split(v):
    high = v.astype(BF)
    rest = v - high.astype(F32)
    mid = rest.astype(BF)
    low = (rest - mid.astype(F32)).astype(BF)
    return jnp.concatenate([high.astype(F32), mid.astype(F32), low.astype(F32)], axis=0).astype(BF)


def train_kernel(
    lat, cot, ker_one, ker_two, err_one, err_two, fac_one, fac_two,
    merged, table_out,
    raw, weights, chunk, lat_ext, cot_ext, even, odd, acc_one, acc_two, acc_three,
    select, order, flat, turn, turn_in, slopes, patches, part, part_half, part_rest, part_in, part_pass, part_sum, errs, err_rows,
    err_proj, thin, proj, proj_in, left_in, lefts, right, right_in, right_tile, gram_in, gram_all, right_all, whole_rows, factors, table,
    local_sem, send_sem, recv_sem,
):
    tile = lax.axis_index("tile")
    rep = lax.axis_index("rep")
    tz, ty = tile // 4, tile % 4
    rx, core = rep // 2, rep % 2
    near = core * tz + (1 - core) * ty
    other = core * ty + (1 - core) * tz
    here = rx * 4 + near
    pair = {"rep": rx * 2 + 1 - core}
    group = sorted(
        [(dx, dg) for dx in range(4) for dg in range(4) if dx or dg],
        key=lambda step: -min(step[0], 4 - step[0]) - min(step[1], 4 - step[1]),
    )

    def place(dx, dg):
        return lax.rem(rx + dx, 4) * 4 + lax.rem(near + dg, 4)

    def member(dx, dg):
        z, y = lax.rem(tz + core * dg, 4), lax.rem(ty + (1 - core) * dg, 4)
        return {"rep": lax.rem(rx + dx, 4) * 2 + core, "tile": z * 4 + y}

    def across(d):
        z, y = lax.rem(tz + (1 - core) * d, 4), lax.rem(ty + core * d, 4)
        return {"tile": z * 4 + y}

    def along(axis, d):
        if axis == "z":
            return lax.rem(tz + d, 4) * 4 + ty
        return tz * 4 + lax.rem(ty + d, 4)

    up, down = lax.rem(tile + 15, 16), lax.rem(tile + 1, 16)

    region = pl.when(tile >= 0)
    totals = {}

    def remote(src, dst, phase, device, total=None):
        if phase not in totals:
            totals[phase] = dst if total is None else total
        pltpu.make_async_remote_copy(
            src_ref=src, dst_ref=dst, send_sem=send_sem.at[phase], recv_sem=recv_sem.at[phase],
            device_id=device, device_id_type=MESH,
        ).start()

    def whole(phase):
        ref = totals[phase]
        return pltpu.make_async_remote_copy(
            src_ref=ref, dst_ref=ref, send_sem=send_sem.at[phase], recv_sem=recv_sem.at[phase],
            device_id={"tile": up}, device_id_type=MESH,
        )

    def arrived(phase):
        whole(phase).wait_recv()

    def send_blocks(k):
        for f in range(FR):
            for d in (1, 3):
                to = {"tile": along("y" if k else "z", d)}
                remote(slopes.at[k, f, 0], slopes.at[k, f, d], 8 + k, to, slopes.at[k, :, pl.ds(1, 2)])

    def forward_blocks(k):
        arrived(8 + k)
        for f in range(FR):
            for d, half in ((1, pl.ds(0, 32)), (3, pl.ds(32, 32))):
                to = {"tile": along("y" if k else "z", d)}
                remote(slopes.at[k, f, d, half], slopes.at[k, f, 2, half], 20 + k, to, slopes.at[k, :, 2])

    low, high = pl.ds(0, 80), pl.ds(80, 64)

    def send_far(k, a):
        axis, mine = ("z", tz) if k else ("y", ty)
        chunk_of = part_half.at[k, a, lax.rem(mine + 2, 4)]
        remote(chunk_of.at[low], part_pass.at[k, a, low], 23 + k, {"tile": along(axis, 1)}, part_pass.at[k])
        remote(chunk_of.at[high], part_pass.at[k, a, high], 23 + k, {"tile": along(axis, 3)})

    def send_near(k, a):
        axis, mine = ("z", tz) if k else ("y", ty)
        after, before = part_half.at[k, a, lax.rem(mine + 1, 4)], part_half.at[k, a, lax.rem(mine + 3, 4)]
        remote(after.at[high], part_in.at[k, 0, a, high], 10 + k, {"tile": along(axis, 1)}, part_in.at[k])
        remote(before.at[low], part_in.at[k, 1, a, low], 10 + k, {"tile": along(axis, 3)})

    def pass_on(k):
        axis, mine = ("z", tz) if k else ("y", ty)
        arrived(23 + k)

        @region
        def _():
            for a in range(3):
                for rows, step in ((low, 1), (high, 3)):
                    own_part = part[k, a, lax.rem(mine + step, 4), rows, :]
                    part_sum[k, a, rows, :] = (own_part + part_pass[k, a, rows, :].astype(F32)).astype(BF)

        for a in range(3):
            for rows, step in ((low, 1), (high, 3)):
                to = {"tile": along(axis, step)}
                remote(part_sum.at[k, a, rows], part_in.at[k, step // 2, a, rows], 10 + k, to)

    def send_slopes(k):
        factor = split(factors[k])
        rows = slopes[k, :, 0].reshape(320, C)
        out = lax.dot_general(factor, rows, NT, preferred_element_type=F32)
        thin[k, 0] = out[0:8] + out[8:16] + out[16:24]
        axis = "y" if k else "z"
        for d in (2, 1, 3):
            to = {"tile": along(axis, d)}
            remote(thin.at[k, 0], thin.at[k, d], 6 + k, to, thin.at[k, pl.ds(1, 3)])
        send_blocks(k)

    def gradients(k):
        arrived(20 + k)
        mine = tz if k else ty
        for a in range(3):

            @region
            def _(a=a):
                count = 3 + a
                rhs = slopes[k, pl.ds(2 - a, count)].reshape(count * 256, C)
                out = jnp.dot(patches[k, :, pl.ds(0, count * 256)], rhs, preferred_element_type=F32)
                part[k, a] = out.reshape(4, 144, C)
                part[k, a, mine] += err_rows[k, a]
                out = part[k, a]
                half = out.astype(BF)
                part_half[k, a] = half
                part_rest[k, a] = (out - half.astype(F32)).astype(BF)

            send_far(k, a)
        for a in range(3):
            send_near(k, a)

    def project_errors():
        for k in range(2):
            mine = tz if k else ty
            for half in range(2):
                loads[6 + 2 * k + half].wait()

            @region
            def _(k=k, mine=mine):
                for half in range(2):
                    for tap in range(27):
                        rows = errs[k, half, pl.ds(tap, 16, stride=27), :]
                        err_rows[k, tap // 9, pl.ds((tap % 9) * 16, 16), pl.ds(half * 128, 128)] = rows
                out = err_rows[k].reshape(OWN, C)
                high = out.astype(BF)
                rest = (out - high.astype(F32)).astype(BF)
                factor = split(factors[k])
                out = lax.dot_general(factor, high, NT, preferred_element_type=F32)
                out += lax.dot_general(factor, rest, NT, preferred_element_type=F32)
                out = out[0:8] + out[8:16] + out[16:24]
                err_proj[k] = jnp.concatenate(
                    [
                        jnp.where(mine == j, out[:, a * 144 : a * 144 + 144], 0.0)
                        for a in range(3)
                        for j in range(4)
                    ],
                    axis=1,
                )

    loads = [
        pltpu.make_async_copy(ker_one, raw.at[0], local_sem.at[0]),
        pltpu.make_async_copy(ker_two, raw.at[1], local_sem.at[1]),
        pltpu.make_async_copy(lat, lat_ext.at[:, pl.ds(3, 8)], local_sem.at[2]),
        pltpu.make_async_copy(cot, cot_ext.at[:, pl.ds(1, 8)], local_sem.at[3]),
    ]
    for k, fac in enumerate((fac_one, fac_two)):
        loads.append(pltpu.make_async_copy(fac, factors.at[k], local_sem.at[4 + k]))
    for k, err in enumerate((err_one, err_two)):
        for half in range(2):
            lanes = pl.ds(half * 128, 128)
            loads.append(
                pltpu.make_async_copy(err.at[:, lanes], errs.at[k, half], local_sem.at[8 + 2 * k + half])
            )
    for load in loads:
        load.start()

    barrier = pltpu.get_barrier_semaphore()
    greeted = [{"tile": lax.rem(tz + dz, 4) * 4 + lax.rem(ty + dy, 4)} for dz, dy in group]
    greeted += [pair] + [member(dx, dg) for dx, dg in group if dx]
    greeted += [{"rep": lax.rem(rx + d, 4) * 2 + 1 - core} for d in range(1, 4)]
    for device in greeted:
        pl.semaphore_signal(barrier, inc=1, device_id=device, device_id_type=MESH)
    held = lax.broadcasted_iota(jnp.int32, (256, 128), 0)
    want = lax.broadcasted_iota(jnp.int32, (256, 128), 1)
    same = (held // 128) == (want // 64)
    held, want = held % 128, want % 64
    for b in range(3):
        for e in range(3):
            hit = jnp.logical_and(held // 8 == want // 8 + b, held % 8 == want % 8 + (e - 1))
            hit = jnp.logical_and(same, hit)
            select[:, pl.ds((b * 3 + e) * 128, 128)] = jnp.where(hit, 1.0, 0.0).astype(BF)

    source = lax.broadcasted_iota(jnp.int32, (OWN, OWN), 0)
    target = lax.broadcasted_iota(jnp.int32, (OWN, OWN), 1)
    order[...] = jnp.where(target == (source % 16) * 27 + source // 16, 1.0, 0.0).astype(BF)

    for k in range(2):
        flat[k, pl.ds(400, 112), :] = jnp.zeros((112, C), F32)

    pl.semaphore_wait(barrier, len(greeted))

    remote(lat.at[:, pl.ds(5, 3)], lat_ext.at[:, pl.ds(0, 3)], 0, {"tile": down})
    remote(lat.at[:, pl.ds(0, 3)], lat_ext.at[:, pl.ds(11, 3)], 1, {"tile": up})
    remote(cot.at[:, pl.ds(7, 1)], cot_ext.at[:, pl.ds(0, 1)], 2, {"tile": down})
    remote(cot.at[:, pl.ds(0, 1)], cot_ext.at[:, pl.ds(9, 1)], 3, {"tile": up})

    for k in range(2):
        loads[k].wait()

        def reorder(j, carry, k=k):
            rows = pl.ds(pl.multiple_of(j * OWN, OWN), OWN)
            for half in range(2):
                lanes = pl.ds(half * 128, 128)
                chunk[half] = raw[k, rows, lanes].astype(F32)
                for tap in range(27):
                    picked = chunk[half, pl.ds(tap, 16, stride=27), :].astype(BF)
                    at = pl.multiple_of((tap % 9) * C + j * 16, 16)
                    weights[k, tap // 9, pl.ds(at, 16), lanes] = picked
            return carry

        lax.fori_loop(0, 16, reorder, 0)

    loads[2].wait()
    loads[3].wait()
    arrived(0)
    arrived(1)

    def enter_one(f, carry):
        field = rows_of(lat_ext[f])
        field = valid_rows(field, -3, tile)
        flat[0, pl.ds(f * 80, 80), :] = field[2:12].reshape(80, C)
        spread(field, f, even, odd)
        return carry

    def transpose(k, first, last):
        for t in range(first, last):
            turn[k, t] = flat[k, pl.ds(t * 128, 128), :].T.astype(BF).reshape(4, 4, 16, 128)

    @region
    def _():
        for f in range(FR):
            enter_one(f, 0)
        transpose(0, 0, 4)

    own = [
        pltpu.make_async_copy(turn.at[0, :, tz], turn_in.at[0, 0], local_sem.at[6]),
        pltpu.make_async_copy(turn.at[1, :, :, ty], turn_in.at[1, 0], local_sem.at[7]),
    ]
    own[0].start()
    for d in (2, 1, 3):
        to = lax.rem(tz + d, 4)
        remote(turn.at[0, :, to], turn_in.at[0, d], 4, {"tile": along("z", d)}, turn_in.at[0, pl.ds(1, 3)])
    region(lambda: conv(even, odd, 12, weights.at[0], acc_one, False))

    totals[5] = turn_in.at[1, pl.ds(1, 3)]
    def enter_two(f, carry):
        pre = acc_one[f]
        hidden = (pre * sigmoid(pre)).astype(BF).astype(F32).reshape(12, WC, C)
        hidden = valid_rows(hidden, -2, tile)
        flat[1, pl.ds(f * 80, 80), :] = hidden[1:11].reshape(80, C)
        spread(hidden, f, even, odd)
        return carry

    for frames, first, last in (((0, 1), 0, 1), ((2, 3, 4), 1, 4)):

        @region
        def _():
            for f in frames:
                enter_two(f, 0)
            transpose(1, first, last)

        for t in range(first, last):
            for d in (2, 1, 3):
                to = lax.rem(ty + d, 4)
                remote(turn.at[1, t, :, to], turn_in.at[1, d, t], 5, {"tile": along("y", d)})
    own[1].start()
    region(lambda: conv(even, odd, 10, weights.at[1], acc_two, False))

    arrived(2)
    arrived(3)
    loads[4].wait()
    loads[5].wait()

    def enter_three(f, carry):
        cots = rows_of(cot_ext[f]).reshape(80, C)
        slope = (cots * silu_slope(acc_two[f])).astype(BF).astype(F32).reshape(10, WC, C)
        slope = valid_rows(slope, -1, tile)
        spread(slope, f, even, odd)
        slopes[1, f, 0] = slope[1:9].reshape(64, C).astype(BF)
        return carry

    region(lambda: [enter_three(f, 0) for f in range(FR)] and None)
    send_slopes(1)
    region(lambda: conv(even, odd, 8, weights.at[1], acc_three, True))

    def leave(f, carry):
        pre = acc_one[f, pl.ds(16, 64), :]
        slopes[0, f, 0] = (acc_three[f] * silu_slope(pre)).astype(BF)
        return carry

    region(lambda: [leave(f, 0) for f in range(FR)] and None)
    send_slopes(0)

    for k in range(2):
        if k == 1:
            project_errors()
        own[k].wait()
        arrived(4 + k)

        @region
        def _(k=k):
            for p in range(2):
                blocks = []
                for s in range(2):
                    wide = [turn_in[k, 2 * p + s, t].reshape(64, 128) for t in range(4)]
                    wide = jnp.concatenate(wide, axis=1)
                    wide = [wide[:, f * 80 : f * 80 + 128] for f in range(FR)]
                    blocks.append(jnp.concatenate(wide, axis=0))
                lhs = jnp.concatenate(blocks, axis=1)
                out = jnp.dot(lhs, select[...], preferred_element_type=F32).astype(BF)
                for f in range(FR):
                    for i in range(9):
                        for j in range(4):
                            block = out[f * 64 + j * 16 : f * 64 + j * 16 + 16, i * 128 : i * 128 + 128]
                            rows = pl.ds(j * 144 + i * 16, 16)
                            patches[k, rows, pl.ds(f * 256 + p * 128, 128)] = block

    for k in (1, 0):
        arrived(6 + k)

        @region
        def _(k=k):
            blocks = [thin[k, d] for d in range(4)]
            wide = jnp.concatenate(
                [blocks[d][:, f * 64 : f * 64 + 64] for f in range(FR) for d in range(4)], axis=1
            )
            shifts = [
                jnp.concatenate([wide[:, (2 - a) * 256 :], jnp.zeros((8, (2 - a) * 256), F32)], axis=1)
                if a < 2
                else wide
                for a in range(3)
            ]
            wide = split(jnp.concatenate(shifts, axis=0))
            out = lax.dot_general(wide, patches[k], NT, preferred_element_type=F32)
            out = out[0:24] + out[24:48] + out[48:72]
            out = jnp.concatenate([out[0:8], out[8:16], out[16:24]], axis=1)
            sample = out + err_proj[k]
            sample = jnp.concatenate([sample, jnp.zeros((8, 2048 - 1728), F32)], axis=1)
            for q in range(16):
                proj[k, q] = sample[:, q * 128 : q * 128 + 128]

    remote(proj.at[1 - core], proj_in, 12, pair)
    arrived(12)
    for q in range(16):
        proj_in[q] = proj_in[q] + proj[core, q]
    for dx, dg in group:
        to = place(dx, dg)
        remote(proj_in.at[to], left_in.at[here], 13, member(dx, dg), left_in.at[pl.ds(0, 15)])
    left_in[here] = proj_in[here]
    forward_blocks(1)
    forward_blocks(0)

    arrived(13)
    piece = left_in[0]
    for q in range(1, 16):
        piece = piece + left_in[q]
    lefts[core, here] = piece * 0.125
    for dx, dg in group:
        block = lefts.at[core, here]
        remote(block, block, 14, member(dx, dg), lefts.at[0, pl.ds(0, 15)])
    gradients(1)
    gradients(0)
    arrived(14)
    remote(lefts.at[core], lefts.at[core], 15, pair)
    arrived(15)

    for k in range(2):

        @region
        def _(k=k):
            rows_all = jnp.concatenate([lefts[k, q] for q in range(16)], axis=1)[:, 0:1728]
            pieces = split(rows_all)
            out = jnp.dot(pieces, part_half[k].reshape(1728, C), preferred_element_type=F32)
            out += jnp.dot(pieces, part_rest[k].reshape(1728, C), preferred_element_type=F32)
            right[k] = out[0:8] + out[8:16] + out[16:24]

    for d in (2, 1, 3):
        for on in (core, 1 - core):
            to = {"rep": lax.rem(rx + d, 4) * 2 + on}
            remote(right.at[on], right_in.at[rep], 17, to, right_in.at[pl.ds(0, 7)])
    remote(right.at[1 - core], right_in.at[rep], 17, pair)
    right_in[rep] = right[core]

    for k in range(2):
        mine = tz if k else ty

        @region
        def _(k=k, mine=mine):
            rows_all = jnp.concatenate([lefts[k, q] for q in range(16)], axis=1)[:, 0:1728]
            gram = lax.dot_general(rows_all, rows_all, NT, precision=HIGH, preferred_element_type=F32)
            gram = jnp.concatenate([gram, jnp.zeros((8, 120), F32)], axis=1)

            @pl.when(core == k)
            def _():
                gram_in[other] = gram

            rows = []
            for a in range(3):
                found = jnp.zeros((8, 144), F32)
                for j in range(4):
                    at = a * 576 + j * 144
                    found = jnp.where(mine == j, rows_all[:, at : at + 144], found)
                rows.append(found)
            out = split(jnp.concatenate(rows, axis=1))
            out = jnp.dot(out, order[...], preferred_element_type=F32)
            out = out[0:8] + out[8:16] + out[16:24]
            table[k, :, pl.ds(0, 512)] = jnp.concatenate([out, jnp.zeros((8, 80), F32)], axis=1)

    for d in (2, 1, 3):
        remote(gram_in.at[other], gram_in.at[other], 22, across(d), gram_in.at[pl.ds(0, 3)])

    pass_on(1)
    pass_on(0)
    arrived(17)
    total = right_in[0]
    for q in range(1, 8):
        total = total + right_in[q]
    right_tile[tile] = total
    for dz, dy in group:
        block = right_tile.at[tile]
        to = lax.rem(tz + dz, 4) * 4 + lax.rem(ty + dy, 4)
        remote(block, block, 18, {"tile": to}, right_tile.at[pl.ds(0, 15)])
    arrived(22)
    gram_all[core] = gram_in[0] + gram_in[1] + gram_in[2] + gram_in[3]
    remote(gram_all.at[core], gram_all.at[core], 16, pair)
    arrived(16)

    @region
    def _():
        row = lax.broadcasted_iota(jnp.int32, (2, RANK, 768), 1)
        lane = lax.broadcasted_iota(jnp.int32, (2, RANK, 128), 2)
        eye = jnp.where(lane == row[:, :, 0:128], 1.0, 0.0)
        rows = jnp.concatenate([table[:, :, 0:512], gram_all[...], eye], axis=2)
        for j in range(RANK):
            scale = lax.rsqrt(rows[:, j : j + 1, 512 + j : 513 + j])
            scaled = rows[:, j : j + 1, :] * scale
            coefs = rows[:, :, 512 + j : 513 + j] * scale
            rows = jnp.where(row == j, scaled, jnp.where(row > j, rows - coefs * scaled, rows))
        table[:, :, pl.ds(0, 512)] = rows[:, :, 0:512]
        table[:, :, pl.ds(768, 128)] = rows[:, :, 640:768]

    arrived(18)
    total = right_tile[0]
    for q in range(1, 16):
        total = total + right_tile[q]
    right_all[core] = total
    remote(right_all.at[core], right_all.at[core], 19, pair)
    stores = []
    for k in (1, 0):
        mine = tz if k else ty
        arrived(10 + k)

        @region
        def _(k=k, mine=mine):
            for tap in range(27):
                a, rows = tap // 9, pl.ds((tap % 9) * 16, 16)
                grad = part[k, a, mine, rows, :]
                for d in range(2):
                    grad = grad + part_in[k, d, a, rows, :].astype(F32)
                for half in range(2):
                    chunk[half, pl.ds(tap, 16, stride=27), :] = grad[:, half * 128 : half * 128 + 128]
            for half in range(2):
                whole_rows[k, :, pl.ds(half * 128, 128)] = chunk[half]

        stores.append(pltpu.make_async_copy(whole_rows.at[k], merged.at[k], local_sem.at[k]))
        stores[-1].start()
    arrived(19)
    table[:, :, pl.ds(512, C)] = right_all[...]
    stores.append(pltpu.make_async_copy(table, table_out, local_sem.at[2]))
    stores[-1].start()

    for store in stores:
        store.wait()
    for phase in totals:
        whole(phase).wait_send()


def finish_kernel(
    merged, table_in, approx_one, approx_two, fresh_one, fresh_two, new_one, new_two,
    table_ref, rows, approx_ref, fresh_ref, factor_ref, sem,
):
    load = pltpu.make_async_copy(table_in, table_ref, sem.at[0])
    load.start()
    loads = [pltpu.make_async_copy(merged.at[k], rows.at[k], sem.at[1 + k]) for k in range(2)]
    for copy in loads:
        copy.start()
    load.wait()
    table = table_ref[...]
    factors = table[:, :, 768:769] * table[:, 0:1, 512:768]
    for j in range(1, RANK):
        factors += table[:, :, 768 + j : 769 + j] * table[:, j : j + 1, 512:768]
    factors = factors * 0.125
    stores = []
    for k, (approx_out, fresh_out, new_out) in enumerate(
        ((approx_one, fresh_one, new_one), (approx_two, fresh_two, new_two))
    ):
        basis = table[k, :, 0:OWN]
        factor = factors[k]
        b, f = split(basis).astype(F32), split(factor)
        b = jnp.concatenate([b[0:8], b[0:8], b[0:8], b[8:16], b[8:16], b[16:24]], axis=0)
        f = jnp.concatenate([f[0:24].astype(F32), f[0:16].astype(F32), f[0:8].astype(F32)], axis=0)
        approx = lax.dot_general(b.astype(BF), f.astype(BF), TN, preferred_element_type=F32)
        factor_ref[k] = factor
        stores.append(pltpu.make_async_copy(factor_ref.at[k], new_out, sem.at[7 + k]))
        stores[-1].start()
        approx_ref[k] = approx
        stores.append(pltpu.make_async_copy(approx_ref.at[k], approx_out, sem.at[3 + k]))
        stores[-1].start()
        loads[k].wait()
        fresh_ref[k] = rows[k] - approx
        stores.append(pltpu.make_async_copy(fresh_ref.at[k], fresh_out, sem.at[5 + k]))
        stores[-1].start()
    for copy in stores:
        copy.wait()


def on_device(
    latents, cotangent, kernel_one, kernel_two, error_one, error_two, factor_one, factor_two
):
    vmem = pl.BlockSpec(memory_space=pltpu.VMEM)
    hbm = pl.BlockSpec(memory_space=pl.ANY)
    sds = jax.ShapeDtypeStruct
    merged, table = pl.pallas_call(
        train_kernel,
        out_shape=(sds((2, OWN, C), F32), sds((2, RANK, 896), F32)),
        in_specs=[hbm] * 8,
        out_specs=(hbm, hbm),
        scratch_shapes=[
            pltpu.VMEM((2, 6912, C), BF),
            pltpu.VMEM((2, 3, 9 * C, C), BF),
            pltpu.VMEM((2, OWN, 128), F32),
            pltpu.VMEM((FR, 14, 16, 128), BF),
            pltpu.VMEM((FR, 10, 16, 128), BF),
            pltpu.VMEM((3, FR, 112, C), BF),
            pltpu.VMEM((3, FR, 96, C), BF),
            pltpu.VMEM((FR, 96, C), F32),
            pltpu.VMEM((FR, 80, C), F32),
            pltpu.VMEM((FR, 64, C), F32),
            pltpu.VMEM((256, 9 * 128), BF),
            pltpu.VMEM((OWN, OWN), BF),
            pltpu.VMEM((2, 512, C), F32),
            pltpu.VMEM((2, 4, 4, 4, 16, 128), BF),
            pltpu.VMEM((2, 4, 4, 4, 16, 128), BF),
            pltpu.VMEM((2, FR, 4, 64, C), BF),
            pltpu.VMEM((2, 9 * 64, FR * 256), BF),
            pltpu.VMEM((2, 3, 4, 144, C), F32),
            pltpu.VMEM((2, 3, 4, 144, C), BF),
            pltpu.VMEM((2, 3, 4, 144, C), BF),
            pltpu.VMEM((2, 2, 3, 144, C), BF),
            pltpu.VMEM((2, 3, 144, C), BF),
            pltpu.VMEM((2, 3, 144, C), BF),
            pltpu.VMEM((2, 2, OWN, 128), F32),
            pltpu.VMEM((2, 3, 144, C), F32),
            pltpu.VMEM((2, 8, 1728), F32),
            pltpu.VMEM((2, 4, 8, 320), F32),
            pltpu.VMEM((2, 16, 8, 128), F32),
            pltpu.VMEM((16, 8, 128), F32),
            pltpu.VMEM((16, 8, 128), F32),
            pltpu.VMEM((2, 16, 8, 128), F32),
            pltpu.VMEM((2, 8, C), F32),
            pltpu.VMEM((8, 8, C), F32),
            pltpu.VMEM((16, 8, C), F32),
            pltpu.VMEM((4, 8, 128), F32),
            pltpu.VMEM((2, 8, 128), F32),
            pltpu.VMEM((2, 8, C), F32),
            pltpu.VMEM((2, OWN, C), F32),
            pltpu.VMEM((2, RANK, C), F32),
            pltpu.VMEM((2, RANK, 896), F32),
            pltpu.SemaphoreType.DMA((12,)),
            pltpu.SemaphoreType.DMA((25,)),
            pltpu.SemaphoreType.DMA((25,)),
        ],
        compiler_params=pltpu.CompilerParams(
            collective_id=0, has_side_effects=True, vmem_limit_bytes=60 * 2**20
        ),
        name="train",
    )(
        row_tiles(latents[0]),
        row_tiles(cotangent[0]),
        kernel_one,
        kernel_two,
        error_one[0],
        error_two[0],
        factor_one.T,
        factor_two.T,
    )
    block, small = sds((OWN, C), F32), sds((RANK, C), F32)
    approx_one, approx_two, fresh_one, fresh_two, new_one, new_two = pl.pallas_call(
        finish_kernel,
        out_shape=(block, block, block, block, small, small),
        in_specs=[hbm] * 2,
        out_specs=(hbm,) * 6,
        scratch_shapes=[
            pltpu.VMEM((2, RANK, 896), F32),
            pltpu.VMEM((2, OWN, C), F32),
            pltpu.VMEM((2, OWN, C), F32),
            pltpu.VMEM((2, OWN, C), F32),
            pltpu.VMEM((2, RANK, C), F32),
            pltpu.SemaphoreType.DMA((9,)),
        ],
        compiler_params=pltpu.CompilerParams(vmem_limit_bytes=60 * 2**20),
        name="finish",
    )(merged, table)
    return approx_one, approx_two, fresh_one[None], fresh_two[None], new_one.T, new_two.T


def solution(mesh):
    placed = (
        P("rep", None, "tile", None, None),
        P("rep", None, "tile", None, None),
        P(),
        P(),
        P("rep", "tile", None),
        P("rep", "tile", None),
        P(),
        P(),
    )
    return jax.shard_map(
        on_device,
        mesh=mesh,
        in_specs=placed,
        out_specs=(
            P("tile", None),
            P("tile", None),
            P("rep", "tile", None),
            P("rep", "tile", None),
            P(),
            P(),
        ),
        check_vma=False,
    )
```
